128 devices in a mesh: dp: 32 (over z, y, core), mp: 4 (over x).
Axes of the slice: x: 4, y: 4, z: 4, core: 2. Of those that a mesh axis runs over, the one named last changes fastest.
Arguments:
- events: bfloat16 [98304, 1024], P('dp'), may hold values from -6 to 6
- upstream: bfloat16 [98304, 1024], P('dp'), may hold values from -1.5 to 1.5
- proj_weight: bfloat16 [1024, 4, 1024], P(None, None, 'mp'), may hold values from -0.1875 to 0.1875
- proj_bias: float32 [4, 1024], P(None, 'mp'), may hold values from -3 to 3
- norm_gain: float32 [1024], P('mp'), may hold values from 0.1 to 1.9
- out_weight: bfloat16 [1024, 1024], P('mp'), may hold values from -0.1875 to 0.1875
- lengths: int32 [32, 48], replicated, may hold values from 0 to 3, as said below
- owners: int32 [32, 48], replicated, may hold values from 0 to 31, as said below
Outputs:
- event_grads: bfloat16 [98304, 1024], P('dp', 'mp')
- proj_weight_grad: float32 [1024, 4, 1024], P(None, None, 'mp')
- proj_bias_grad: float32 [4, 1024], P(None, 'mp')
- norm_gain_grad: float32 [1024], P('mp')
- out_weight_grad: float32 [1024, 1024], P('mp')
The draws below stay inside these ranges and needn't reach their ends.
Inputs may be any that keep to these rules, and one draw needn't show every extreme that they name: Each home's histories fill its tiles from the first tile on, zero lengths only after the last history; some home has all 48 tiles filled, and some history has exactly 3 tiles. The histories one home gives one dp index hold 0 or exactly 3 tiles, and every home gives itself 3; one dp index is given at most 21 tiles in all, and some dp index exactly that. `owners`: entries of zero-length histories carry no meaning. The result does not depend on this map.
All inputs are finite; a program needn't handle non-finite values.
Results may differ from the reference program's by a relative error of at most 0.004.
The reference program's roundings to bfloat16 on the way count: a program that leaves them out, or rounds other values in their place, can miss the bound.
Values may be sent and summed in bfloat16 or wider, within the bound.
No kernel may reach another device: no remote copies, remote signals or barrier semaphores. Data moves between devices by JAX's collectives and lax.ppermute only.
A program may use at most 192 MiB of HBM per device.

```python
import jax
import jax.numpy as jnp
from jax import lax

D = 1024
HEADS = 8
TILE = 64
CAP = 3
HOME_TILES = 48
WORK_TILES = 21
ROWS = 98304
N_DP = 32


def plan_draw(key):
    device_count = N_DP
    capacity = CAP
    home_tiles = HOME_TILES
    box_count = home_tiles // capacity
    shuffle = jax.random.permutation(jax.random.fold_in(key, 101), device_count).astype(jnp.int32)
    position = jnp.zeros((device_count,), jnp.int32).at[shuffle].set(jnp.arange(device_count, dtype=jnp.int32))
    crowded = position % 4 == 0
    used_boxes = jnp.where(crowded, box_count, device_count // 8)
    box_ids = jnp.arange(box_count, dtype=jnp.int32)
    box_used = (box_ids[None, :] < used_boxes[:, None]).astype(jnp.int32)
    box_owner = shuffle[(position[:, None] + box_ids[None, :]) % device_count]
    tile_box = jnp.arange(home_tiles, dtype=jnp.int32) // capacity
    tile_spot = jnp.arange(home_tiles, dtype=jnp.int32) % capacity
    coin_flips = jax.random.randint(jax.random.fold_in(key, 102), (device_count, home_tiles), 0, 2, dtype=jnp.int32)
    inner = jnp.where(tile_box[None, :] == 0, 0, coin_flips)
    occupied = box_used[:, tile_box]
    starts = jnp.where(tile_spot[None, :] == 0, 1, inner) * occupied
    history = jnp.cumsum(starts, axis=1, dtype=jnp.int32) - 1
    member = (history[:, :, None] == jnp.arange(home_tiles, dtype=jnp.int32)[None, None, :]) & (occupied[:, :, None] > 0)
    lengths = jnp.sum(member.astype(jnp.int32), axis=1, dtype=jnp.int32)
    heads_of = member & (starts[:, :, None] > 0)
    owners = jnp.sum(jnp.where(heads_of, box_owner[:, tile_box][:, :, None], 0), axis=1, dtype=jnp.int32)
    return (lengths, owners)


def draw_lengths(key, part):
    return plan_draw(key)[0]


def draw_owners(key, part):
    return plan_draw(key)[1]


def level_of(rng, dims, cuts, smallest, top_value):
    factor_of, own = 1.0, jax.random.fold_in(rng, 6)
    for axis_at, shards_of in cuts:
        draws = jnp.exp(jax.random.uniform(jax.random.fold_in(own, axis_at), (shards_of,), jnp.float32, smallest / len(cuts), top_value / len(cuts)))
        factor_of = factor_of * jnp.repeat(draws, dims[axis_at] // shards_of).reshape([-1 if axis == axis_at else 1 for axis in range(len(dims))])
    return factor_of


def centred(stream_key, dims, spread, most, cuts=(), held_as=jnp.bfloat16):
    entries = spread * jax.random.normal(stream_key, dims, jnp.float32)
    if cuts:
        entries = entries * level_of(stream_key, dims, cuts, -0.22, 0.18)
    return jnp.clip(entries, -most, most).astype(held_as)


def setup_inputs(seed: int = 0) -> dict:
    seeds = jax.random.split(jax.random.key(seed), 9)
    return {
        "events": centred(seeds[0], (ROWS, D), 1.0, 6.0, ((0, 32),)),
        "upstream": centred(seeds[1], (ROWS, D), 0.25, 1.5, ((0, 32),)),
        "proj_weight": centred(seeds[2], (D, 4, D), D ** -0.5, 0.1875, ((2, 4),)),
        "proj_bias": centred(seeds[3], (4, D), 0.5, 3.0, ((1, 4),), jnp.float32),
        "norm_gain": jnp.clip(1.0 + 0.18 * jax.random.normal(seeds[4], (D,), jnp.float32), 0.1, 1.9),
        "out_weight": centred(seeds[5], (D, D), D ** -0.5, 0.1875, ((0, 4),)),
        "lengths": draw_lengths(jax.random.fold_in(seeds[8], 71), 0),
        "owners": draw_owners(jax.random.fold_in(seeds[8], 71), 0),
    }


EPSILON = 1e-05

def silu_slope(values):
    sigmoid = jax.nn.sigmoid(values)
    return sigmoid * (1.0 + values * (1.0 - sigmoid))

def plan_tables(lengths, owners):
    device_count = lengths.shape[0]
    targets = jnp.arange(device_count, dtype=jnp.int32)
    chosen = (owners[:, :, None] == targets[None, None, :]).astype(jnp.int32)
    weighted = chosen * lengths[:, :, None]
    home_start = jnp.cumsum(lengths, axis=1, dtype=jnp.int32) - lengths
    within = jnp.cumsum(weighted, axis=1, dtype=jnp.int32) - weighted
    pair_offset = lax.optimization_barrier(jnp.sum(within * chosen, axis=2, dtype=jnp.int32))
    pair_total = lax.optimization_barrier(jnp.sum(weighted, axis=1, dtype=jnp.int32))
    earlier = jnp.cumsum(pair_total, axis=0, dtype=jnp.int32) - pair_total
    work_start = lax.optimization_barrier(jnp.sum(earlier[:, None, :] * chosen, axis=2, dtype=jnp.int32)) + pair_offset
    return (home_start, pair_offset, work_start)

def work_map(lengths, home_start, pair_offset, work_start, owners, device, capacity, work_tiles, home_tiles):
    device_count = lengths.shape[0]
    tile_ids = jnp.arange(work_tiles, dtype=jnp.int32)[:, None, None]
    offset = tile_ids - work_start[None]
    inside = (owners[None] == device) & (lengths[None] > 0) & (offset >= 0) & (offset < lengths[None]) & (pair_offset[None] + offset < capacity)
    sources = jnp.arange(device_count, dtype=jnp.int32)[None, :, None]
    occupied = jnp.any(inside, axis=(1, 2))
    slot_index = lax.optimization_barrier(jnp.sum(jnp.where(inside, sources * capacity + pair_offset[None] + offset, 0), axis=(1, 2), dtype=jnp.int32))
    home_tile = lax.optimization_barrier(jnp.sum(jnp.where(inside, sources * home_tiles + home_start[None] + offset, 0), axis=(1, 2), dtype=jnp.int32))
    first_tile = lax.optimization_barrier(jnp.sum(jnp.where(inside, work_start[None], 0), axis=(1, 2), dtype=jnp.int32))
    return (jnp.where(occupied, slot_index, -1), jnp.where(occupied, home_tile, -1), jnp.where(occupied, first_tile, -1))

def row_starts(first_tile, tile_rows):
    row_count = first_tile.shape[0] * tile_rows
    row_ids = jnp.arange(row_count, dtype=jnp.int32)
    expanded = jnp.repeat(first_tile, tile_rows)
    return jnp.where(expanded >= 0, expanded * tile_rows, row_ids + 1)

def layer_terms(rows_x, rows_g, start_rows, weight_in, bias_in, gain_vector, weight_out, head_count):
    row_count = rows_x.shape[0]
    local_width = weight_out.shape[0]
    head_size = local_width // head_count
    score_scale = head_size ** (-0.5)
    preact = jnp.dot(rows_x, weight_in, preferred_element_type=jnp.float32) + bias_in
    activated = jax.nn.silu(preact).astype(jnp.bfloat16)
    sections = [activated[:, column_part * local_width:(column_part + 1) * local_width].reshape(row_count, head_count, head_size).astype(jnp.float32) for column_part in range(4)]
    gate_rows, value_rows, query_rows, key_rows = sections
    row_ids = jnp.arange(row_count, dtype=jnp.int32)
    visible = (row_ids[None, :] >= start_rows[:, None]) & (row_ids[None, :] <= row_ids[:, None])
    scores = jnp.einsum('qhd,khd->hqk', query_rows, key_rows) * score_scale
    attention = jnp.where(visible[None], jax.nn.silu(scores), 0.0).astype(jnp.bfloat16)
    mixture = jnp.einsum('hqk,khd->qhd', attention.astype(jnp.float32), value_rows)
    centered = mixture - lax.optimization_barrier(jnp.mean(mixture, axis=2, keepdims=True))
    inverse = lax.rsqrt(lax.optimization_barrier(jnp.mean(centered * centered, axis=2, keepdims=True)) + EPSILON)
    normed = centered * inverse
    gain_heads = gain_vector.reshape(head_count, head_size)
    hidden = (normed * gain_heads * gate_rows).astype(jnp.bfloat16)
    out_grad = jnp.dot(hidden.reshape(row_count, local_width).T, rows_g, preferred_element_type=jnp.float32)
    hidden_grad = jnp.dot(rows_g, weight_out.T, preferred_element_type=jnp.float32).reshape(row_count, head_count, head_size)
    gain_grad = lax.optimization_barrier(jnp.sum(hidden_grad * gate_rows * normed, axis=0)).reshape(local_width)
    gate_grad = hidden_grad * normed * gain_heads
    normed_grad = hidden_grad * gate_rows * gain_heads
    mixture_grad = ((normed_grad - lax.optimization_barrier(jnp.mean(normed_grad, axis=2, keepdims=True)) - normed * lax.optimization_barrier(jnp.mean(normed_grad * normed, axis=2, keepdims=True))) * inverse).astype(jnp.bfloat16)
    values_grad = jnp.einsum('hqk,qhd->khd', attention.astype(jnp.float32), mixture_grad.astype(jnp.float32))
    attention_grad = jnp.einsum('qhd,khd->hqk', mixture_grad.astype(jnp.float32), value_rows)
    score_grad = jnp.where(visible[None], attention_grad * silu_slope(scores) * score_scale, 0.0).astype(jnp.bfloat16)
    queries_grad = jnp.einsum('hqk,khd->qhd', score_grad.astype(jnp.float32), key_rows)
    keys_grad = jnp.einsum('hqk,qhd->khd', score_grad.astype(jnp.float32), query_rows)
    joined = jnp.concatenate([section.reshape(row_count, local_width) for section in (gate_grad, values_grad, queries_grad, keys_grad)], axis=1)
    preact_grad = (joined * silu_slope(preact)).astype(jnp.bfloat16)
    in_grad = jnp.dot(rows_x.T, preact_grad, preferred_element_type=jnp.float32)
    bias_grad = lax.optimization_barrier(jnp.sum(preact_grad.astype(jnp.float32), axis=0))
    partial_rows = jnp.dot(preact_grad, weight_in.T, preferred_element_type=jnp.float32)
    return (partial_rows, in_grad, bias_grad, gain_grad, out_grad)

def reference(events, upstream, proj_weight, proj_bias, norm_gain, out_weight, lengths, owners):
    device_count = N_DP
    home_start, pair_offset, work_start = plan_tables(lengths, owners)
    tiled_x = events.reshape(device_count * HOME_TILES, TILE, D)
    tiled_g = upstream.reshape(device_count * HOME_TILES, TILE, D)
    weight_in = proj_weight.reshape(D, 4 * D)
    bias_in = proj_bias.reshape(4 * D)

    def per_worker(running, device):
        slot_index, home_tile, first_tile = work_map(lengths, home_start, pair_offset, work_start, owners, device, CAP, WORK_TILES, HOME_TILES)
        present = (home_tile >= 0)[:, None, None]
        picked = jnp.maximum(home_tile, 0)
        work_x = jnp.where(present, tiled_x[picked], jnp.zeros((), jnp.bfloat16)).reshape(WORK_TILES * TILE, D)
        work_g = jnp.where(present, tiled_g[picked], jnp.zeros((), jnp.bfloat16)).reshape(WORK_TILES * TILE, D)
        start_rows = row_starts(first_tile, TILE)
        partial_rows, in_grad, bias_grad, gain_grad, out_grad = layer_terms(work_x, work_g, start_rows, weight_in, bias_in, norm_gain, out_weight, HEADS)
        row_grads = (partial_rows + work_g.astype(jnp.float32)).astype(jnp.bfloat16)
        running = (running[0] + in_grad, running[1] + bias_grad, running[2] + gain_grad, running[3] + out_grad)
        return (running, row_grads)
    start_sums = (jnp.zeros((D, 4 * D), jnp.float32), jnp.zeros((4 * D,), jnp.float32), jnp.zeros((D,), jnp.float32), jnp.zeros((D, D), jnp.float32))
    totals, worked = lax.scan(per_worker, start_sums, jnp.arange(device_count, dtype=jnp.int32))
    tile_ids = jnp.arange(HOME_TILES, dtype=jnp.int32)[None, :, None]
    offset = tile_ids - home_start[:, None, :]
    inside = (lengths[:, None, :] > 0) & (offset >= 0) & (offset < lengths[:, None, :]) & (pair_offset[:, None, :] + offset < CAP) & (work_start[:, None, :] + offset < WORK_TILES)
    flat_index = lax.optimization_barrier(jnp.sum(jnp.where(inside, owners[:, None, :] * WORK_TILES + work_start[:, None, :] + offset, 0), axis=2, dtype=jnp.int32)).reshape(device_count * HOME_TILES)
    valid = jnp.any(inside, axis=2).reshape(device_count * HOME_TILES)
    flat_work = worked.reshape(device_count * WORK_TILES, TILE, D)
    event_grads = jnp.where(valid[:, None, None], flat_work[jnp.maximum(flat_index, 0)], jnp.zeros((), jnp.bfloat16)).reshape(ROWS, D)
    return (event_grads, (totals[0] / device_count).reshape(D, 4, D), (totals[1] / device_count).reshape(4, D), totals[2] / device_count, totals[3] / device_count)
```

```python
import functools

import jax
import jax.numpy as jnp
from jax import lax
from jax.experimental import pallas as pl
from jax.experimental.pallas import tpu as pltpu
from jax.sharding import PartitionSpec as P

HEADS = 8
TILE = 64
EPSILON = 1e-05
STEP = 256
PAIR = 128
HEAD = 128
WIDTH = 256
SPAN = 512
CALLS = (2, 2, 2, 2, 2, 2)
F32 = jnp.float32
BF16 = jnp.bfloat16
NT = (((1,), (1,)), ((), ()))
TN = (((0,), (0,)), ((), ()))


def dot(a, b, dims=(((1,), (0,)), ((), ()))):
    return lax.dot_general(a, b, dims, preferred_element_type=F32)


def sigmoid(v):
    return 0.5 * jnp.tanh(0.5 * v) + 0.5


def tile_column(values, rows):
    ids = lax.broadcasted_iota(jnp.int32, (rows, 1), 0)
    column = jnp.full((rows, 1), values[0], jnp.int32)
    for i in range(1, len(values)):
        column = jnp.where(ids >= i * TILE, values[i], column)
    return column


def layer_kernel(first, last, q0, nq, tiles, *refs):
    it = iter(refs)
    first_ref, part_ref = next(it), next(it)
    x_ref, g_ref, w_ref, wo_ref, b_ref, gain_ref = (next(it) for _ in range(6))
    if not first:
        kv_in, dkv_in, sl_in, pg_in, sum_in = (next(it) for _ in range(5))
        next(it), next(it)
    pg_out, hid_out, own_out, s1f_out, s1b_out, r2f_out, r2b_out, sum_out = (next(it) for _ in range(8))
    if not last:
        kv_out, dkv_out, sl_out, pgc_out = (next(it) for _ in range(4))
    kv, dkv, sl, pgq, gq, slgq, hg = (next(it) for _ in range(7))
    j = pl.program_id(0)
    cur = pl.ds(STEP, STEP)
    old = pl.ds(0, STEP)

    @pl.when(j == 0)
    def _():
        if first:
            kv[old] = jnp.zeros((STEP, SPAN), BF16)
            dkv[old] = jnp.zeros((STEP, SPAN), F32)
            sl[old] = jnp.zeros((STEP, SPAN), F32)
            pgq[...] = jnp.zeros((STEP, SPAN), BF16)
            sum_out[...] = jnp.zeros(sum_out.shape, F32)
        else:
            kv[old] = kv_in[...]
            dkv[old] = dkv_in[...]
            sl[old] = sl_in[...]
            pgq[...] = pg_in[...]
            sum_out[...] = sum_in[...]

    def finish():
        pg_out[:, 0:WIDTH] = pgq[:, 0:WIDTH]
        pg_out[:, WIDTH : 2 * WIDTH] = (dkv[old, 0:WIDTH] * sl[old, 0:WIDTH]).astype(BF16)
        pg_out[:, 2 * WIDTH : 3 * WIDTH] = pgq[:, WIDTH:]
        pg_out[:, 3 * WIDTH :] = (dkv[old, WIDTH:] * sl[old, WIDTH:]).astype(BF16)
        grads = pg_out[...]
        sum_out[:, 0 : 4 * WIDTH] += jnp.sum(grads.astype(F32).reshape(STEP // 8, 8, 4 * WIDTH), axis=0)
        me = part_ref[0]

        def chunk(shift):
            start = pl.multiple_of(lax.rem(me + shift, 4) * WIDTH, WIDTH)
            return dot(grads, w_ref[pl.ds(start, WIDTH), :], NT)

        own_out[...] = chunk(0)
        ahead = chunk(1).astype(BF16)
        across = chunk(2).astype(BF16)
        behind = chunk(3).astype(BF16)
        s1f_out[:, 0:HEAD] = across[:, 0:HEAD]
        s1f_out[:, HEAD:] = ahead[:, HEAD:]
        s1b_out[:, 0:HEAD] = behind[:, 0:HEAD]
        s1b_out[:, HEAD:] = across[:, HEAD:]
        r2f_out[...] = ahead[:, 0:HEAD]
        r2b_out[...] = behind[:, HEAD:]

    def query():
        t0 = (q0 + j) * (STEP // TILE)
        firsts = [first_ref[t0 + i] for i in range(STEP // TILE)]
        base = (q0 + j) * STEP
        starts = [jnp.where(f >= 0, f * TILE - base, STEP) for f in firsts]
        x = x_ref[...]
        used = tile_column(firsts, STEP) >= 0
        g = jnp.where(used, g_ref[...], jnp.zeros((), BF16))
        hg[...] = dot(g, wo_ref[...], NT)
        for part in range(4):
            cols = slice(part * WIDTH, (part + 1) * WIDTH)
            pre = dot(x, w_ref[:, cols]) + b_ref[:, cols]
            sig = sigmoid(pre)
            act = pre * sig
            slope = sig + act * (1.0 - sig)
            half = slice(0, WIDTH) if part < 2 else slice(WIDTH, SPAN)
            if part % 2 == 0:
                gq[:, half] = act.astype(BF16)
                slgq[:, half] = slope
            else:
                kv[cur, half] = act.astype(BF16)
                sl[cur, half] = slope
        scale = HEAD**-0.5
        row = lax.broadcasted_iota(jnp.int32, (PAIR, 2 * PAIR), 0)
        col = lax.broadcasted_iota(jnp.int32, (PAIR, 2 * PAIR), 1) - PAIR
        for i in range(STEP // PAIR):
            rows = slice(i * PAIR, (i + 1) * PAIR)
            window = pl.ds(PAIR + i * PAIR, 2 * PAIR)
            begin = tile_column(starts[2 * i : 2 * i + 2], PAIR) - i * PAIR
            visible = (col >= begin) & (col <= row)
            for h in range(2):
                hc = slice(h * HEAD, (h + 1) * HEAD)
                kc = slice(WIDTH + h * HEAD, WIDTH + (h + 1) * HEAD)
                gate = gq[rows, hc].astype(F32)
                q = gq[rows, kc]
                v = kv[window, hc]
                k = kv[window, kc]
                s = dot(q, k, NT) * scale
                sig = sigmoid(s)
                a = s * sig
                attn = jnp.where(visible, a, 0.0).astype(BF16)
                mix = dot(attn, v)
                centered = mix - jnp.mean(mix, axis=1, keepdims=True)
                inverse = lax.rsqrt(jnp.mean(centered * centered, axis=1, keepdims=True) + EPSILON)
                normed = centered * inverse
                gain = gain_ref[:, hc]
                local = hg[rows, hc]
                scaled = normed * gain
                hid_out[rows, hc] = (scaled * gate).astype(BF16)
                pgq_new = (local * scaled * slgq[rows, hc]).astype(BF16)
                lg = local * gate
                gsum = lg * normed
                sum_out[:, 4 * WIDTH + h * HEAD : 4 * WIDTH + (h + 1) * HEAD] += jnp.sum(
                    gsum.reshape(PAIR // 8, 8, HEAD), axis=0
                )
                ng = lg * gain
                dm = (
                    (
                        ng
                        - jnp.mean(ng, axis=1, keepdims=True)
                        - normed * jnp.mean(ng * normed, axis=1, keepdims=True)
                    )
                    * inverse
                ).astype(BF16)
                da = dot(dm, v, NT)
                sg = jnp.where(visible, da * (sig + a * (1.0 - sig)) * scale, 0.0).astype(BF16)
                dq = dot(sg, k)
                dv = dot(attn, dm, TN)
                dk = dot(sg, q, TN)
                low = pl.ds(PAIR + i * PAIR, PAIR)
                high = pl.ds(2 * PAIR + i * PAIR, PAIR)
                dkv[low, hc] += dv[:PAIR]
                dkv[high, hc] = dv[PAIR:]
                dkv[low, kc] += dk[:PAIR]
                dkv[high, kc] = dk[PAIR:]
                gq[rows, hc] = pgq_new
                gq[rows, kc] = (dq * slgq[rows, kc]).astype(BF16)

    def shift():
        kv[old] = kv[cur]
        dkv[old] = dkv[cur]
        sl[old] = sl[cur]
        pgq[...] = gq[...]

    if last:

        @pl.when(j < nq)
        def _():
            query()
            finish()
            shift()

        @pl.when(j == nq)
        def _():
            finish()
    else:
        query()
        finish()
        shift()

        @pl.when(j == nq - 1)
        def _():
            kv_out[...] = kv[old]
            dkv_out[...] = dkv[old]
            sl_out[...] = sl[old]
            pgc_out[...] = pgq[...]


def layer_call(index, q0, nq, steps_all, rows, first_tile, part, x, g, w, wo, bias, gain, carry):
    first, last = q0 == 0, q0 + nq == steps_all
    grid = nq + (1 if last else 0)
    f0 = max(q0 - 1, 0)
    nf = q0 + nq - 1 - f0 + (1 if last else 0)
    lag = 1 if first else 0

    def in_block(j, *_):
        return (jnp.minimum(q0 + j, steps_all - 1), 0)

    def local_block(j, *_):
        return (jnp.maximum(j - lag, 0), 0)

    def pg_block(j, *_):
        return (f0 + jnp.maximum(j - lag, 0), 0)

    def whole(j, *_):
        return (0, 0)

    in_specs = [
        pl.BlockSpec((STEP, x.shape[1]), in_block),
        pl.BlockSpec((STEP, x.shape[1]), in_block),
        pl.BlockSpec(w.shape, whole),
        pl.BlockSpec(wo.shape, whole),
        pl.BlockSpec(bias.shape, whole),
        pl.BlockSpec(gain.shape, whole),
    ]
    operands = [x, g, w, wo, bias, gain]
    carry_shapes = [
        jax.ShapeDtypeStruct((STEP, SPAN), BF16),
        jax.ShapeDtypeStruct((STEP, SPAN), F32),
        jax.ShapeDtypeStruct((STEP, SPAN), F32),
        jax.ShapeDtypeStruct((STEP, SPAN), BF16),
    ]
    sum_shape = jax.ShapeDtypeStruct((8, 5 * WIDTH), F32)
    aliases = {}
    if not first:
        in_specs += [pl.BlockSpec(s.shape, whole) for s in carry_shapes + [sum_shape]]
        in_specs += [pl.BlockSpec(memory_space=pl.ANY)] * 2
        operands += list(carry)
        aliases = {2 + 11: 0, 2 + 12: 1}
    out_shape = [
        jax.ShapeDtypeStruct((rows, 4 * WIDTH), BF16),
        jax.ShapeDtypeStruct((rows, WIDTH), BF16),
        jax.ShapeDtypeStruct((nf * STEP, WIDTH), F32),
        jax.ShapeDtypeStruct((nf * STEP, WIDTH), BF16),
        jax.ShapeDtypeStruct((nf * STEP, WIDTH), BF16),
        jax.ShapeDtypeStruct((nf * STEP, HEAD), BF16),
        jax.ShapeDtypeStruct((nf * STEP, HEAD), BF16),
        sum_shape,
    ]
    out_specs = [
        pl.BlockSpec((STEP, 4 * WIDTH), pg_block),
        pl.BlockSpec((STEP, WIDTH), in_block),
        pl.BlockSpec((STEP, WIDTH), local_block),
        pl.BlockSpec((STEP, WIDTH), local_block),
        pl.BlockSpec((STEP, WIDTH), local_block),
        pl.BlockSpec((STEP, HEAD), local_block),
        pl.BlockSpec((STEP, HEAD), local_block),
        pl.BlockSpec(sum_shape.shape, whole),
    ]
    if not last:
        out_shape += carry_shapes
        out_specs += [pl.BlockSpec(s.shape, whole) for s in carry_shapes]
    macs = nq * STEP * (1024 * 1024 * 2 + 256 * 1024 + 6 * 256 * 256)
    return pl.pallas_call(
        functools.partial(layer_kernel, first, last, q0, nq, first_tile.shape[0]),
        out_shape=out_shape,
        grid_spec=pltpu.PrefetchScalarGridSpec(
            num_scalar_prefetch=2,
            grid=(grid,),
            in_specs=in_specs,
            out_specs=out_specs,
            scratch_shapes=[
                pltpu.VMEM((2 * STEP, SPAN), BF16),
                pltpu.VMEM((2 * STEP, SPAN), F32),
                pltpu.VMEM((2 * STEP, SPAN), F32),
                pltpu.VMEM((STEP, SPAN), BF16),
                pltpu.VMEM((STEP, SPAN), BF16),
                pltpu.VMEM((STEP, SPAN), F32),
                pltpu.VMEM((STEP, WIDTH), F32),
            ],
        ),
        input_output_aliases=aliases,
        compiler_params=pltpu.CompilerParams(
            dimension_semantics=("arbitrary",), vmem_limit_bytes=40 * 1024 * 1024
        ),
        cost_estimate=pl.CostEstimate(
            flops=4 * macs, bytes_accessed=grid * STEP * 9000, transcendentals=nq * STEP * 2048
        ),
        name="layer_rows",
    )(first_tile, part, *operands)


def ring(step):
    return [(i, (i + step) % 4) for i in range(4)]


def dp_perm(axis, step):
    pairs = []
    for i in range(32):
        z, y, c = i // 8, i // 2 % 4, i % 2
        if axis == "z":
            z = (z + step) % 4
        elif axis == "y":
            y = (y + step) % 4
        else:
            c = (c + step) % 2
        pairs.append((i, z * 8 + y * 2 + c))
    return pairs


def pick(array, index):
    return lax.dynamic_index_in_dim(array, index, 0, keepdims=False)


def reduce_stage(array, axis, place):
    total = pick(array, place)
    got = []
    for step in (1, 3, 2):
        sent = pick(array, lax.rem(place + step, 4)).astype(BF16)
        got.append(lax.ppermute(sent, "dp", dp_perm(axis, step)))
    return total + got[0].astype(F32) + got[1].astype(F32) + got[2].astype(F32)


def gather_stage(array, axis):
    got = [array] + [lax.ppermute(array, "dp", dp_perm(axis, step)) for step in (1, 2, 3)]
    return jnp.stack(got)


def unrelate(array, dim, place):
    order = lax.rem(place - jnp.arange(4, dtype=jnp.int32) + 4, 4)
    return jnp.take(array, order, axis=dim)


def sum_over_dp(payload, index):
    z, y, c = index // 8, index // 2 % 4, index % 2
    pieces = payload.reshape(2, 2, 4, 4, 16, payload.shape[1])
    sent = pick(pieces, 1 - c).astype(BF16)
    mine = pick(pieces, c) + lax.ppermute(sent, "dp", dp_perm("c", 1)).astype(F32)
    one = reduce_stage(mine[0], "y", y)
    two = reduce_stage(mine[1], "z", z)
    one = reduce_stage(one, "z", z).astype(BF16)
    two = reduce_stage(two, "y", y).astype(BF16)
    one = gather_stage(one, "z")
    two = gather_stage(two, "y")
    one = gather_stage(one, "y")
    two = gather_stage(two, "z")
    both = jnp.stack([one, two])
    other = lax.ppermute(both, "dp", dp_perm("c", 1))
    full = jnp.stack([jnp.where(c == 0, both, other), jnp.where(c == 0, other, both)])
    one = unrelate(unrelate(full[:, 0], 1, y), 2, z)
    two = unrelate(unrelate(full[:, 1], 1, z), 2, y)
    return jnp.stack([one, two], axis=1).reshape(payload.shape).astype(F32)


def body(events, upstream, proj_weight, proj_bias, norm_gain, out_weight, lengths, owners):
    model_width = events.shape[1]
    rows = events.shape[0]
    local_width = out_weight.shape[0]
    home_tiles = lengths.shape[1]
    device_count = lax.axis_size("dp")
    my_index = lax.axis_index("dp")
    my_part = lax.axis_index("mp")
    weight_in = proj_weight.reshape(model_width, 4 * local_width)
    bias_in = proj_bias.reshape(1, 4 * local_width)
    gain = norm_gain.reshape(1, local_width)
    mine = lengths[my_index]
    ends = jnp.cumsum(mine, dtype=jnp.int32)
    begins = ends - mine
    tile_ids = jnp.arange(home_tiles, dtype=jnp.int32)[:, None]
    inside = (tile_ids >= begins[None]) & (tile_ids < ends[None])
    first_tile = jnp.max(jnp.where(inside, begins[None], -1), axis=1).astype(jnp.int32)
    part = my_part.astype(jnp.int32).reshape(1)

    own_rows = lax.dynamic_slice_in_dim(upstream, my_part * local_width, local_width, 1)
    used = jnp.repeat(first_tile >= 0, TILE)[:, None]
    own_rows = jnp.where(used, own_rows, jnp.zeros((), BF16))

    steps_all = rows // STEP
    carry = None
    q0 = 0
    pieces = []
    done = 0
    for index, nq in enumerate(CALLS):
        outs = layer_call(
            index, q0, nq, steps_all, rows, first_tile, part,
            events, upstream, weight_in, out_weight, bias_in, gain, carry,
        )
        grads, hidden, own, s1f, s1b, r2f, r2b, sums = outs[:8]
        carry = list(outs[8:]) + [sums, grads, hidden]
        q0 += nq
        t1f = lax.ppermute(s1f, "mp", ring(1))
        t1b = lax.ppermute(s1b, "mp", ring(3))
        t2f = lax.ppermute((r2f.astype(F32) + t1f[:, :HEAD].astype(F32)).astype(BF16), "mp", ring(1))
        t2b = lax.ppermute((r2b.astype(F32) + t1b[:, HEAD:].astype(F32)).astype(BF16), "mp", ring(3))
        count = own.shape[0]
        left = t1b[:, :HEAD].astype(F32) + t2f.astype(F32)
        right = t1f[:, HEAD:].astype(F32) + t2b.astype(F32)
        total = own + jnp.concatenate([left, right], axis=1) + own_rows[done : done + count].astype(F32)
        pieces.append(total.astype(BF16))
        done += count
    event_grads = jnp.concatenate(pieces, axis=0)

    in_grad = dot(events, grads, TN)
    out_grad = dot(upstream, hidden, TN)
    small = jnp.sum(sums, axis=0).reshape(64, 5 * WIDTH // 64)
    small = jnp.pad(small, ((0, 0), (0, 2048 - small.shape[1]))).reshape(1024, 128)
    payload = jnp.concatenate([in_grad, out_grad, small], axis=1)
    summed = sum_over_dp(payload, my_index) * (1.0 / device_count)
    small = summed[:, 5 * WIDTH :].reshape(64, 2048)[:, : 5 * WIDTH // 64].reshape(5 * WIDTH)
    return (
        event_grads,
        summed[:, : 4 * WIDTH].reshape(model_width, 4, local_width),
        small[: 4 * WIDTH].reshape(4, local_width),
        small[4 * WIDTH :],
        summed[:, 4 * WIDTH : 5 * WIDTH].T,
    )


def solution(mesh):
    placed = (
        P("dp", None),
        P("dp", None),
        P(None, None, "mp"),
        P(None, "mp"),
        P("mp"),
        P("mp", None),
        P(),
        P(),
    )
    return jax.shard_map(
        body,
        mesh=mesh,
        in_specs=placed,
        out_specs=(P("dp", "mp"), P(None, None, "mp"), P(None, "mp"), P("mp"), P("mp", None)),
        check_vma=False,
    )
```

```python
import functools

import jax
import jax.numpy as jnp
from jax import lax
from jax.experimental import pallas as pl
from jax.experimental.pallas import tpu as pltpu
from jax.sharding import Mesh, PartitionSpec as P

HEADS = 8
TILE = 64
EPSILON = 1e-05
STEP = 512
PAIR = 128
HEAD = 128
WIDTH = 256
SPAN = 512
MODEL = 1024
COLUMNS = 5 * WIDTH + 128
PIECES = 8
ROW_PARTS = 3
F32 = jnp.float32
BF16 = jnp.bfloat16
NT = (((1,), (1,)), ((), ()))
TN = (((0,), (0,)), ((), ()))
DP = ("z", "y", "c")


def dot(a, b, dims=(((1,), (0,)), ((), ()))):
    return lax.dot_general(a, b, dims, preferred_element_type=F32)


def sigmoid(v):
    return 0.5 * jnp.tanh(0.5 * v) + 0.5


def tile_column(values, rows):
    ids = lax.broadcasted_iota(jnp.int32, (rows, 1), 0)
    column = jnp.full((rows, 1), values[0], jnp.int32)
    for i in range(1, len(values)):
        column = jnp.where(ids >= i * TILE, values[i], column)
    return column


def layer_kernel(
    steps, first_ref, core_ref, x_ref, g_ref, xp_ref, w_ref, wo_ref, b_ref, gain_ref, ones_ref,
    pg_out, sent_out, mine_out,
    kv, dkv, sl, pgq, gq, slgq, hg, hid, pgs, acc, sums, attn_s, dsl_s, mix_s, dm_s,
):
    j = pl.program_id(0)
    cur = pl.ds(STEP, STEP)
    old = pl.ds(0, STEP)
    pairs = STEP // PAIR
    chains = [(i, h) for i in range(pairs) for h in range(2)]

    @pl.when(j == 0)
    def _():
        kv[old] = jnp.zeros((STEP, SPAN), BF16)
        dkv[old] = jnp.zeros((STEP, SPAN), F32)
        sl[old] = jnp.zeros((STEP, SPAN), F32)
        pgq[...] = jnp.zeros((STEP, SPAN), BF16)
        pgs[...] = jnp.zeros(pgs.shape, BF16)
        acc[...] = jnp.zeros(acc.shape, F32)
        sums[...] = jnp.zeros(sums.shape, F32)

    def in_grad_piece(n):
        depth = MODEL // PIECES
        r = slice(n * depth, (n + 1) * depth)
        acc[r, 0 : 4 * WIDTH] += dot(xp_ref[:, r], pgs[...], TN)

    def finish():
        pg_out[:, 0:WIDTH] = pgq[:, 0:WIDTH]
        pg_out[:, WIDTH : 2 * WIDTH] = (dkv[old, 0:WIDTH] * sl[old, 0:WIDTH]).astype(BF16)
        pg_out[:, 2 * WIDTH : 3 * WIDTH] = pgq[:, WIDTH:]
        pg_out[:, 3 * WIDTH :] = (dkv[old, WIDTH:] * sl[old, WIDTH:]).astype(BF16)
        grads = pg_out[...]
        pgs[...] = grads
        sums[:, 0 : 4 * WIDTH] += jnp.sum(grads.astype(F32).reshape(STEP // 8, 8, 4 * WIDTH), axis=0)

    def rows_of(i):
        return slice(i * PAIR, (i + 1) * PAIR)

    def window(i):
        return pl.ds(STEP - PAIR + i * PAIR, 2 * PAIR)

    def first_cols(h):
        return slice(h * HEAD, (h + 1) * HEAD)

    def second_cols(h):
        return slice(WIDTH + h * HEAD, WIDTH + (h + 1) * HEAD)

    def query():
        t0 = j * (STEP // TILE)
        firsts = [first_ref[t0 + i] for i in range(STEP // TILE)]
        base = j * STEP
        starts = [jnp.where(f >= 0, f * TILE - base, STEP) for f in firsts]
        x = x_ref[...]
        used = tile_column(firsts, STEP) >= 0
        g = jnp.where(used, g_ref[...], jnp.zeros((), BF16))
        hg[...] = dot(g, wo_ref[...], NT)
        for part in range(4):
            cols = slice(part * WIDTH, (part + 1) * WIDTH)
            pre = dot(x, w_ref[:, cols]) + b_ref[:, cols]
            sig = sigmoid(pre)
            act = pre * sig
            slope = sig + act * (1.0 - sig)
            half = slice(0, WIDTH) if part < 2 else slice(WIDTH, SPAN)
            if part % 2 == 0:
                gq[:, half] = act.astype(BF16)
                slgq[:, half] = slope
            else:
                kv[cur, half] = act.astype(BF16)
                sl[cur, half] = slope
        scale = HEAD**-0.5
        row = lax.broadcasted_iota(jnp.int32, (PAIR, 2 * PAIR), 0)
        col = lax.broadcasted_iota(jnp.int32, (PAIR, 2 * PAIR), 1) - PAIR
        visible = []
        for i in range(pairs):
            begin = tile_column(starts[2 * i : 2 * i + 2], PAIR) - i * PAIR
            visible.append((col >= begin) & (col <= row))
        for n, (i, h) in enumerate(chains):
            s = dot(gq[rows_of(i), second_cols(h)], kv[window(i), second_cols(h)], NT) * scale
            sig = jnp.where(visible[i], sigmoid(s), 0.0)
            a = s * sig
            attn = a.astype(BF16)
            attn_s[i, h] = attn
            dsl_s[i, h] = (sig + a * (1.0 - sig)) * scale
            mix_s[rows_of(i), first_cols(h)] = dot(attn, kv[window(i), first_cols(h)])
            for t in range(n * PIECES // len(chains), (n + 1) * PIECES // len(chains)):
                in_grad_piece(t)
        ones = ones_ref[...]
        mix = mix_s[...]
        high = mix.astype(BF16)
        low = (mix - high.astype(F32)).astype(BF16)
        centered = mix - (dot(high, ones) + dot(low, ones))
        inverse = lax.rsqrt(dot((centered * centered).astype(BF16), ones) + EPSILON)
        normed = centered * inverse
        gate = gq[:, 0:WIDTH].astype(F32)
        gain = gain_ref[...]
        local = hg[...]
        scaled = normed * gain
        hid[...] = (scaled * gate).astype(BF16)
        gq[:, 0:WIDTH] = (local * scaled * slgq[:, 0:WIDTH]).astype(BF16)
        lg = local * gate
        gn = lg * normed
        sums[:, 4 * WIDTH :] += jnp.sum(gn.reshape(STEP // 8, 8, WIDTH), axis=0)
        ng = lg * gain
        mean_one = dot(ng.astype(BF16), ones)
        mean_two = dot((gn * gain).astype(BF16), ones)
        dm_s[...] = ((ng - mean_one - normed * mean_two) * inverse).astype(BF16)
        for i, h in chains:
            hc, kc = first_cols(h), second_cols(h)
            dm = dm_s[rows_of(i), hc]
            q = gq[rows_of(i), kc]
            da = dot(dm, kv[window(i), hc], NT)
            sg = (da * dsl_s[i, h]).astype(BF16)
            dq = dot(sg, kv[window(i), kc])
            dv = dot(attn_s[i, h], dm, TN)
            dk = dot(sg, q, TN)
            before = pl.ds(STEP - PAIR + i * PAIR, PAIR)
            here = pl.ds(STEP + i * PAIR, PAIR)
            dkv[before, hc] += dv[:PAIR]
            dkv[here, hc] = dv[PAIR:]
            dkv[before, kc] += dk[:PAIR]
            dkv[here, kc] = dk[PAIR:]
            gq[rows_of(i), kc] = (dq * slgq[rows_of(i), kc]).astype(BF16)
        acc[:, 4 * WIDTH : 5 * WIDTH] += dot(g, hid[...], TN)

    @pl.when(j < steps)
    def _():
        query()
        finish()
        kv[old] = kv[cur]
        dkv[old] = dkv[cur]
        sl[old] = sl[cur]
        pgq[...] = gq[...]

    @pl.when(j == steps)
    def _():
        for n in range(PIECES):
            in_grad_piece(n)
        finish()

    @pl.when(j == steps + 1)
    def _():
        for n in range(PIECES):
            in_grad_piece(n)
        total = jnp.sum(sums[...], axis=0, keepdims=True)
        for p in range(5 * WIDTH // 128):
            acc[pl.ds(32 * p, 8), 5 * WIDTH :] = jnp.broadcast_to(total[:, p * 128 : (p + 1) * 128], (8, 128))
        core = core_ref[0]
        half = MODEL // 2
        mine_out[...] = acc[pl.ds(pl.multiple_of(core * half, half), half), :]
        sent_out[...] = acc[pl.ds(pl.multiple_of((1 - core) * half, half), half), :].astype(BF16)


def layer(first_tile, core, x, g, w, wo, bias, gain):
    rows = x.shape[0]
    steps = rows // STEP
    half = MODEL // 2
    ones = jnp.kron(jnp.eye(2, dtype=F32), jnp.full((HEAD, HEAD), 1.0 / HEAD, F32)).astype(BF16)

    def in_block(j, *_):
        return (jnp.minimum(j, steps - 1), 0)

    def out_block(j, *_):
        return (jnp.clip(j - 1, 0, steps - 1), 0)

    def late_block(j, *_):
        return (jnp.maximum(j - 2, 0), 0)

    def whole(j, *_):
        return (0, 0)

    macs = rows * (MODEL * MODEL * 2 + 2 * WIDTH * MODEL + 6 * WIDTH * WIDTH)
    return pl.pallas_call(
        functools.partial(layer_kernel, steps),
        out_shape=[
            jax.ShapeDtypeStruct((rows, MODEL), BF16),
            jax.ShapeDtypeStruct((half, COLUMNS), BF16),
            jax.ShapeDtypeStruct((half, COLUMNS), F32),
        ],
        grid_spec=pltpu.PrefetchScalarGridSpec(
            num_scalar_prefetch=2,
            grid=(steps + 2,),
            in_specs=[
                pl.BlockSpec((STEP, MODEL), in_block),
                pl.BlockSpec((STEP, MODEL), in_block),
                pl.BlockSpec((STEP, MODEL), late_block),
                pl.BlockSpec(w.shape, whole),
                pl.BlockSpec(wo.shape, whole),
                pl.BlockSpec(bias.shape, whole),
                pl.BlockSpec(gain.shape, whole),
                pl.BlockSpec(ones.shape, whole),
            ],
            out_specs=[
                pl.BlockSpec((STEP, MODEL), out_block),
                pl.BlockSpec((half, COLUMNS), whole),
                pl.BlockSpec((half, COLUMNS), whole),
            ],
            scratch_shapes=[
                pltpu.VMEM((2 * STEP, SPAN), BF16),
                pltpu.VMEM((2 * STEP, SPAN), F32),
                pltpu.VMEM((2 * STEP, SPAN), F32),
                pltpu.VMEM((STEP, SPAN), BF16),
                pltpu.VMEM((STEP, SPAN), BF16),
                pltpu.VMEM((STEP, SPAN), F32),
                pltpu.VMEM((STEP, WIDTH), F32),
                pltpu.VMEM((STEP, WIDTH), BF16),
                pltpu.VMEM((STEP, MODEL), BF16),
                pltpu.VMEM((MODEL, COLUMNS), F32),
                pltpu.VMEM((8, 5 * WIDTH), F32),
                pltpu.VMEM((STEP // PAIR, 2, PAIR, 2 * PAIR), BF16),
                pltpu.VMEM((STEP // PAIR, 2, PAIR, 2 * PAIR), F32),
                pltpu.VMEM((STEP, WIDTH), F32),
                pltpu.VMEM((STEP, WIDTH), BF16),
            ],
        ),
        compiler_params=pltpu.CompilerParams(
            dimension_semantics=("arbitrary",), vmem_limit_bytes=56 * 1024 * 1024
        ),
        cost_estimate=pl.CostEstimate(flops=2 * macs, bytes_accessed=rows * 8000, transcendentals=rows * 2048),
        name="layer",
    )(first_tile, core, x, g, x, w, wo, bias, gain, ones)


def partial_kernel(pg_ref, w_ref, out_ref):
    grads = pg_ref[...]
    for d in range(4):
        out_ref[d] = dot(grads, w_ref[d * WIDTH : (d + 1) * WIDTH, :], NT).astype(BF16)


def partial_rows(grads, w, begin, count):
    block = 512
    return pl.pallas_call(
        partial_kernel,
        out_shape=jax.ShapeDtypeStruct((4, count, WIDTH), BF16),
        grid=(count // block,),
        in_specs=[
            pl.BlockSpec((block, MODEL), lambda i: (begin // block + i, 0)),
            pl.BlockSpec(w.shape, lambda i: (0, 0)),
        ],
        out_specs=pl.BlockSpec((4, block, WIDTH), lambda i: (0, i, 0)),
        compiler_params=pltpu.CompilerParams(
            dimension_semantics=("arbitrary",), vmem_limit_bytes=32 * 1024 * 1024
        ),
        cost_estimate=pl.CostEstimate(
            flops=2 * count * MODEL * MODEL, bytes_accessed=count * 4096 + w.size * 2, transcendentals=0
        ),
        name="partial_rows",
    )(grads, w)


def event_kernel(begin, block, first_ref, part_ref, got_ref, g_ref, *refs):
    out_ref = refs[-1]
    t0 = (begin + pl.program_id(0) * block) // TILE
    firsts = [first_ref[t0 + i] for i in range(block // TILE)]
    used = tile_column(firsts, block) >= 0
    g = jnp.where(used, g_ref[...], jnp.zeros((), BF16)).astype(F32)
    total = (got_ref[0].astype(F32) + got_ref[1].astype(F32)) + (got_ref[2].astype(F32) + got_ref[3].astype(F32))
    out_ref[...] = (total + g).astype(BF16)


def event_rows(first_tile, part, got, g, begin, out):
    block = 512
    count = got.shape[1]
    in_specs = [
        pl.BlockSpec((4, block, WIDTH), lambda i, f, p: (0, i, 0)),
        pl.BlockSpec((block, WIDTH), lambda i, f, p: (begin // block + i, p[0])),
    ]
    operands = [got, g]
    aliases = {}
    if out is not None:
        in_specs.append(pl.BlockSpec(memory_space=pl.ANY))
        operands.append(out)
        aliases = {4: 0}
    return pl.pallas_call(
        functools.partial(event_kernel, begin, block),
        out_shape=jax.ShapeDtypeStruct((g.shape[0], WIDTH), BF16),
        grid_spec=pltpu.PrefetchScalarGridSpec(
            num_scalar_prefetch=2,
            grid=(count // block,),
            in_specs=in_specs,
            out_specs=pl.BlockSpec((block, WIDTH), lambda i, f, p: (begin // block + i, 0)),
        ),
        input_output_aliases=aliases,
        compiler_params=pltpu.CompilerParams(
            dimension_semantics=("arbitrary",), vmem_limit_bytes=16 * 1024 * 1024
        ),
        cost_estimate=pl.CostEstimate(flops=count * 2048, bytes_accessed=count * 3072, transcendentals=0),
        name="event_rows",
    )(first_tile, part, *operands)


def weights_kernel(core_ref, mine_ref, other_ref, pw_out, ow_out, small_out):
    i = pl.program_id(0)
    half = MODEL // 2
    own = core_ref[0] == i

    def write(ref):
        values = ref[...].astype(F32) * (1.0 / 32.0)
        for p in range(4):
            pw_out[:, p, :] = values[:, p * WIDTH : (p + 1) * WIDTH]
        ow_out[...] = values[:, 4 * WIDTH : 5 * WIDTH].T

        @pl.when(i == 0)
        def _():
            for p in range(5 * WIDTH // 128):
                small_out[:, p * 128 : (p + 1) * 128] = values[32 * p : 32 * p + 1, 5 * WIDTH :]

    @pl.when(own)
    def _():
        write(mine_ref)

    @pl.when(jnp.logical_not(own))
    def _():
        write(other_ref)


def weights_out(core, mine, other):
    half = MODEL // 2
    return pl.pallas_call(
        weights_kernel,
        out_shape=[
            jax.ShapeDtypeStruct((MODEL, 4, WIDTH), F32),
            jax.ShapeDtypeStruct((WIDTH, MODEL), F32),
            jax.ShapeDtypeStruct((1, 5 * WIDTH), F32),
        ],
        grid_spec=pltpu.PrefetchScalarGridSpec(
            num_scalar_prefetch=1,
            grid=(2,),
            in_specs=[
                pl.BlockSpec((half, COLUMNS), lambda i, c: (0, 0)),
                pl.BlockSpec((half, COLUMNS), lambda i, c: (0, 0)),
            ],
            out_specs=[
                pl.BlockSpec((half, 4, WIDTH), lambda i, c: (i, 0, 0)),
                pl.BlockSpec((WIDTH, half), lambda i, c: (0, i)),
                pl.BlockSpec((1, 5 * WIDTH), lambda i, c: (0, 0)),
            ],
        ),
        compiler_params=pltpu.CompilerParams(
            dimension_semantics=("arbitrary",), vmem_limit_bytes=40 * 1024 * 1024
        ),
        cost_estimate=pl.CostEstimate(flops=4000000, bytes_accessed=8500000, transcendentals=0),
        name="weights_out",
    )(core, mine, other)


def body(events, upstream, proj_weight, proj_bias, norm_gain, out_weight, lengths, owners):
    rows = events.shape[0]
    home_tiles = lengths.shape[1]
    my_index = lax.axis_index(DP)
    my_core = lax.axis_index("c").astype(jnp.int32).reshape(1)
    my_part = lax.axis_index("mp").astype(jnp.int32).reshape(1)
    weight_in = proj_weight.reshape(MODEL, 4 * WIDTH)
    bias_in = proj_bias.reshape(1, 4 * WIDTH)
    gain = norm_gain.reshape(1, WIDTH)
    mine = lengths[my_index]
    ends = jnp.cumsum(mine, dtype=jnp.int32)
    begins = ends - mine
    tile_ids = jnp.arange(home_tiles, dtype=jnp.int32)[:, None]
    inside = (tile_ids >= begins[None]) & (tile_ids < ends[None])
    first_tile = jnp.max(jnp.where(inside, begins[None], -1), axis=1).astype(jnp.int32)

    grads, sent, kept = layer(first_tile, my_core, events, upstream, weight_in, out_weight, bias_in, gain)

    swap = [(0, 1), (1, 0)]
    half = MODEL // 2
    kept = kept + lax.ppermute(sent, "c", swap).astype(F32)
    pieces = lax.all_to_all(kept.astype(BF16).reshape(16, half // 16, COLUMNS), ("z", "y"), 0, 0, tiled=True)
    piece = jnp.sum(pieces.astype(F32), axis=0).astype(BF16)
    pieces = lax.all_to_all(
        jnp.broadcast_to(piece[None], (16,) + piece.shape), ("z", "y"), 0, 0, tiled=True
    ).reshape(half, COLUMNS)
    other = lax.ppermute(pieces, "c", swap)
    proj_grad, out_grad, small = weights_out(my_core, pieces, other)

    event_grads = None
    count = rows // ROW_PARTS
    for n in range(ROW_PARTS):
        shares = partial_rows(grads, weight_in, n * count, count)
        got = lax.all_to_all(shares, "mp", 0, 0, tiled=True)
        event_grads = event_rows(first_tile, my_part, got, upstream, n * count, event_grads)
    return (
        event_grads,
        proj_grad,
        small[0, : 4 * WIDTH].reshape(4, WIDTH),
        small[0, 4 * WIDTH :],
        out_grad,
    )


def solution(mesh):
    grid = Mesh(mesh.devices.reshape(4, 4, 2, 4), ("z", "y", "c", "mp"))
    placed = (
        P(DP, None),
        P(DP, None),
        P(None, None, "mp"),
        P(None, "mp"),
        P("mp"),
        P("mp", None),
        P(),
        P(),
    )
    return jax.shard_map(
        body,
        mesh=grid,
        in_specs=placed,
        out_specs=(P(DP, "mp"), P(None, None, "mp"), P(None, "mp"), P("mp"), P("mp", None)),
        check_vma=False,
    )
```

```python
import functools

import jax
import jax.numpy as jnp
from jax import lax
from jax.experimental import pallas as pl
from jax.experimental.pallas import tpu as pltpu
from jax.sharding import Mesh, PartitionSpec as P

HEADS = 8
TILE = 64
EPSILON = 1e-05
STEP = 512
PAIR = 128
HEAD = 128
WIDTH = 256
SPAN = 512
MODEL = 1024
COLUMNS = 5 * WIDTH + 128
PIECES = 8
ROW_PARTS = 2
HISTORY = 3
F32 = jnp.float32
BF16 = jnp.bfloat16
NT = (((1,), (1,)), ((), ()))
TN = (((0,), (0,)), ((), ()))
DP = ("z", "y", "c")


def dot(a, b, dims=(((1,), (0,)), ((), ()))):
    return lax.dot_general(a, b, dims, preferred_element_type=F32)


def sigmoid(v):
    return 0.5 * jnp.tanh(0.5 * v) + 0.5


def tile_column(values, rows):
    ids = lax.broadcasted_iota(jnp.int32, (rows, 1), 0)
    column = jnp.full((rows, 1), values[0], jnp.int32)
    for i in range(1, len(values)):
        column = jnp.where(ids >= i * TILE, values[i], column)
    return column


def layer_kernel(
    steps, lengths_ref, place_ref, x_ref, g_ref, xp_ref, wp_ref, wo_ref, b_ref, gain_ref,
    pg_out, sent_out, mine_out, w_ref,
    first_ref, ones_ref, kv, dkv, sl, pgq, gq, slgq, hg, hid, pgs, acc, sums, attn_s, dsl_s, mix_s, dm_s,
):
    j = pl.program_id(0)
    cur = pl.ds(STEP, STEP)
    old = pl.ds(0, STEP)
    pairs = STEP // PAIR
    chains = [(i, h) for i in range(pairs) for h in range(2)]

    @pl.when(j == 0)
    def _():
        kv[old] = jnp.zeros((STEP, SPAN), BF16)
        dkv[old] = jnp.zeros((STEP, SPAN), F32)
        sl[old] = jnp.zeros((STEP, SPAN), F32)
        pgq[...] = jnp.zeros((STEP, SPAN), BF16)
        pgs[...] = jnp.zeros(pgs.shape, BF16)
        acc[...] = jnp.zeros(acc.shape, F32)
        sums[...] = jnp.zeros(sums.shape, F32)
        for p in range(4):
            w_ref[:, p * WIDTH : (p + 1) * WIDTH] = wp_ref[:, p, :]
        head_row = lax.broadcasted_iota(jnp.int32, (WIDTH, WIDTH), 0) >= HEAD
        head_col = lax.broadcasted_iota(jnp.int32, (WIDTH, WIDTH), 1) >= HEAD
        ones_ref[...] = jnp.where(head_row == head_col, 1.0 / HEAD, 0.0).astype(BF16)
        home = place_ref[0]
        tiles = steps * (STEP // TILE)

        @pl.loop(0, tiles)
        def _(t):
            first_ref[t] = -1

        def place(u, begin):
            count = lengths_ref[home, u]
            for t in range(HISTORY):

                @pl.when(t < count)
                def _():
                    first_ref[begin + t] = begin

            return begin + count

        lax.fori_loop(0, lengths_ref.shape[1], place, jnp.int32(0))

    def in_grad_piece(n):
        depth = MODEL // PIECES
        r = slice(n * depth, (n + 1) * depth)
        acc[r, 0 : 4 * WIDTH] += dot(xp_ref[:, r], pgs[...], TN)

    def finish():
        pg_out[:, 0:WIDTH] = pgq[:, 0:WIDTH]
        pg_out[:, WIDTH : 2 * WIDTH] = (dkv[old, 0:WIDTH] * sl[old, 0:WIDTH]).astype(BF16)
        pg_out[:, 2 * WIDTH : 3 * WIDTH] = pgq[:, WIDTH:]
        pg_out[:, 3 * WIDTH :] = (dkv[old, WIDTH:] * sl[old, WIDTH:]).astype(BF16)
        grads = pg_out[...]
        pgs[...] = grads
        sums[:, 0 : 4 * WIDTH] += jnp.sum(grads.astype(F32).reshape(STEP // 8, 8, 4 * WIDTH), axis=0)

    def rows_of(i):
        return slice(i * PAIR, (i + 1) * PAIR)

    def window(i):
        return pl.ds(STEP - PAIR + i * PAIR, 2 * PAIR)

    def first_cols(h):
        return slice(h * HEAD, (h + 1) * HEAD)

    def second_cols(h):
        return slice(WIDTH + h * HEAD, WIDTH + (h + 1) * HEAD)

    def query():
        t0 = j * (STEP // TILE)
        firsts = [first_ref[t0 + i] for i in range(STEP // TILE)]
        base = j * STEP
        starts = [jnp.where(f >= 0, f * TILE - base, STEP) for f in firsts]
        x = x_ref[...]
        used = tile_column(firsts, STEP) >= 0
        g = jnp.where(used, g_ref[...], jnp.zeros((), BF16))
        hg[...] = dot(g, wo_ref[...], NT)
        for part in range(4):
            cols = slice(part * WIDTH, (part + 1) * WIDTH)
            pre = dot(x, w_ref[:, cols]) + b_ref[part : part + 1, :]
            sig = sigmoid(pre)
            act = pre * sig
            slope = sig + act * (1.0 - sig)
            half = slice(0, WIDTH) if part < 2 else slice(WIDTH, SPAN)
            if part % 2 == 0:
                gq[:, half] = act.astype(BF16)
                slgq[:, half] = slope
            else:
                kv[cur, half] = act.astype(BF16)
                sl[cur, half] = slope
        scale = HEAD**-0.5
        row = lax.broadcasted_iota(jnp.int32, (PAIR, 2 * PAIR), 0)
        col = lax.broadcasted_iota(jnp.int32, (PAIR, 2 * PAIR), 1) - PAIR
        visible = []
        for i in range(pairs):
            begin = tile_column(starts[2 * i : 2 * i + 2], PAIR) - i * PAIR
            visible.append((col >= begin) & (col <= row))
        for n, (i, h) in enumerate(chains):
            s = dot(gq[rows_of(i), second_cols(h)], kv[window(i), second_cols(h)], NT) * scale
            sig = jnp.where(visible[i], sigmoid(s), 0.0)
            a = s * sig
            attn = a.astype(BF16)
            attn_s[i, h] = attn
            dsl_s[i, h] = (sig + a * (1.0 - sig)) * scale
            mix_s[rows_of(i), first_cols(h)] = dot(attn, kv[window(i), first_cols(h)])
            for t in range(n * PIECES // len(chains), (n + 1) * PIECES // len(chains)):
                in_grad_piece(t)
        ones = ones_ref[...]
        mix = mix_s[...]
        high = mix.astype(BF16)
        low = (mix - high.astype(F32)).astype(BF16)
        centered = mix - (dot(high, ones) + dot(low, ones))
        inverse = lax.rsqrt(dot((centered * centered).astype(BF16), ones) + EPSILON)
        normed = centered * inverse
        gate = gq[:, 0:WIDTH].astype(F32)
        gain = gain_ref[...]
        local = hg[...]
        scaled = normed * gain
        hid[...] = (scaled * gate).astype(BF16)
        gq[:, 0:WIDTH] = (local * scaled * slgq[:, 0:WIDTH]).astype(BF16)
        lg = local * gate
        gn = lg * normed
        sums[:, 4 * WIDTH :] += jnp.sum(gn.reshape(STEP // 8, 8, WIDTH), axis=0)
        ng = lg * gain
        mean_one = dot(ng.astype(BF16), ones)
        mean_two = dot((gn * gain).astype(BF16), ones)
        dm_s[...] = ((ng - mean_one - normed * mean_two) * inverse).astype(BF16)
        for i, h in chains:
            hc, kc = first_cols(h), second_cols(h)
            dm = dm_s[rows_of(i), hc]
            q = gq[rows_of(i), kc]
            da = dot(dm, kv[window(i), hc], NT)
            sg = (da * dsl_s[i, h]).astype(BF16)
            dq = dot(sg, kv[window(i), kc])
            dv = dot(attn_s[i, h], dm, TN)
            dk = dot(sg, q, TN)
            before = pl.ds(STEP - PAIR + i * PAIR, PAIR)
            here = pl.ds(STEP + i * PAIR, PAIR)
            dkv[before, hc] += dv[:PAIR]
            dkv[here, hc] = dv[PAIR:]
            dkv[before, kc] += dk[:PAIR]
            dkv[here, kc] = dk[PAIR:]
            gq[rows_of(i), kc] = (dq * slgq[rows_of(i), kc]).astype(BF16)
        acc[:, 4 * WIDTH : 5 * WIDTH] += dot(g, hid[...], TN)

    @pl.when(j < steps)
    def _():
        query()
        finish()
        kv[old] = kv[cur]
        dkv[old] = dkv[cur]
        sl[old] = sl[cur]
        pgq[...] = gq[...]

    @pl.when(j == steps)
    def _():
        for n in range(PIECES):
            in_grad_piece(n)
        finish()

    @pl.when(j == steps + 1)
    def _():
        for n in range(PIECES):
            in_grad_piece(n)
        total = jnp.sum(sums[...], axis=0, keepdims=True)
        for p in range(5 * WIDTH // 128):
            acc[pl.ds(32 * p, 8), 5 * WIDTH :] = jnp.broadcast_to(total[:, p * 128 : (p + 1) * 128], (8, 128))
        core = place_ref[1]
        half = MODEL // 2
        mine_out[...] = acc[pl.ds(pl.multiple_of(core * half, half), half), :]
        sent_out[...] = acc[pl.ds(pl.multiple_of((1 - core) * half, half), half), :].astype(BF16)


def layer(lengths, place, x, g, w, wo, bias, gain):
    rows = x.shape[0]
    steps = rows // STEP
    half = MODEL // 2

    def in_block(j, *_):
        return (jnp.minimum(j, steps - 1), 0)

    def out_block(j, *_):
        return (jnp.clip(j - 1, 0, steps - 1), 0)

    def late_block(j, *_):
        return (jnp.maximum(j - 2, 0), 0)

    def whole(j, *_):
        return (0, 0)

    macs = rows * (MODEL * MODEL * 2 + 2 * WIDTH * MODEL + 6 * WIDTH * WIDTH)
    return pl.pallas_call(
        functools.partial(layer_kernel, steps),
        out_shape=[
            jax.ShapeDtypeStruct((rows, MODEL), BF16),
            jax.ShapeDtypeStruct((half, COLUMNS), BF16),
            jax.ShapeDtypeStruct((half, COLUMNS), F32),
            jax.ShapeDtypeStruct((MODEL, 4 * WIDTH), BF16),
        ],
        grid_spec=pltpu.PrefetchScalarGridSpec(
            num_scalar_prefetch=2,
            grid=(steps + 2,),
            in_specs=[
                pl.BlockSpec((STEP, MODEL), in_block),
                pl.BlockSpec((STEP, MODEL), in_block),
                pl.BlockSpec((STEP, MODEL), late_block),
                pl.BlockSpec(w.shape, lambda j, *_: (0, 0, 0)),
                pl.BlockSpec(wo.shape, whole),
                pl.BlockSpec(bias.shape, whole),
                pl.BlockSpec(gain.shape, whole),
            ],
            out_specs=[
                pl.BlockSpec((STEP, MODEL), out_block),
                pl.BlockSpec((half, COLUMNS), whole),
                pl.BlockSpec((half, COLUMNS), whole),
                pl.BlockSpec((MODEL, 4 * WIDTH), whole),
            ],
            scratch_shapes=[
                pltpu.SMEM((steps * (STEP // TILE),), jnp.int32),
                pltpu.VMEM((WIDTH, WIDTH), BF16),
                pltpu.VMEM((2 * STEP, SPAN), BF16),
                pltpu.VMEM((2 * STEP, SPAN), F32),
                pltpu.VMEM((2 * STEP, SPAN), F32),
                pltpu.VMEM((STEP, SPAN), BF16),
                pltpu.VMEM((STEP, SPAN), BF16),
                pltpu.VMEM((STEP, SPAN), F32),
                pltpu.VMEM((STEP, WIDTH), F32),
                pltpu.VMEM((STEP, WIDTH), BF16),
                pltpu.VMEM((STEP, MODEL), BF16),
                pltpu.VMEM((MODEL, COLUMNS), F32),
                pltpu.VMEM((8, 5 * WIDTH), F32),
                pltpu.VMEM((STEP // PAIR, 2, PAIR, 2 * PAIR), BF16),
                pltpu.VMEM((STEP // PAIR, 2, PAIR, 2 * PAIR), F32),
                pltpu.VMEM((STEP, WIDTH), F32),
                pltpu.VMEM((STEP, WIDTH), BF16),
            ],
        ),
        compiler_params=pltpu.CompilerParams(
            dimension_semantics=("arbitrary",), vmem_limit_bytes=56 * 1024 * 1024
        ),
        cost_estimate=pl.CostEstimate(flops=2 * macs, bytes_accessed=rows * 8000, transcendentals=rows * 2048),
        name="layer",
    )(lengths, place, x, g, x, w, wo, bias, gain)


def partial_kernel(place_ref, pg_ref, w_ref, own_out, ahead_out, across_out, behind_out):
    grads = pg_ref[...]
    me = place_ref[2]

    def chunk(shift):
        start = pl.multiple_of(lax.rem(me + shift, 4) * WIDTH, WIDTH)
        return dot(grads, w_ref[pl.ds(start, WIDTH), :], NT)

    ahead_out[...] = chunk(1).astype(BF16)
    across_out[...] = chunk(2).astype(BF16)
    behind_out[...] = chunk(3).astype(BF16)
    own_out[...] = chunk(0)


def partial_rows(place, grads, w, begin, count):
    block = 512
    here = pl.BlockSpec((block, WIDTH), lambda i, p: (i, 0))
    return pl.pallas_call(
        partial_kernel,
        out_shape=[jax.ShapeDtypeStruct((count, WIDTH), F32)] + [jax.ShapeDtypeStruct((count, WIDTH), BF16)] * 3,
        grid_spec=pltpu.PrefetchScalarGridSpec(
            num_scalar_prefetch=1,
            grid=(count // block,),
            in_specs=[
                pl.BlockSpec((block, MODEL), lambda i, p: (begin // block + i, 0)),
                pl.BlockSpec(w.shape, lambda i, p: (0, 0)),
            ],
            out_specs=[here, here, here, here],
        ),
        compiler_params=pltpu.CompilerParams(
            dimension_semantics=("arbitrary",), vmem_limit_bytes=56 * 1024 * 1024
        ),
        cost_estimate=pl.CostEstimate(
            flops=2 * count * MODEL * MODEL, bytes_accessed=count * 4096 + w.size * 2, transcendentals=0
        ),
        name="partial_rows",
    )(place, grads, w)


def event_kernel(begin, block, lengths_ref, place_ref, own_ref, a_ref, b_ref, c_ref, g_ref, *refs):
    out_ref = refs[-1]
    home = place_ref[0]
    tiles = lax.fori_loop(0, lengths_ref.shape[1], lambda u, t: t + lengths_ref[home, u], jnp.int32(0))
    row = lax.broadcasted_iota(jnp.int32, (block, WIDTH), 0) + begin + pl.program_id(0) * block
    g = jnp.where(row < tiles * TILE, g_ref[...].astype(F32), 0.0)
    got = a_ref[...].astype(F32) + b_ref[...].astype(F32) + c_ref[...].astype(F32)
    out_ref[...] = (own_ref[...] + got + g).astype(BF16)


def event_rows(lengths, place, shares, g, begin, out):
    block = 512
    count = shares[0].shape[0]
    here = pl.BlockSpec((block, WIDTH), lambda i, f, p: (i, 0))
    in_specs = [here] * 4 + [pl.BlockSpec((block, WIDTH), lambda i, f, p: (begin // block + i, p[2]))]
    operands = list(shares) + [g]
    aliases = {}
    if out is not None:
        in_specs.append(pl.BlockSpec(memory_space=pl.ANY))
        operands.append(out)
        aliases = {7: 0}
    return pl.pallas_call(
        functools.partial(event_kernel, begin, block),
        out_shape=jax.ShapeDtypeStruct((g.shape[0], WIDTH), BF16),
        grid_spec=pltpu.PrefetchScalarGridSpec(
            num_scalar_prefetch=2,
            grid=(count // block,),
            in_specs=in_specs,
            out_specs=pl.BlockSpec((block, WIDTH), lambda i, f, p: (begin // block + i, 0)),
        ),
        input_output_aliases=aliases,
        compiler_params=pltpu.CompilerParams(
            dimension_semantics=("arbitrary",), vmem_limit_bytes=56 * 1024 * 1024
        ),
        cost_estimate=pl.CostEstimate(flops=count * 2048, bytes_accessed=count * 3072, transcendentals=0),
        name="event_rows",
    )(lengths, place, *operands)


def spread_kernel(got_ref, out_ref):
    total = jnp.sum(got_ref[...].astype(F32), axis=0).astype(BF16)
    out_ref[...] = jnp.broadcast_to(total[None], out_ref.shape)


def spread(pieces):
    return pl.pallas_call(
        spread_kernel,
        out_shape=jax.ShapeDtypeStruct(pieces.shape, BF16),
        compiler_params=pltpu.CompilerParams(vmem_limit_bytes=32 * 1024 * 1024),
        cost_estimate=pl.CostEstimate(flops=pieces.size, bytes_accessed=pieces.size * 4, transcendentals=0),
        name="spread",
    )(pieces)


def weights_kernel(place_ref, mine_ref, other_ref, pw_out, ow_out, bias_out, gain_out):
    i, k = pl.program_id(0), pl.program_id(1)
    own = place_ref[1] == i

    def write(ref):
        values = ref[...].astype(F32) * (1.0 / 32.0)
        for p in range(4):
            pw_out[:, p, :] = values[:, p * WIDTH : (p + 1) * WIDTH]
        ow_out[...] = values[:, 4 * WIDTH : 5 * WIDTH].T
        for p in range(5 * WIDTH // 128):
            block, at = divmod(32 * p, values.shape[0])

            @pl.when((i == 0) & (k == block))
            def _():
                lanes = slice(p % 2 * 128, p % 2 * 128 + 128)
                small = values[at : at + 1, 5 * WIDTH :]
                if p < 8:
                    bias_out[p // 2 : p // 2 + 1, lanes] = small
                else:
                    gain_out[:, lanes] = small

    @pl.when(own)
    def _():
        write(mine_ref)

    @pl.when(jnp.logical_not(own))
    def _():
        write(other_ref)


def weights_out(place, mine, other):
    half = MODEL // 2
    block = 128
    per = half // block
    return pl.pallas_call(
        weights_kernel,
        out_shape=[
            jax.ShapeDtypeStruct((MODEL, 4, WIDTH), F32),
            jax.ShapeDtypeStruct((WIDTH, MODEL), F32),
            jax.ShapeDtypeStruct((4, WIDTH), F32),
            jax.ShapeDtypeStruct((1, WIDTH), F32),
        ],
        grid_spec=pltpu.PrefetchScalarGridSpec(
            num_scalar_prefetch=1,
            grid=(2, per),
            in_specs=[
                pl.BlockSpec((block, COLUMNS), lambda i, k, c: (k, 0)),
                pl.BlockSpec((block, COLUMNS), lambda i, k, c: (k, 0)),
            ],
            out_specs=[
                pl.BlockSpec((block, 4, WIDTH), lambda i, k, c: (i * per + k, 0, 0)),
                pl.BlockSpec((WIDTH, block), lambda i, k, c: (0, i * per + k)),
                pl.BlockSpec((4, WIDTH), lambda i, k, c: (0, 0)),
                pl.BlockSpec((1, WIDTH), lambda i, k, c: (0, 0)),
            ],
        ),
        compiler_params=pltpu.CompilerParams(
            dimension_semantics=("arbitrary", "arbitrary"), vmem_limit_bytes=40 * 1024 * 1024
        ),
        cost_estimate=pl.CostEstimate(flops=4000000, bytes_accessed=8500000, transcendentals=0),
        name="weights_out",
    )(place, mine, other)


def ring(step):
    return [(i, (i + step) % 4) for i in range(4)]


def body(events, upstream, proj_weight, proj_bias, norm_gain, out_weight, lengths, owners):
    rows = events.shape[0]
    place = jnp.stack([lax.axis_index(DP), lax.axis_index("c"), lax.axis_index("mp")]).astype(jnp.int32)
    gain = norm_gain.reshape(1, WIDTH)
    grads, sent, kept, weight_in = layer(lengths, place, events, upstream, proj_weight, out_weight, proj_bias, gain)

    swap = [(0, 1), (1, 0)]
    half = MODEL // 2
    kept = kept + lax.ppermute(sent, "c", swap).astype(F32)
    pieces = lax.all_to_all(kept.astype(BF16).reshape(16, half // 16, COLUMNS), ("z", "y"), 0, 0, tiled=True)
    pieces = lax.all_to_all(spread(pieces), ("z", "y"), 0, 0, tiled=True).reshape(half, COLUMNS)
    other = lax.ppermute(pieces, "c", swap)
    proj_grad, out_grad, bias_grad, gain_grad = weights_out(place, pieces, other)

    event_grads = None
    count = rows // ROW_PARTS
    for n in range(ROW_PARTS):
        own, ahead, across, behind = partial_rows(place, grads, weight_in, n * count, count)
        shares = (
            own,
            lax.ppermute(ahead, "mp", ring(1)),
            lax.ppermute(across, "mp", ring(2)),
            lax.ppermute(behind, "mp", ring(3)),
        )
        event_grads = event_rows(lengths, place, shares, upstream, n * count, event_grads)
    return event_grads, proj_grad, bias_grad, gain_grad.reshape(WIDTH), out_grad


def solution(mesh):
    grid = Mesh(mesh.devices.reshape(4, 4, 2, 4), ("z", "y", "c", "mp"))
    placed = (
        P(DP, None),
        P(DP, None),
        P(None, None, "mp"),
        P(None, "mp"),
        P("mp"),
        P("mp", None),
        P(),
        P(),
    )
    return jax.shard_map(
        body,
        mesh=grid,
        in_specs=placed,
        out_specs=(P(DP, "mp"), P(None, None, "mp"), P(None, "mp"), P("mp"), P("mp", None)),
        check_vma=False,
    )
```

```python
import functools

import jax
import jax.numpy as jnp
from jax import lax
from jax.experimental import pallas as pl
from jax.experimental.pallas import tpu as pltpu
from jax.sharding import Mesh, PartitionSpec as P

HEADS = 8
TILE = 64
EPSILON = 1e-05
STEP = 512
PAIR = 128
HEAD = 128
WIDTH = 256
SPAN = 512
MODEL = 1024
COLUMNS = 5 * WIDTH + 128
PIECES = 8
ROW_PARTS = 2
HISTORY = 3
F32 = jnp.float32
BF16 = jnp.bfloat16
NT = (((1,), (1,)), ((), ()))
TN = (((0,), (0,)), ((), ()))
DP = ("z", "y", "c")


def dot(a, b, dims=(((1,), (0,)), ((), ()))):
    return lax.dot_general(a, b, dims, preferred_element_type=F32)


def sigmoid(v):
    return 0.5 * jnp.tanh(0.5 * v) + 0.5


def tile_column(values, rows):
    ids = lax.broadcasted_iota(jnp.int32, (rows, 1), 0)
    column = jnp.full((rows, 1), values[0], jnp.int32)
    for i in range(1, len(values)):
        column = jnp.where(ids >= i * TILE, values[i], column)
    return column


def layer_kernel(
    steps, lengths_ref, place_ref, x_ref, g_ref, xp_ref, wp_ref, wo_ref, b_ref, gain_ref,
    pg_out, sent_out, mine_out, w_ref,
    first_ref, ones_ref, kv, dkv, sl, pgq, gq, slgq, hg, hid, pgs, acc, sums, attn_s, dsl_s, mix_s, dm_s,
):
    j = pl.program_id(0)
    cur = pl.ds(STEP, STEP)
    old = pl.ds(0, STEP)
    pairs = STEP // PAIR
    chains = [(i, h) for i in range(pairs) for h in range(2)]

    @pl.when(j == 0)
    def _():
        kv[old] = jnp.zeros((STEP, SPAN), BF16)
        dkv[old] = jnp.zeros((STEP, SPAN), F32)
        sl[old] = jnp.zeros((STEP, SPAN), F32)
        pgq[...] = jnp.zeros((STEP, SPAN), BF16)
        pgs[...] = jnp.zeros(pgs.shape, BF16)
        acc[...] = jnp.zeros(acc.shape, F32)
        sums[...] = jnp.zeros(sums.shape, F32)
        for p in range(4):
            w_ref[:, p * WIDTH : (p + 1) * WIDTH] = wp_ref[:, p, :]
        head_row = lax.broadcasted_iota(jnp.int32, (WIDTH, WIDTH), 0) >= HEAD
        head_col = lax.broadcasted_iota(jnp.int32, (WIDTH, WIDTH), 1) >= HEAD
        ones_ref[...] = jnp.where(head_row == head_col, 1.0 / HEAD, 0.0).astype(BF16)
        home = place_ref[0]
        tiles = steps * (STEP // TILE)

        @pl.loop(0, tiles)
        def _(t):
            first_ref[t] = -1

        def place(u, begin):
            count = lengths_ref[home, u]
            for t in range(HISTORY):

                @pl.when(t < count)
                def _():
                    first_ref[begin + t] = begin

            return begin + count

        lax.fori_loop(0, lengths_ref.shape[1], place, jnp.int32(0))

    def in_grad_piece(n):
        depth = MODEL // PIECES
        r = slice(n * depth, (n + 1) * depth)
        acc[r, 0 : 4 * WIDTH] += dot(xp_ref[:, r], pgs[...], TN)

    def finish():
        pg_out[:, 0:WIDTH] = pgq[:, 0:WIDTH]
        pg_out[:, WIDTH : 2 * WIDTH] = (dkv[old, 0:WIDTH] * sl[old, 0:WIDTH]).astype(BF16)
        pg_out[:, 2 * WIDTH : 3 * WIDTH] = pgq[:, WIDTH:]
        pg_out[:, 3 * WIDTH :] = (dkv[old, WIDTH:] * sl[old, WIDTH:]).astype(BF16)
        grads = pg_out[...]
        pgs[...] = grads
        sums[:, 0 : 4 * WIDTH] += jnp.sum(grads.astype(F32).reshape(STEP // 8, 8, 4 * WIDTH), axis=0)

    def rows_of(i):
        return slice(i * PAIR, (i + 1) * PAIR)

    def window(i):
        return pl.ds(STEP - PAIR + i * PAIR, 2 * PAIR)

    def first_cols(h):
        return slice(h * HEAD, (h + 1) * HEAD)

    def second_cols(h):
        return slice(WIDTH + h * HEAD, WIDTH + (h + 1) * HEAD)

    def query():
        t0 = j * (STEP // TILE)
        firsts = [first_ref[t0 + i] for i in range(STEP // TILE)]
        base = j * STEP
        starts = [jnp.where(f >= 0, f * TILE - base, STEP) for f in firsts]
        x = x_ref[...]
        used = tile_column(firsts, STEP) >= 0
        g = jnp.where(used, g_ref[...], jnp.zeros((), BF16))
        hg[...] = dot(g, wo_ref[...], NT)
        for part in range(4):
            cols = slice(part * WIDTH, (part + 1) * WIDTH)
            pre = dot(x, w_ref[:, cols]) + b_ref[part : part + 1, :]
            sig = sigmoid(pre)
            act = pre * sig
            slope = sig + act * (1.0 - sig)
            half = slice(0, WIDTH) if part < 2 else slice(WIDTH, SPAN)
            if part % 2 == 0:
                gq[:, half] = act.astype(BF16)
                slgq[:, half] = slope
            else:
                kv[cur, half] = act.astype(BF16)
                sl[cur, half] = slope
        scale = HEAD**-0.5
        row = lax.broadcasted_iota(jnp.int32, (PAIR, 2 * PAIR), 0)
        col = lax.broadcasted_iota(jnp.int32, (PAIR, 2 * PAIR), 1) - PAIR
        visible = []
        for i in range(pairs):
            begin = tile_column(starts[2 * i : 2 * i + 2], PAIR) - i * PAIR
            visible.append((col >= begin) & (col <= row))
        for n, (i, h) in enumerate(chains):
            s = dot(gq[rows_of(i), second_cols(h)], kv[window(i), second_cols(h)], NT) * scale
            sig = jnp.where(visible[i], sigmoid(s), 0.0)
            a = s * sig
            attn = a.astype(BF16)
            attn_s[i, h] = attn
            dsl_s[i, h] = (sig + a * (1.0 - sig)) * scale
            mix_s[rows_of(i), first_cols(h)] = dot(attn, kv[window(i), first_cols(h)])
            for t in range(n * PIECES // len(chains), (n + 1) * PIECES // len(chains)):
                in_grad_piece(t)
        ones = ones_ref[...]
        mix = mix_s[...]
        high = mix.astype(BF16)
        low = (mix - high.astype(F32)).astype(BF16)
        centered = mix - (dot(high, ones) + dot(low, ones))
        inverse = lax.rsqrt(dot((centered * centered).astype(BF16), ones) + EPSILON)
        normed = centered * inverse
        gate = gq[:, 0:WIDTH].astype(F32)
        gain = gain_ref[...]
        local = hg[...]
        scaled = normed * gain
        hid[...] = (scaled * gate).astype(BF16)
        gq[:, 0:WIDTH] = (local * scaled * slgq[:, 0:WIDTH]).astype(BF16)
        lg = local * gate
        gn = lg * normed
        sums[:, 4 * WIDTH :] += jnp.sum(gn.reshape(STEP // 8, 8, WIDTH), axis=0)
        ng = lg * gain
        mean_one = dot(ng.astype(BF16), ones)
        mean_two = dot((gn * gain).astype(BF16), ones)
        dm_s[...] = ((ng - mean_one - normed * mean_two) * inverse).astype(BF16)
        for i, h in chains:
            hc, kc = first_cols(h), second_cols(h)
            dm = dm_s[rows_of(i), hc]
            q = gq[rows_of(i), kc]
            da = dot(dm, kv[window(i), hc], NT)
            sg = (da * dsl_s[i, h]).astype(BF16)
            dq = dot(sg, kv[window(i), kc])
            dv = dot(attn_s[i, h], dm, TN)
            dk = dot(sg, q, TN)
            before = pl.ds(STEP - PAIR + i * PAIR, PAIR)
            here = pl.ds(STEP + i * PAIR, PAIR)
            dkv[before, hc] += dv[:PAIR]
            dkv[here, hc] = dv[PAIR:]
            dkv[before, kc] += dk[:PAIR]
            dkv[here, kc] = dk[PAIR:]
            gq[rows_of(i), kc] = (dq * slgq[rows_of(i), kc]).astype(BF16)
        acc[:, 4 * WIDTH : 5 * WIDTH] += dot(g, hid[...], TN)

    @pl.when(j < steps)
    def _():
        query()
        finish()
        kv[old] = kv[cur]
        dkv[old] = dkv[cur]
        sl[old] = sl[cur]
        pgq[...] = gq[...]

    @pl.when(j == steps)
    def _():
        for n in range(PIECES):
            in_grad_piece(n)
        finish()

    @pl.when(j == steps + 1)
    def _():
        for n in range(PIECES):
            in_grad_piece(n)
        total = jnp.sum(sums[...], axis=0, keepdims=True)
        for p in range(5 * WIDTH // 128):
            acc[pl.ds(32 * p, 8), 5 * WIDTH :] = jnp.broadcast_to(total[:, p * 128 : (p + 1) * 128], (8, 128))
        core = place_ref[1]
        half = MODEL // 2
        mine_out[...] = acc[pl.ds(pl.multiple_of(core * half, half), half), :]
        sent_out[...] = acc[pl.ds(pl.multiple_of((1 - core) * half, half), half), :].astype(BF16)


def layer(lengths, place, x, g, w, wo, bias, gain):
    rows = x.shape[0]
    steps = rows // STEP
    half = MODEL // 2

    def in_block(j, *_):
        return (jnp.minimum(j, steps - 1), 0)

    def out_block(j, *_):
        return (jnp.clip(j - 1, 0, steps - 1), 0)

    def late_block(j, *_):
        return (jnp.maximum(j - 2, 0), 0)

    def whole(j, *_):
        return (0, 0)

    macs = rows * (MODEL * MODEL * 2 + 2 * WIDTH * MODEL + 6 * WIDTH * WIDTH)
    return pl.pallas_call(
        functools.partial(layer_kernel, steps),
        out_shape=[
            jax.ShapeDtypeStruct((rows, MODEL), BF16),
            jax.ShapeDtypeStruct((half, COLUMNS), BF16),
            jax.ShapeDtypeStruct((half, COLUMNS), F32),
            jax.ShapeDtypeStruct((MODEL, 4 * WIDTH), BF16),
        ],
        grid_spec=pltpu.PrefetchScalarGridSpec(
            num_scalar_prefetch=2,
            grid=(steps + 2,),
            in_specs=[
                pl.BlockSpec((STEP, MODEL), in_block),
                pl.BlockSpec((STEP, MODEL), in_block),
                pl.BlockSpec((STEP, MODEL), late_block),
                pl.BlockSpec(w.shape, lambda j, *_: (0, 0, 0)),
                pl.BlockSpec(wo.shape, whole),
                pl.BlockSpec(bias.shape, whole),
                pl.BlockSpec(gain.shape, whole),
            ],
            out_specs=[
                pl.BlockSpec((STEP, MODEL), out_block),
                pl.BlockSpec((half, COLUMNS), whole),
                pl.BlockSpec((half, COLUMNS), whole),
                pl.BlockSpec((MODEL, 4 * WIDTH), whole),
            ],
            scratch_shapes=[
                pltpu.SMEM((steps * (STEP // TILE),), jnp.int32),
                pltpu.VMEM((WIDTH, WIDTH), BF16),
                pltpu.VMEM((2 * STEP, SPAN), BF16),
                pltpu.VMEM((2 * STEP, SPAN), F32),
                pltpu.VMEM((2 * STEP, SPAN), F32),
                pltpu.VMEM((STEP, SPAN), BF16),
                pltpu.VMEM((STEP, SPAN), BF16),
                pltpu.VMEM((STEP, SPAN), F32),
                pltpu.VMEM((STEP, WIDTH), F32),
                pltpu.VMEM((STEP, WIDTH), BF16),
                pltpu.VMEM((STEP, MODEL), BF16),
                pltpu.VMEM((MODEL, COLUMNS), F32),
                pltpu.VMEM((8, 5 * WIDTH), F32),
                pltpu.VMEM((STEP // PAIR, 2, PAIR, 2 * PAIR), BF16),
                pltpu.VMEM((STEP // PAIR, 2, PAIR, 2 * PAIR), F32),
                pltpu.VMEM((STEP, WIDTH), F32),
                pltpu.VMEM((STEP, WIDTH), BF16),
            ],
        ),
        compiler_params=pltpu.CompilerParams(
            dimension_semantics=("arbitrary",), vmem_limit_bytes=56 * 1024 * 1024
        ),
        cost_estimate=pl.CostEstimate(flops=2 * macs, bytes_accessed=rows * 8000, transcendentals=rows * 2048),
        name="layer",
    )(lengths, place, x, g, x, w, wo, bias, gain)


def partial_kernel(place_ref, pg_ref, w_ref, own_out, s1f_out, s1b_out, r2f_out, r2b_out):
    grads = pg_ref[...]
    me = place_ref[2]

    def share(shift):
        start = pl.multiple_of(lax.rem(me + shift, 4) * WIDTH, WIDTH)
        return dot(grads, w_ref[pl.ds(start, WIDTH), :], NT)

    across = share(2).astype(BF16)
    s1f_out[:, :HEAD] = across[:, :HEAD]
    s1b_out[:, HEAD:] = across[:, HEAD:]
    ahead = share(1).astype(BF16)
    r2f_out[...] = ahead[:, :HEAD]
    s1f_out[:, HEAD:] = ahead[:, HEAD:]
    behind = share(3).astype(BF16)
    s1b_out[:, :HEAD] = behind[:, :HEAD]
    r2b_out[...] = behind[:, HEAD:]
    own_out[...] = share(0)


def partial_rows(place, grads, w, begin, count):
    block = 512
    wide = pl.BlockSpec((block, WIDTH), lambda i, p: (i, 0))
    slim = pl.BlockSpec((block, HEAD), lambda i, p: (i, 0))
    return pl.pallas_call(
        partial_kernel,
        out_shape=[jax.ShapeDtypeStruct((count, WIDTH), F32)]
        + [jax.ShapeDtypeStruct((count, WIDTH), BF16)] * 2
        + [jax.ShapeDtypeStruct((count, HEAD), BF16)] * 2,
        grid_spec=pltpu.PrefetchScalarGridSpec(
            num_scalar_prefetch=1,
            grid=(count // block,),
            in_specs=[
                pl.BlockSpec((block, MODEL), lambda i, p: (begin // block + i, 0)),
                pl.BlockSpec(w.shape, lambda i, p: (0, 0)),
            ],
            out_specs=[wide, wide, wide, slim, slim],
        ),
        compiler_params=pltpu.CompilerParams(
            dimension_semantics=("arbitrary",), vmem_limit_bytes=56 * 1024 * 1024
        ),
        cost_estimate=pl.CostEstimate(
            flops=2 * count * MODEL * MODEL, bytes_accessed=count * 4096 + w.size * 2, transcendentals=0
        ),
        name="partial_rows",
    )(place, grads, w)


def event_kernel(begin, block, lengths_ref, place_ref, own_ref, t1f_ref, t1b_ref, t2f_ref, t2b_ref, g_ref, *refs):
    out_ref = refs[-1]
    home = place_ref[0]
    tiles = lax.fori_loop(0, lengths_ref.shape[1], lambda u, t: t + lengths_ref[home, u], jnp.int32(0))
    row = lax.broadcasted_iota(jnp.int32, (block, WIDTH), 0) + begin + pl.program_id(0) * block
    base = own_ref[...] + jnp.where(row < tiles * TILE, g_ref[...].astype(F32), 0.0)
    left = t1b_ref[:, :HEAD].astype(F32) + t2f_ref[...].astype(F32)
    right = t1f_ref[:, HEAD:].astype(F32) + t2b_ref[...].astype(F32)
    out_ref[:, :HEAD] = (base[:, :HEAD] + left).astype(BF16)
    out_ref[:, HEAD:] = (base[:, HEAD:] + right).astype(BF16)


def event_rows(lengths, place, shares, g, begin, out):
    block = 512
    count = shares[0].shape[0]
    wide = pl.BlockSpec((block, WIDTH), lambda i, f, p: (i, 0))
    slim = pl.BlockSpec((block, HEAD), lambda i, f, p: (i, 0))
    in_specs = [wide, wide, wide, slim, slim]
    in_specs.append(pl.BlockSpec((block, WIDTH), lambda i, f, p: (begin // block + i, p[2])))
    operands = list(shares) + [g]
    aliases = {}
    if out is not None:
        in_specs.append(pl.BlockSpec(memory_space=pl.ANY))
        operands.append(out)
        aliases = {8: 0}
    return pl.pallas_call(
        functools.partial(event_kernel, begin, block),
        out_shape=jax.ShapeDtypeStruct((g.shape[0], WIDTH), BF16),
        grid_spec=pltpu.PrefetchScalarGridSpec(
            num_scalar_prefetch=2,
            grid=(count // block,),
            in_specs=in_specs,
            out_specs=pl.BlockSpec((block, WIDTH), lambda i, f, p: (begin // block + i, 0)),
        ),
        input_output_aliases=aliases,
        compiler_params=pltpu.CompilerParams(
            dimension_semantics=("arbitrary",), vmem_limit_bytes=56 * 1024 * 1024
        ),
        cost_estimate=pl.CostEstimate(flops=count * 2048, bytes_accessed=count * 3072, transcendentals=0),
        name="event_rows",
    )(lengths, place, *operands)


def relay_kernel(r2f_ref, r2b_ref, t1f_ref, t1b_ref, f_out, b_out):
    f_out[...] = (r2f_ref[...].astype(F32) + t1f_ref[...].astype(F32)).astype(BF16)
    b_out[...] = (r2b_ref[...].astype(F32) + t1b_ref[...].astype(F32)).astype(BF16)


def relay(r2f, r2b, t1f, t1b):
    block = 512
    rows = r2f.shape[0]
    slim = pl.BlockSpec((block, HEAD), lambda i: (i, 0))
    return pl.pallas_call(
        relay_kernel,
        out_shape=[jax.ShapeDtypeStruct((rows, HEAD), BF16)] * 2,
        grid=(rows // block,),
        in_specs=[slim, slim, slim, pl.BlockSpec((block, HEAD), lambda i: (i, 1))],
        out_specs=[slim, slim],
        compiler_params=pltpu.CompilerParams(
            dimension_semantics=("arbitrary",), vmem_limit_bytes=56 * 1024 * 1024
        ),
        cost_estimate=pl.CostEstimate(flops=rows * 512, bytes_accessed=rows * 1536, transcendentals=0),
        name="relay",
    )(r2f, r2b, t1f, t1b)


def spread_kernel(got_ref, out_ref):
    total = jnp.sum(got_ref[...].astype(F32), axis=0).astype(BF16)
    out_ref[...] = jnp.broadcast_to(total[None], out_ref.shape)


def spread(pieces):
    return pl.pallas_call(
        spread_kernel,
        out_shape=jax.ShapeDtypeStruct(pieces.shape, BF16),
        compiler_params=pltpu.CompilerParams(vmem_limit_bytes=32 * 1024 * 1024),
        cost_estimate=pl.CostEstimate(flops=pieces.size, bytes_accessed=pieces.size * 4, transcendentals=0),
        name="spread",
    )(pieces)


def weights_kernel(place_ref, mine_ref, other_ref, pw_out, ow_out, bias_out, gain_out):
    i, k = pl.program_id(0), pl.program_id(1)
    own = place_ref[1] == i

    def write(ref):
        values = ref[...].astype(F32) * (1.0 / 32.0)
        for p in range(4):
            pw_out[:, p, :] = values[:, p * WIDTH : (p + 1) * WIDTH]
        ow_out[...] = values[:, 4 * WIDTH : 5 * WIDTH].T
        for p in range(5 * WIDTH // 128):
            block, at = divmod(32 * p, values.shape[0])

            @pl.when((i == 0) & (k == block))
            def _():
                lanes = slice(p % 2 * 128, p % 2 * 128 + 128)
                small = values[at : at + 1, 5 * WIDTH :]
                if p < 8:
                    bias_out[p // 2 : p // 2 + 1, lanes] = small
                else:
                    gain_out[:, lanes] = small

    @pl.when(own)
    def _():
        write(mine_ref)

    @pl.when(jnp.logical_not(own))
    def _():
        write(other_ref)


def weights_out(place, mine, other):
    half = MODEL // 2
    block = 128
    per = half // block
    return pl.pallas_call(
        weights_kernel,
        out_shape=[
            jax.ShapeDtypeStruct((MODEL, 4, WIDTH), F32),
            jax.ShapeDtypeStruct((WIDTH, MODEL), F32),
            jax.ShapeDtypeStruct((4, WIDTH), F32),
            jax.ShapeDtypeStruct((1, WIDTH), F32),
        ],
        grid_spec=pltpu.PrefetchScalarGridSpec(
            num_scalar_prefetch=1,
            grid=(2, per),
            in_specs=[
                pl.BlockSpec((block, COLUMNS), lambda i, k, c: (k, 0)),
                pl.BlockSpec((block, COLUMNS), lambda i, k, c: (k, 0)),
            ],
            out_specs=[
                pl.BlockSpec((block, 4, WIDTH), lambda i, k, c: (i * per + k, 0, 0)),
                pl.BlockSpec((WIDTH, block), lambda i, k, c: (0, i * per + k)),
                pl.BlockSpec((4, WIDTH), lambda i, k, c: (0, 0)),
                pl.BlockSpec((1, WIDTH), lambda i, k, c: (0, 0)),
            ],
        ),
        compiler_params=pltpu.CompilerParams(
            dimension_semantics=("arbitrary", "arbitrary"), vmem_limit_bytes=40 * 1024 * 1024
        ),
        cost_estimate=pl.CostEstimate(flops=4000000, bytes_accessed=8500000, transcendentals=0),
        name="weights_out",
    )(place, mine, other)


def ring(step):
    return [(i, (i + step) % 4) for i in range(4)]


def body(events, upstream, proj_weight, proj_bias, norm_gain, out_weight, lengths, owners):
    rows = events.shape[0]
    place = jnp.stack([lax.axis_index(DP), lax.axis_index("c"), lax.axis_index("mp")]).astype(jnp.int32)
    gain = norm_gain.reshape(1, WIDTH)
    grads, sent, kept, weight_in = layer(lengths, place, events, upstream, proj_weight, out_weight, proj_bias, gain)

    swap = [(0, 1), (1, 0)]
    half = MODEL // 2
    other = lax.ppermute(sent, "c", swap)
    parts = []
    count = rows // ROW_PARTS
    own, s1f, s1b, r2f, r2b = partial_rows(place, grads, weight_in, 0, count)
    parts.append([own, r2f, r2b, lax.ppermute(s1f, "mp", ring(1)), lax.ppermute(s1b, "mp", ring(3))])
    kept = (kept + other.astype(F32)).astype(BF16)
    grads, weight_in, kept = lax.optimization_barrier((grads, weight_in, kept))
    pieces = lax.all_to_all(kept.reshape(16, half // 16, COLUMNS), ("z", "y"), 0, 0, tiled=True)
    own, s1f, s1b, r2f, r2b = partial_rows(place, grads, weight_in, count, count)
    parts.append([own, r2f, r2b, lax.ppermute(s1f, "mp", ring(1)), lax.ppermute(s1b, "mp", ring(3))])
    pieces = spread(pieces)
    second_step = [relay(*p[1:]) for p in parts]
    second_step, pieces = lax.optimization_barrier((second_step, pieces))
    shares = []
    for (own, _, _, t1f, t1b), (r2f, r2b) in zip(parts, second_step):
        shares.append((own, t1f, t1b, lax.ppermute(r2f, "mp", ring(1)), lax.ppermute(r2b, "mp", ring(3))))
    pieces = lax.all_to_all(pieces, ("z", "y"), 0, 0, tiled=True).reshape(half, COLUMNS)
    other = lax.ppermute(pieces, "c", swap)
    proj_grad, out_grad, bias_grad, gain_grad = weights_out(place, pieces, other)
    event_grads = None
    for n in range(ROW_PARTS):
        event_grads = event_rows(lengths, place, shares[n], upstream, n * count, event_grads)
    return event_grads, proj_grad, bias_grad, gain_grad.reshape(WIDTH), out_grad


def solution(mesh):
    grid = Mesh(mesh.devices.reshape(4, 4, 2, 4), ("z", "y", "c", "mp"))
    placed = (
        P(DP, None),
        P(DP, None),
        P(None, None, "mp"),
        P(None, "mp"),
        P("mp"),
        P("mp", None),
        P(),
        P(),
    )
    return jax.shard_map(
        body,
        mesh=grid,
        in_specs=placed,
        out_specs=(P(DP, "mp"), P(None, None, "mp"), P(None, "mp"), P("mp"), P("mp", None)),
        check_vma=False,
    )
```

```python
import functools

import jax
import jax.numpy as jnp
from jax import lax
from jax.experimental import pallas as pl
from jax.experimental.pallas import tpu as pltpu
from jax.sharding import Mesh, PartitionSpec as P

HEADS = 8
TILE = 64
EPSILON = 1e-05
STEP = 512
PAIR = 128
HEAD = 128
WIDTH = 256
SPAN = 512
MODEL = 1024
COLUMNS = 5 * WIDTH + 128
PIECES = 8
HISTORY = 3
F32 = jnp.float32
BF16 = jnp.bfloat16
NT = (((1,), (1,)), ((), ()))
TN = (((0,), (0,)), ((), ()))
DP = ("z", "y", "c")


def dot(a, b, dims=(((1,), (0,)), ((), ()))):
    return lax.dot_general(a, b, dims, preferred_element_type=F32)


def sigmoid(v):
    return 0.5 * jnp.tanh(0.5 * v) + 0.5


def tile_column(values, rows):
    ids = lax.broadcasted_iota(jnp.int32, (rows, 1), 0)
    column = jnp.full((rows, 1), values[0], jnp.int32)
    for i in range(1, len(values)):
        column = jnp.where(ids >= i * TILE, values[i], column)
    return column


def layer_kernel(
    steps, lengths_ref, place_ref, x_ref, g_ref, xp_ref, wp_ref, wo_ref, b_ref, gain_ref,
    pg_out, sent_out, mine_out, w_ref,
    first_ref, ones_ref, kv, dkv, sl, pgq, gq, slgq, hg, hid, pgs, acc, sums, attn_s, dsl_s, mix_s, dm_s,
):
    j = pl.program_id(0)
    cur = pl.ds(STEP, STEP)
    old = pl.ds(0, STEP)
    pairs = STEP // PAIR
    chains = [(i, h) for i in range(pairs) for h in range(2)]

    @pl.when(j == 0)
    def _():
        kv[old] = jnp.zeros((STEP, SPAN), BF16)
        dkv[old] = jnp.zeros((STEP, SPAN), F32)
        sl[old] = jnp.zeros((STEP, SPAN), F32)
        pgq[...] = jnp.zeros((STEP, SPAN), BF16)
        pgs[...] = jnp.zeros(pgs.shape, BF16)
        acc[...] = jnp.zeros(acc.shape, F32)
        sums[...] = jnp.zeros(sums.shape, F32)
        for p in range(4):
            w_ref[:, p * WIDTH : (p + 1) * WIDTH] = wp_ref[:, p, :]
        head_row = lax.broadcasted_iota(jnp.int32, (WIDTH, WIDTH), 0) >= HEAD
        head_col = lax.broadcasted_iota(jnp.int32, (WIDTH, WIDTH), 1) >= HEAD
        ones_ref[...] = jnp.where(head_row == head_col, 1.0 / HEAD, 0.0).astype(BF16)
        home = place_ref[0]
        tiles = steps * (STEP // TILE)

        @pl.loop(0, tiles)
        def _(t):
            first_ref[t] = -1

        def place(u, begin):
            count = lengths_ref[home, u]
            for t in range(HISTORY):

                @pl.when(t < count)
                def _():
                    first_ref[begin + t] = begin

            return begin + count

        lax.fori_loop(0, lengths_ref.shape[1], place, jnp.int32(0))

    def in_grad_piece(n):
        depth = MODEL // PIECES
        r = slice(n * depth, (n + 1) * depth)
        acc[r, 0 : 4 * WIDTH] += dot(xp_ref[:, r], pgs[...], TN)

    def finish():
        pg_out[:, 0:WIDTH] = pgq[:, 0:WIDTH]
        pg_out[:, WIDTH : 2 * WIDTH] = (dkv[old, 0:WIDTH] * sl[old, 0:WIDTH]).astype(BF16)
        pg_out[:, 2 * WIDTH : 3 * WIDTH] = pgq[:, WIDTH:]
        pg_out[:, 3 * WIDTH :] = (dkv[old, WIDTH:] * sl[old, WIDTH:]).astype(BF16)
        grads = pg_out[...]
        pgs[...] = grads
        sums[:, 0 : 4 * WIDTH] += jnp.sum(grads.astype(F32).reshape(STEP // 8, 8, 4 * WIDTH), axis=0)

    def rows_of(i):
        return slice(i * PAIR, (i + 1) * PAIR)

    def window(i):
        return pl.ds(STEP - PAIR + i * PAIR, 2 * PAIR)

    def first_cols(h):
        return slice(h * HEAD, (h + 1) * HEAD)

    def second_cols(h):
        return slice(WIDTH + h * HEAD, WIDTH + (h + 1) * HEAD)

    def query():
        t0 = j * (STEP // TILE)
        firsts = [first_ref[t0 + i] for i in range(STEP // TILE)]
        base = j * STEP
        starts = [jnp.where(f >= 0, f * TILE - base, STEP) for f in firsts]
        x = x_ref[...]
        used = tile_column(firsts, STEP) >= 0
        g = jnp.where(used, g_ref[...], jnp.zeros((), BF16))
        hg[...] = dot(g, wo_ref[...], NT)
        for part in range(4):
            cols = slice(part * WIDTH, (part + 1) * WIDTH)
            pre = dot(x, w_ref[:, cols]) + b_ref[part : part + 1, :]
            sig = sigmoid(pre)
            act = pre * sig
            slope = sig + act * (1.0 - sig)
            half = slice(0, WIDTH) if part < 2 else slice(WIDTH, SPAN)
            if part % 2 == 0:
                gq[:, half] = act.astype(BF16)
                slgq[:, half] = slope
            else:
                kv[cur, half] = act.astype(BF16)
                sl[cur, half] = slope
        scale = HEAD**-0.5
        row = lax.broadcasted_iota(jnp.int32, (PAIR, 2 * PAIR), 0)
        col = lax.broadcasted_iota(jnp.int32, (PAIR, 2 * PAIR), 1) - PAIR
        visible = []
        for i in range(pairs):
            begin = tile_column(starts[2 * i : 2 * i + 2], PAIR) - i * PAIR
            visible.append((col >= begin) & (col <= row))
        for n, (i, h) in enumerate(chains):
            s = dot(gq[rows_of(i), second_cols(h)], kv[window(i), second_cols(h)], NT) * scale
            sig = jnp.where(visible[i], sigmoid(s), 0.0)
            a = s * sig
            attn = a.astype(BF16)
            attn_s[i, h] = attn
            dsl_s[i, h] = (sig + a * (1.0 - sig)) * scale
            mix_s[rows_of(i), first_cols(h)] = dot(attn, kv[window(i), first_cols(h)])
            for t in range(n * PIECES // len(chains), (n + 1) * PIECES // len(chains)):
                in_grad_piece(t)
        ones = ones_ref[...]
        mix = mix_s[...]
        high = mix.astype(BF16)
        low = (mix - high.astype(F32)).astype(BF16)
        centered = mix - (dot(high, ones) + dot(low, ones))
        inverse = lax.rsqrt(dot((centered * centered).astype(BF16), ones) + EPSILON)
        normed = centered * inverse
        gate = gq[:, 0:WIDTH].astype(F32)
        gain = gain_ref[...]
        local = hg[...]
        scaled = normed * gain
        hid[...] = (scaled * gate).astype(BF16)
        gq[:, 0:WIDTH] = (local * scaled * slgq[:, 0:WIDTH]).astype(BF16)
        lg = local * gate
        gn = lg * normed
        sums[:, 4 * WIDTH :] += jnp.sum(gn.reshape(STEP // 8, 8, WIDTH), axis=0)
        ng = lg * gain
        mean_one = dot(ng.astype(BF16), ones)
        mean_two = dot((gn * gain).astype(BF16), ones)
        dm_s[...] = ((ng - mean_one - normed * mean_two) * inverse).astype(BF16)
        for i, h in chains:
            hc, kc = first_cols(h), second_cols(h)
            dm = dm_s[rows_of(i), hc]
            q = gq[rows_of(i), kc]
            da = dot(dm, kv[window(i), hc], NT)
            sg = (da * dsl_s[i, h]).astype(BF16)
            dq = dot(sg, kv[window(i), kc])
            dv = dot(attn_s[i, h], dm, TN)
            dk = dot(sg, q, TN)
            before = pl.ds(STEP - PAIR + i * PAIR, PAIR)
            here = pl.ds(STEP + i * PAIR, PAIR)
            dkv[before, hc] += dv[:PAIR]
            dkv[here, hc] = dv[PAIR:]
            dkv[before, kc] += dk[:PAIR]
            dkv[here, kc] = dk[PAIR:]
            gq[rows_of(i), kc] = (dq * slgq[rows_of(i), kc]).astype(BF16)
        acc[:, 4 * WIDTH : 5 * WIDTH] += dot(g, hid[...], TN)

    @pl.when(j < steps)
    def _():
        query()
        finish()
        kv[old] = kv[cur]
        dkv[old] = dkv[cur]
        sl[old] = sl[cur]
        pgq[...] = gq[...]

    @pl.when(j == steps)
    def _():
        for n in range(PIECES):
            in_grad_piece(n)
        finish()

    @pl.when(j == steps + 1)
    def _():
        for n in range(PIECES):
            in_grad_piece(n)
        total = jnp.sum(sums[...], axis=0, keepdims=True)
        for p in range(5 * WIDTH // 128):
            acc[pl.ds(32 * p, 8), 5 * WIDTH :] = jnp.broadcast_to(total[:, p * 128 : (p + 1) * 128], (8, 128))
        core = place_ref[1]
        half = MODEL // 2
        mine_out[...] = acc[pl.ds(pl.multiple_of(core * half, half), half), :]
        sent_out[...] = acc[pl.ds(pl.multiple_of((1 - core) * half, half), half), :].astype(BF16)


def layer(lengths, place, x, g, w, wo, bias, gain):
    rows = x.shape[0]
    steps = rows // STEP
    half = MODEL // 2

    def in_block(j, *_):
        return (jnp.minimum(j, steps - 1), 0)

    def out_block(j, *_):
        return (jnp.clip(j - 1, 0, steps - 1), 0)

    def late_block(j, *_):
        return (jnp.maximum(j - 2, 0), 0)

    def whole(j, *_):
        return (0, 0)

    macs = rows * (MODEL * MODEL * 2 + 2 * WIDTH * MODEL + 6 * WIDTH * WIDTH)
    return pl.pallas_call(
        functools.partial(layer_kernel, steps),
        out_shape=[
            jax.ShapeDtypeStruct((rows, MODEL), BF16),
            jax.ShapeDtypeStruct((half, COLUMNS), BF16),
            jax.ShapeDtypeStruct((half, COLUMNS), F32),
            jax.ShapeDtypeStruct((MODEL, 4 * WIDTH), BF16),
        ],
        grid_spec=pltpu.PrefetchScalarGridSpec(
            num_scalar_prefetch=2,
            grid=(steps + 2,),
            in_specs=[
                pl.BlockSpec((STEP, MODEL), in_block),
                pl.BlockSpec((STEP, MODEL), in_block),
                pl.BlockSpec((STEP, MODEL), late_block),
                pl.BlockSpec(w.shape, lambda j, *_: (0, 0, 0)),
                pl.BlockSpec(wo.shape, whole),
                pl.BlockSpec(bias.shape, whole),
                pl.BlockSpec(gain.shape, whole),
            ],
            out_specs=[
                pl.BlockSpec((STEP, MODEL), out_block),
                pl.BlockSpec((half, COLUMNS), whole),
                pl.BlockSpec((half, COLUMNS), whole),
                pl.BlockSpec((MODEL, 4 * WIDTH), whole),
            ],
            scratch_shapes=[
                pltpu.SMEM((steps * (STEP // TILE),), jnp.int32),
                pltpu.VMEM((WIDTH, WIDTH), BF16),
                pltpu.VMEM((2 * STEP, SPAN), BF16),
                pltpu.VMEM((2 * STEP, SPAN), F32),
                pltpu.VMEM((2 * STEP, SPAN), F32),
                pltpu.VMEM((STEP, SPAN), BF16),
                pltpu.VMEM((STEP, SPAN), BF16),
                pltpu.VMEM((STEP, SPAN), F32),
                pltpu.VMEM((STEP, WIDTH), F32),
                pltpu.VMEM((STEP, WIDTH), BF16),
                pltpu.VMEM((STEP, MODEL), BF16),
                pltpu.VMEM((MODEL, COLUMNS), F32),
                pltpu.VMEM((8, 5 * WIDTH), F32),
                pltpu.VMEM((STEP // PAIR, 2, PAIR, 2 * PAIR), BF16),
                pltpu.VMEM((STEP // PAIR, 2, PAIR, 2 * PAIR), F32),
                pltpu.VMEM((STEP, WIDTH), F32),
                pltpu.VMEM((STEP, WIDTH), BF16),
            ],
        ),
        compiler_params=pltpu.CompilerParams(
            dimension_semantics=("arbitrary",), vmem_limit_bytes=56 * 1024 * 1024
        ),
        cost_estimate=pl.CostEstimate(flops=2 * macs, bytes_accessed=rows * 8000, transcendentals=rows * 2048),
        name="layer",
    )(lengths, place, x, g, x, w, wo, bias, gain)


def partial_kernel(place_ref, pg_ref, w_ref, own_out, ahead_out, across_out, behind_out):
    grads = pg_ref[...]
    me = place_ref[2]

    def share(shift):
        start = pl.multiple_of(lax.rem(me + shift, 4) * WIDTH, WIDTH)
        return dot(grads, w_ref[pl.ds(start, WIDTH), :], NT)

    ahead_out[...] = share(1).astype(BF16)
    across_out[...] = share(2).astype(BF16)
    behind_out[...] = share(3).astype(BF16)
    own_out[...] = share(0)


def partial_rows(place, grads, w):
    block = 512
    rows = grads.shape[0]
    wide = pl.BlockSpec((block, WIDTH), lambda i, p: (i, 0))
    return pl.pallas_call(
        partial_kernel,
        out_shape=[jax.ShapeDtypeStruct((rows, WIDTH), F32)] + [jax.ShapeDtypeStruct((rows, WIDTH), BF16)] * 3,
        grid_spec=pltpu.PrefetchScalarGridSpec(
            num_scalar_prefetch=1,
            grid=(rows // block,),
            in_specs=[
                pl.BlockSpec((block, MODEL), lambda i, p: (i, 0)),
                pl.BlockSpec(w.shape, lambda i, p: (0, 0)),
            ],
            out_specs=[wide, wide, wide, wide],
        ),
        compiler_params=pltpu.CompilerParams(
            dimension_semantics=("arbitrary",), vmem_limit_bytes=56 * 1024 * 1024
        ),
        cost_estimate=pl.CostEstimate(
            flops=2 * rows * MODEL * MODEL, bytes_accessed=rows * 4608 + w.size * 2, transcendentals=0
        ),
        name="partial_rows",
    )(place, grads, w)


def event_kernel(block, lengths_ref, place_ref, own_ref, a_ref, b_ref, c_ref, g_ref, out_ref):
    home = place_ref[0]
    tiles = lax.fori_loop(0, lengths_ref.shape[1], lambda u, t: t + lengths_ref[home, u], jnp.int32(0))
    row = lax.broadcasted_iota(jnp.int32, (block, WIDTH), 0) + pl.program_id(0) * block
    base = own_ref[...] + jnp.where(row < tiles * TILE, g_ref[...].astype(F32), 0.0)
    got = a_ref[...].astype(F32) + b_ref[...].astype(F32) + c_ref[...].astype(F32)
    out_ref[...] = (base + got).astype(BF16)


def event_rows(lengths, place, shares, g):
    block = 512
    rows = g.shape[0]
    wide = pl.BlockSpec((block, WIDTH), lambda i, f, p: (i, 0))
    return pl.pallas_call(
        functools.partial(event_kernel, block),
        out_shape=jax.ShapeDtypeStruct((rows, WIDTH), BF16),
        grid_spec=pltpu.PrefetchScalarGridSpec(
            num_scalar_prefetch=2,
            grid=(rows // block,),
            in_specs=[wide, wide, wide, wide, pl.BlockSpec((block, WIDTH), lambda i, f, p: (i, p[2]))],
            out_specs=wide,
        ),
        compiler_params=pltpu.CompilerParams(
            dimension_semantics=("arbitrary",), vmem_limit_bytes=56 * 1024 * 1024
        ),
        cost_estimate=pl.CostEstimate(flops=rows * 2048, bytes_accessed=rows * 3584, transcendentals=0),
        name="event_rows",
    )(lengths, place, *shares, g)


def spread_kernel(got_ref, out_ref):
    total = jnp.sum(got_ref[...].astype(F32), axis=0).astype(BF16)
    out_ref[...] = jnp.broadcast_to(total[None], out_ref.shape)


def spread(pieces):
    return pl.pallas_call(
        spread_kernel,
        out_shape=jax.ShapeDtypeStruct(pieces.shape, BF16),
        compiler_params=pltpu.CompilerParams(vmem_limit_bytes=32 * 1024 * 1024),
        cost_estimate=pl.CostEstimate(flops=pieces.size, bytes_accessed=pieces.size * 4, transcendentals=0),
        name="spread",
    )(pieces)


def weights_kernel(place_ref, mine_ref, other_ref, pw_out, ow_out, bias_out, gain_out):
    i, k = pl.program_id(0), pl.program_id(1)
    own = place_ref[1] == i

    def write(ref):
        values = ref[...].astype(F32) * (1.0 / 32.0)
        for p in range(4):
            pw_out[:, p, :] = values[:, p * WIDTH : (p + 1) * WIDTH]
        ow_out[...] = values[:, 4 * WIDTH : 5 * WIDTH].T
        for p in range(5 * WIDTH // 128):
            block, at = divmod(32 * p, values.shape[0])

            @pl.when((i == 0) & (k == block))
            def _():
                lanes = slice(p % 2 * 128, p % 2 * 128 + 128)
                small = values[at : at + 1, 5 * WIDTH :]
                if p < 8:
                    bias_out[p // 2 : p // 2 + 1, lanes] = small
                else:
                    gain_out[:, lanes] = small

    @pl.when(own)
    def _():
        write(mine_ref)

    @pl.when(jnp.logical_not(own))
    def _():
        write(other_ref)


def weights_out(place, mine, other):
    half = MODEL // 2
    block = 128
    per = half // block
    return pl.pallas_call(
        weights_kernel,
        out_shape=[
            jax.ShapeDtypeStruct((MODEL, 4, WIDTH), F32),
            jax.ShapeDtypeStruct((WIDTH, MODEL), F32),
            jax.ShapeDtypeStruct((4, WIDTH), F32),
            jax.ShapeDtypeStruct((1, WIDTH), F32),
        ],
        grid_spec=pltpu.PrefetchScalarGridSpec(
            num_scalar_prefetch=1,
            grid=(2, per),
            in_specs=[
                pl.BlockSpec((block, COLUMNS), lambda i, k, c: (k, 0)),
                pl.BlockSpec((block, COLUMNS), lambda i, k, c: (k, 0)),
            ],
            out_specs=[
                pl.BlockSpec((block, 4, WIDTH), lambda i, k, c: (i * per + k, 0, 0)),
                pl.BlockSpec((WIDTH, block), lambda i, k, c: (0, i * per + k)),
                pl.BlockSpec((4, WIDTH), lambda i, k, c: (0, 0)),
                pl.BlockSpec((1, WIDTH), lambda i, k, c: (0, 0)),
            ],
        ),
        compiler_params=pltpu.CompilerParams(
            dimension_semantics=("arbitrary", "arbitrary"), vmem_limit_bytes=40 * 1024 * 1024
        ),
        cost_estimate=pl.CostEstimate(flops=4000000, bytes_accessed=8500000, transcendentals=0),
        name="weights_out",
    )(place, mine, other)


def ring(step):
    return [(i, (i + step) % 4) for i in range(4)]


def body(events, upstream, proj_weight, proj_bias, norm_gain, out_weight, lengths, owners):
    rows = events.shape[0]
    place = jnp.stack([lax.axis_index(DP), lax.axis_index("c"), lax.axis_index("mp")]).astype(jnp.int32)
    gain = norm_gain.reshape(1, WIDTH)
    grads, sent, kept, weight_in = layer(lengths, place, events, upstream, proj_weight, out_weight, proj_bias, gain)

    swap = [(0, 1), (1, 0)]
    half = MODEL // 2
    other = lax.ppermute(sent, "c", swap)
    shares = partial_rows(place, grads, weight_in)
    kept = (kept + other.astype(F32)).astype(BF16)
    shares, kept = lax.optimization_barrier((shares, kept))
    shares = [shares[0]] + [lax.ppermute(shares[step], "mp", ring(step)) for step in (1, 2, 3)]
    pieces = lax.all_to_all(kept.reshape(16, half // 16, COLUMNS), ("z", "y"), 0, 0, tiled=True)
    pieces = lax.all_to_all(spread(pieces), ("z", "y"), 0, 0, tiled=True).reshape(half, COLUMNS)
    other = lax.ppermute(pieces, "c", swap)
    proj_grad, out_grad, bias_grad, gain_grad = weights_out(place, pieces, other)
    event_grads = event_rows(lengths, place, shares, upstream)
    return event_grads, proj_grad, bias_grad, gain_grad.reshape(WIDTH), out_grad


def solution(mesh):
    grid = Mesh(mesh.devices.reshape(4, 4, 2, 4), ("z", "y", "c", "mp"))
    placed = (
        P(DP, None),
        P(DP, None),
        P(None, None, "mp"),
        P(None, "mp"),
        P("mp"),
        P("mp", None),
        P(),
        P(),
    )
    return jax.shard_map(
        body,
        mesh=grid,
        in_specs=placed,
        out_specs=(P(DP, "mp"), P(None, None, "mp"), P(None, "mp"), P("mp"), P("mp", None)),
        check_vma=False,
    )
```

```python
import functools

import jax
import jax.numpy as jnp
from jax import lax
from jax.experimental import pallas as pl
from jax.experimental.pallas import tpu as pltpu
from jax.sharding import Mesh, PartitionSpec as P

HEADS = 8
TILE = 64
EPSILON = 1e-05
STEP = 512
PAIR = 128
HEAD = 128
WIDTH = 256
SPAN = 512
MODEL = 1024
COLUMNS = 5 * WIDTH + 128
PIECES = 8
HISTORY = 3
ROW_PARTS = (1280, 1024, 768)
F32 = jnp.float32
BF16 = jnp.bfloat16
NT = (((1,), (1,)), ((), ()))
TN = (((0,), (0,)), ((), ()))
DP = ("z", "y", "c")


def dot(a, b, dims=(((1,), (0,)), ((), ()))):
    return lax.dot_general(a, b, dims, preferred_element_type=F32)


def sigmoid(v):
    return 0.5 * jnp.tanh(0.5 * v) + 0.5


def tile_column(values, rows):
    ids = lax.broadcasted_iota(jnp.int32, (rows, 1), 0)
    column = jnp.full((rows, 1), values[0], jnp.int32)
    for i in range(1, len(values)):
        column = jnp.where(ids >= i * TILE, values[i], column)
    return column


def layer_kernel(
    steps, lengths_ref, place_ref, x_ref, g_ref, xp_ref, wp_ref, wo_ref, b_ref, gain_ref,
    pg_out, sent_out, mine_out, w_ref,
    first_ref, ones_ref, kv, dkv, sl, pgq, gq, slgq, hg, hid, pgs, acc, sums, attn_s, dsl_s, mix_s, dm_s,
):
    j = pl.program_id(0)
    cur = pl.ds(STEP, STEP)
    old = pl.ds(0, STEP)
    pairs = STEP // PAIR
    chains = [(i, h) for i in range(pairs) for h in range(2)]

    @pl.when(j == 0)
    def _():
        kv[old] = jnp.zeros((STEP, SPAN), BF16)
        dkv[old] = jnp.zeros((STEP, SPAN), F32)
        sl[old] = jnp.zeros((STEP, SPAN), F32)
        pgq[...] = jnp.zeros((STEP, SPAN), BF16)
        pgs[...] = jnp.zeros(pgs.shape, BF16)
        acc[...] = jnp.zeros(acc.shape, F32)
        sums[...] = jnp.zeros(sums.shape, F32)
        for p in range(4):
            w_ref[:, p * WIDTH : (p + 1) * WIDTH] = wp_ref[:, p, :]
        head_row = lax.broadcasted_iota(jnp.int32, (WIDTH, WIDTH), 0) >= HEAD
        head_col = lax.broadcasted_iota(jnp.int32, (WIDTH, WIDTH), 1) >= HEAD
        ones_ref[...] = jnp.where(head_row == head_col, 1.0 / HEAD, 0.0).astype(BF16)
        home = place_ref[0]
        tiles = steps * (STEP // TILE)

        @pl.loop(0, tiles)
        def _(t):
            first_ref[t] = -1

        def place(u, begin):
            count = lengths_ref[home, u]
            for t in range(HISTORY):

                @pl.when(t < count)
                def _():
                    first_ref[begin + t] = begin

            return begin + count

        lax.fori_loop(0, lengths_ref.shape[1], place, jnp.int32(0))

    def in_grad_piece(n):
        depth = MODEL // PIECES
        r = slice(n * depth, (n + 1) * depth)
        acc[r, 0 : 4 * WIDTH] += dot(xp_ref[:, r], pgs[...], TN)

    def finish():
        pg_out[:, 0:WIDTH] = pgq[:, 0:WIDTH]
        pg_out[:, WIDTH : 2 * WIDTH] = (dkv[old, 0:WIDTH] * sl[old, 0:WIDTH]).astype(BF16)
        pg_out[:, 2 * WIDTH : 3 * WIDTH] = pgq[:, WIDTH:]
        pg_out[:, 3 * WIDTH :] = (dkv[old, WIDTH:] * sl[old, WIDTH:]).astype(BF16)
        grads = pg_out[...]
        pgs[...] = grads
        sums[:, 0 : 4 * WIDTH] += jnp.sum(grads.astype(F32).reshape(STEP // 8, 8, 4 * WIDTH), axis=0)

    def rows_of(i):
        return slice(i * PAIR, (i + 1) * PAIR)

    def window(i):
        return pl.ds(STEP - PAIR + i * PAIR, 2 * PAIR)

    def first_cols(h):
        return slice(h * HEAD, (h + 1) * HEAD)

    def second_cols(h):
        return slice(WIDTH + h * HEAD, WIDTH + (h + 1) * HEAD)

    def query():
        t0 = j * (STEP // TILE)
        firsts = [first_ref[t0 + i] for i in range(STEP // TILE)]
        base = j * STEP
        starts = [jnp.where(f >= 0, f * TILE - base, STEP) for f in firsts]
        x = x_ref[...]
        used = tile_column(firsts, STEP) >= 0
        g = jnp.where(used, g_ref[...], jnp.zeros((), BF16))
        hg[...] = dot(g, wo_ref[...], NT)
        for part in range(4):
            cols = slice(part * WIDTH, (part + 1) * WIDTH)
            pre = dot(x, w_ref[:, cols]) + b_ref[part : part + 1, :]
            sig = sigmoid(pre)
            act = pre * sig
            slope = sig + act * (1.0 - sig)
            half = slice(0, WIDTH) if part < 2 else slice(WIDTH, SPAN)
            if part % 2 == 0:
                gq[:, half] = act.astype(BF16)
                slgq[:, half] = slope
            else:
                kv[cur, half] = act.astype(BF16)
                sl[cur, half] = slope
        scale = HEAD**-0.5
        row = lax.broadcasted_iota(jnp.int32, (PAIR, 2 * PAIR), 0)
        col = lax.broadcasted_iota(jnp.int32, (PAIR, 2 * PAIR), 1) - PAIR
        visible = []
        for i in range(pairs):
            begin = tile_column(starts[2 * i : 2 * i + 2], PAIR) - i * PAIR
            visible.append((col >= begin) & (col <= row))
        for n, (i, h) in enumerate(chains):
            s = dot(gq[rows_of(i), second_cols(h)], kv[window(i), second_cols(h)], NT) * scale
            sig = jnp.where(visible[i], sigmoid(s), 0.0)
            a = s * sig
            attn = a.astype(BF16)
            attn_s[i, h] = attn
            dsl_s[i, h] = (sig + a * (1.0 - sig)) * scale
            mix_s[rows_of(i), first_cols(h)] = dot(attn, kv[window(i), first_cols(h)])
            for t in range(n * PIECES // len(chains), (n + 1) * PIECES // len(chains)):
                in_grad_piece(t)
        ones = ones_ref[...]
        mix = mix_s[...]
        high = mix.astype(BF16)
        low = (mix - high.astype(F32)).astype(BF16)
        centered = mix - (dot(high, ones) + dot(low, ones))
        inverse = lax.rsqrt(dot((centered * centered).astype(BF16), ones) + EPSILON)
        normed = centered * inverse
        gate = gq[:, 0:WIDTH].astype(F32)
        gain = gain_ref[...]
        local = hg[...]
        scaled = normed * gain
        hid[...] = (scaled * gate).astype(BF16)
        gq[:, 0:WIDTH] = (local * scaled * slgq[:, 0:WIDTH]).astype(BF16)
        lg = local * gate
        gn = lg * normed
        sums[:, 4 * WIDTH :] += jnp.sum(gn.reshape(STEP // 8, 8, WIDTH), axis=0)
        ng = lg * gain
        mean_one = dot(ng.astype(BF16), ones)
        mean_two = dot((gn * gain).astype(BF16), ones)
        dm_s[...] = ((ng - mean_one - normed * mean_two) * inverse).astype(BF16)
        for i, h in chains:
            hc, kc = first_cols(h), second_cols(h)
            dm = dm_s[rows_of(i), hc]
            q = gq[rows_of(i), kc]
            da = dot(dm, kv[window(i), hc], NT)
            sg = (da * dsl_s[i, h]).astype(BF16)
            dq = dot(sg, kv[window(i), kc])
            dv = dot(attn_s[i, h], dm, TN)
            dk = dot(sg, q, TN)
            before = pl.ds(STEP - PAIR + i * PAIR, PAIR)
            here = pl.ds(STEP + i * PAIR, PAIR)
            dkv[before, hc] += dv[:PAIR]
            dkv[here, hc] = dv[PAIR:]
            dkv[before, kc] += dk[:PAIR]
            dkv[here, kc] = dk[PAIR:]
            gq[rows_of(i), kc] = (dq * slgq[rows_of(i), kc]).astype(BF16)
        acc[:, 4 * WIDTH : 5 * WIDTH] += dot(g, hid[...], TN)

    @pl.when(j < steps)
    def _():
        query()
        finish()
        kv[old] = kv[cur]
        dkv[old] = dkv[cur]
        sl[old] = sl[cur]
        pgq[...] = gq[...]

    @pl.when(j == steps)
    def _():
        for n in range(PIECES):
            in_grad_piece(n)
        finish()

    @pl.when(j == steps + 1)
    def _():
        for n in range(PIECES):
            in_grad_piece(n)
        total = jnp.sum(sums[...], axis=0, keepdims=True)
        for p in range(5 * WIDTH // 128):
            acc[pl.ds(32 * p, 8), 5 * WIDTH :] = jnp.broadcast_to(total[:, p * 128 : (p + 1) * 128], (8, 128))
        core = place_ref[1]
        half = MODEL // 2
        mine_out[...] = acc[pl.ds(pl.multiple_of(core * half, half), half), :]
        sent_out[...] = acc[pl.ds(pl.multiple_of((1 - core) * half, half), half), :].astype(BF16)


def layer(lengths, place, x, g, w, wo, bias, gain):
    rows = x.shape[0]
    steps = rows // STEP
    half = MODEL // 2

    def in_block(j, *_):
        return (jnp.minimum(j, steps - 1), 0)

    def out_block(j, *_):
        return (jnp.clip(j - 1, 0, steps - 1), 0)

    def late_block(j, *_):
        return (jnp.maximum(j - 2, 0), 0)

    def whole(j, *_):
        return (0, 0)

    macs = rows * (MODEL * MODEL * 2 + 2 * WIDTH * MODEL + 6 * WIDTH * WIDTH)
    return pl.pallas_call(
        functools.partial(layer_kernel, steps),
        out_shape=[
            jax.ShapeDtypeStruct((rows, MODEL), BF16),
            jax.ShapeDtypeStruct((half, COLUMNS), BF16),
            jax.ShapeDtypeStruct((half, COLUMNS), F32),
            jax.ShapeDtypeStruct((MODEL, 4 * WIDTH), BF16),
        ],
        grid_spec=pltpu.PrefetchScalarGridSpec(
            num_scalar_prefetch=2,
            grid=(steps + 2,),
            in_specs=[
                pl.BlockSpec((STEP, MODEL), in_block),
                pl.BlockSpec((STEP, MODEL), in_block),
                pl.BlockSpec((STEP, MODEL), late_block),
                pl.BlockSpec(w.shape, lambda j, *_: (0, 0, 0)),
                pl.BlockSpec(wo.shape, whole),
                pl.BlockSpec(bias.shape, whole),
                pl.BlockSpec(gain.shape, whole),
            ],
            out_specs=[
                pl.BlockSpec((STEP, MODEL), out_block),
                pl.BlockSpec((half, COLUMNS), whole),
                pl.BlockSpec((half, COLUMNS), whole),
                pl.BlockSpec((MODEL, 4 * WIDTH), whole),
            ],
            scratch_shapes=[
                pltpu.SMEM((steps * (STEP // TILE),), jnp.int32),
                pltpu.VMEM((WIDTH, WIDTH), BF16),
                pltpu.VMEM((2 * STEP, SPAN), BF16),
                pltpu.VMEM((2 * STEP, SPAN), F32),
                pltpu.VMEM((2 * STEP, SPAN), F32),
                pltpu.VMEM((STEP, SPAN), BF16),
                pltpu.VMEM((STEP, SPAN), BF16),
                pltpu.VMEM((STEP, SPAN), F32),
                pltpu.VMEM((STEP, WIDTH), F32),
                pltpu.VMEM((STEP, WIDTH), BF16),
                pltpu.VMEM((STEP, MODEL), BF16),
                pltpu.VMEM((MODEL, COLUMNS), F32),
                pltpu.VMEM((8, 5 * WIDTH), F32),
                pltpu.VMEM((STEP // PAIR, 2, PAIR, 2 * PAIR), BF16),
                pltpu.VMEM((STEP // PAIR, 2, PAIR, 2 * PAIR), F32),
                pltpu.VMEM((STEP, WIDTH), F32),
                pltpu.VMEM((STEP, WIDTH), BF16),
            ],
        ),
        compiler_params=pltpu.CompilerParams(
            dimension_semantics=("arbitrary",), vmem_limit_bytes=56 * 1024 * 1024
        ),
        cost_estimate=pl.CostEstimate(flops=2 * macs, bytes_accessed=rows * 8000, transcendentals=rows * 2048),
        name="layer",
    )(lengths, place, x, g, x, w, wo, bias, gain)


def partial_kernel(place_ref, pg_ref, w_ref, own_out, ahead_out, across_out, behind_out):
    grads = pg_ref[...]
    me = place_ref[2]

    def share(shift):
        start = pl.multiple_of(lax.rem(me + shift, 4) * WIDTH, WIDTH)
        return dot(grads, w_ref[pl.ds(start, WIDTH), :], NT)

    ahead_out[...] = share(1).astype(BF16)
    across_out[...] = share(2).astype(BF16)
    behind_out[...] = share(3).astype(BF16)
    own_out[...] = share(0)


def partial_rows(place, grads, w, begin, rows):
    block = 256
    wide = pl.BlockSpec((block, WIDTH), lambda i, p: (i, 0))
    return pl.pallas_call(
        partial_kernel,
        out_shape=[jax.ShapeDtypeStruct((rows, WIDTH), F32)] + [jax.ShapeDtypeStruct((rows, WIDTH), BF16)] * 3,
        grid_spec=pltpu.PrefetchScalarGridSpec(
            num_scalar_prefetch=1,
            grid=(rows // block,),
            in_specs=[
                pl.BlockSpec((block, MODEL), lambda i, p: (begin // block + i, 0)),
                pl.BlockSpec(w.shape, lambda i, p: (0, 0)),
            ],
            out_specs=[wide, wide, wide, wide],
        ),
        compiler_params=pltpu.CompilerParams(
            dimension_semantics=("arbitrary",), vmem_limit_bytes=56 * 1024 * 1024
        ),
        cost_estimate=pl.CostEstimate(
            flops=2 * rows * MODEL * MODEL, bytes_accessed=rows * 4608 + w.size * 2, transcendentals=0
        ),
        name="partial_rows",
    )(place, grads, w)


def event_kernel(begin, block, lengths_ref, place_ref, own_ref, a_ref, b_ref, c_ref, g_ref, *refs):
    out_ref, tiles_ref = refs[-2:]
    home = place_ref[0]

    @pl.when(pl.program_id(0) == 0)
    def _():
        tiles_ref[0] = lax.fori_loop(0, lengths_ref.shape[1], lambda u, t: t + lengths_ref[home, u], jnp.int32(0))

    row = lax.broadcasted_iota(jnp.int32, (block, WIDTH), 0) + begin + pl.program_id(0) * block
    base = own_ref[...] + jnp.where(row < tiles_ref[0] * TILE, g_ref[...].astype(F32), 0.0)
    got = a_ref[...].astype(F32) + b_ref[...].astype(F32) + c_ref[...].astype(F32)
    out_ref[...] = (base + got).astype(BF16)


def event_rows(lengths, place, shares, g, begin, out):
    block = 256
    rows = shares[0].shape[0]
    wide = pl.BlockSpec((block, WIDTH), lambda i, f, p: (i, 0))
    in_specs = [wide, wide, wide, wide]
    in_specs.append(pl.BlockSpec((block, WIDTH), lambda i, f, p: (begin // block + i, p[2])))
    operands = list(shares) + [g]
    aliases = {}
    if out is not None:
        in_specs.append(pl.BlockSpec(memory_space=pl.ANY))
        operands.append(out)
        aliases = {7: 0}
    return pl.pallas_call(
        functools.partial(event_kernel, begin, block),
        out_shape=jax.ShapeDtypeStruct((g.shape[0], WIDTH), BF16),
        grid_spec=pltpu.PrefetchScalarGridSpec(
            num_scalar_prefetch=2,
            grid=(rows // block,),
            in_specs=in_specs,
            out_specs=pl.BlockSpec((block, WIDTH), lambda i, f, p: (begin // block + i, 0)),
            scratch_shapes=[pltpu.SMEM((1,), jnp.int32)],
        ),
        input_output_aliases=aliases,
        compiler_params=pltpu.CompilerParams(
            dimension_semantics=("arbitrary",), vmem_limit_bytes=56 * 1024 * 1024
        ),
        cost_estimate=pl.CostEstimate(flops=rows * 2048, bytes_accessed=rows * 3584, transcendentals=0),
        name="event_rows",
    )(lengths, place, *operands)


def spread_kernel(got_ref, out_ref):
    total = jnp.sum(got_ref[...].astype(F32), axis=0).astype(BF16)
    out_ref[...] = jnp.broadcast_to(total[None], out_ref.shape)


def spread(pieces):
    return pl.pallas_call(
        spread_kernel,
        out_shape=jax.ShapeDtypeStruct(pieces.shape, BF16),
        compiler_params=pltpu.CompilerParams(vmem_limit_bytes=32 * 1024 * 1024),
        cost_estimate=pl.CostEstimate(flops=pieces.size, bytes_accessed=pieces.size * 4, transcendentals=0),
        name="spread",
    )(pieces)


def weights_kernel(other, place_ref, got_ref, *refs):
    pw_out, ow_out, bias_out, gain_out = refs[-4:]
    k = pl.program_id(0)
    core = place_ref[1]
    first_half = (1 - core if other else core) == 0
    values = got_ref[...].astype(F32) * (1.0 / 32.0)
    for p in range(4):
        pw_out[:, p, :] = values[:, p * WIDTH : (p + 1) * WIDTH]
    ow_out[...] = values[:, 4 * WIDTH : 5 * WIDTH].T
    if other:

        @pl.when(k == 0)
        def _():
            bias_out[...] = refs[2][...]
            gain_out[...] = refs[3][...]

    for p in range(5 * WIDTH // 128):
        block, at = divmod(32 * p, values.shape[0])

        @pl.when(first_half & (k == block))
        def _():
            lanes = slice(p % 2 * 128, p % 2 * 128 + 128)
            small = values[at : at + 1, 5 * WIDTH :]
            if p < 8:
                bias_out[p // 2 : p // 2 + 1, lanes] = small
            else:
                gain_out[:, lanes] = small


def weights_out(place, got, earlier):
    other = earlier is not None
    block = 128
    per = got.shape[0] // block

    def half(p):
        return (1 - p[1] if other else p[1]) * per

    small_specs = [
        pl.BlockSpec((4, WIDTH), lambda k, p: (0, 0)),
        pl.BlockSpec((1, WIDTH), lambda k, p: (0, 0)),
    ]
    in_specs = [pl.BlockSpec((block, COLUMNS), lambda k, p: (k, 0))]
    operands = [got]
    aliases = {}
    if other:
        in_specs += [pl.BlockSpec(memory_space=pl.ANY)] * 2 + small_specs
        operands += list(earlier)
        aliases = {2: 0, 3: 1}
    return pl.pallas_call(
        functools.partial(weights_kernel, other),
        out_shape=[
            jax.ShapeDtypeStruct((MODEL, 4, WIDTH), F32),
            jax.ShapeDtypeStruct((WIDTH, MODEL), F32),
            jax.ShapeDtypeStruct((4, WIDTH), F32),
            jax.ShapeDtypeStruct((1, WIDTH), F32),
        ],
        grid_spec=pltpu.PrefetchScalarGridSpec(
            num_scalar_prefetch=1,
            grid=(per,),
            in_specs=in_specs,
            out_specs=[
                pl.BlockSpec((block, 4, WIDTH), lambda k, p: (half(p) + k, 0, 0)),
                pl.BlockSpec((WIDTH, block), lambda k, p: (0, half(p) + k)),
            ]
            + small_specs,
        ),
        input_output_aliases=aliases,
        compiler_params=pltpu.CompilerParams(
            dimension_semantics=("arbitrary",), vmem_limit_bytes=40 * 1024 * 1024
        ),
        cost_estimate=pl.CostEstimate(flops=2000000, bytes_accessed=4200000, transcendentals=0),
        name="weights_out",
    )(place, *operands)


def ring(step):
    return [(i, (i + step) % 4) for i in range(4)]


def body(events, upstream, proj_weight, proj_bias, norm_gain, out_weight, lengths, owners):
    rows = events.shape[0]
    place = jnp.stack([lax.axis_index(DP), lax.axis_index("c"), lax.axis_index("mp")]).astype(jnp.int32)
    gain = norm_gain.reshape(1, WIDTH)
    grads, sent, kept, weight_in = layer(lengths, place, events, upstream, proj_weight, out_weight, proj_bias, gain)

    swap = [(0, 1), (1, 0)]
    half = MODEL // 2
    other = lax.ppermute(sent, "c", swap)
    begins = [sum(ROW_PARTS[:n]) for n in range(len(ROW_PARTS))]
    one, two, three = (partial_rows(place, grads, weight_in, b, n) for b, n in zip(begins, ROW_PARTS))

    def send(shares):
        return [shares[0]] + [lax.ppermute(shares[step], "mp", ring(step)) for step in (1, 2, 3)]

    kept = (kept + other.astype(F32)).astype(BF16)
    one, two, three, kept = lax.optimization_barrier((one, two, three, kept))
    one = send(one)
    pieces = lax.all_to_all(kept.reshape(16, half // 16, COLUMNS), ("z", "y"), 0, 0, tiled=True)
    one, two, three, pieces = lax.optimization_barrier((one, two, three, spread(pieces)))
    two = send(two)
    pieces = lax.all_to_all(pieces, ("z", "y"), 0, 0, tiled=True).reshape(half, COLUMNS)
    two, three, pieces = lax.optimization_barrier((two, three, pieces))
    three = send(three)
    event_grads = event_rows(lengths, place, one, upstream, begins[0], None)
    other = lax.ppermute(pieces, "c", swap)
    weights = weights_out(place, pieces, None)
    event_grads = event_rows(lengths, place, two, upstream, begins[1], event_grads)
    proj_grad, out_grad, bias_grad, gain_grad = weights_out(place, other, weights)
    event_grads = event_rows(lengths, place, three, upstream, begins[2], event_grads)
    return event_grads, proj_grad, bias_grad, gain_grad.reshape(WIDTH), out_grad


def solution(mesh):
    grid = Mesh(mesh.devices.reshape(4, 4, 2, 4), ("z", "y", "c", "mp"))
    placed = (
        P(DP, None),
        P(DP, None),
        P(None, None, "mp"),
        P(None, "mp"),
        P("mp"),
        P("mp", None),
        P(),
        P(),
    )
    return jax.shard_map(
        body,
        mesh=grid,
        in_specs=placed,
        out_specs=(P(DP, "mp"), P(None, None, "mp"), P(None, "mp"), P("mp"), P("mp", None)),
        check_vma=False,
    )
```

```python
import functools

import jax
import jax.numpy as jnp
from jax import lax
from jax.experimental import pallas as pl
from jax.experimental.pallas import tpu as pltpu
from jax.sharding import Mesh, PartitionSpec as P

HEADS = 8
TILE = 64
EPSILON = 1e-05
STEP = 512
PAIR = 128
HEAD = 128
WIDTH = 256
SPAN = 512
MODEL = 1024
COLUMNS = 5 * WIDTH + 128
PIECES = 8
HISTORY = 3
F32 = jnp.float32
BF16 = jnp.bfloat16
NT = (((1,), (1,)), ((), ()))
TN = (((0,), (0,)), ((), ()))
DP = ("z", "y", "c")


def dot(a, b, dims=(((1,), (0,)), ((), ()))):
    return lax.dot_general(a, b, dims, preferred_element_type=F32)


def sigmoid(v):
    return 0.5 * jnp.tanh(0.5 * v) + 0.5


def tile_column(values, rows):
    ids = lax.broadcasted_iota(jnp.int32, (rows, 1), 0)
    column = jnp.full((rows, 1), values[0], jnp.int32)
    for i in range(1, len(values)):
        column = jnp.where(ids >= i * TILE, values[i], column)
    return column


def layer_kernel(
    steps, lengths_ref, place_ref, x_ref, g_ref, xp_ref, wp_ref, wo_ref, b_ref, gain_ref,
    pg_out, sent_out, mine_out, w_ref,
    first_ref, ones_ref, kv, dkv, sl, pgq, gq, slgq, hg, hid, pgs, acc, sums, attn_s, dsl_s, mix_s, dm_s,
):
    j = pl.program_id(0)
    cur = pl.ds(STEP, STEP)
    old = pl.ds(0, STEP)
    pairs = STEP // PAIR
    chains = [(i, h) for i in range(pairs) for h in range(2)]

    @pl.when(j == 0)
    def _():
        kv[old] = jnp.zeros((STEP, SPAN), BF16)
        dkv[old] = jnp.zeros((STEP, SPAN), F32)
        sl[old] = jnp.zeros((STEP, SPAN), F32)
        pgq[...] = jnp.zeros((STEP, SPAN), BF16)
        pgs[...] = jnp.zeros(pgs.shape, BF16)
        acc[...] = jnp.zeros(acc.shape, F32)
        sums[...] = jnp.zeros(sums.shape, F32)
        for p in range(4):
            w_ref[:, p * WIDTH : (p + 1) * WIDTH] = wp_ref[:, p, :]
        head_row = lax.broadcasted_iota(jnp.int32, (WIDTH, WIDTH), 0) >= HEAD
        head_col = lax.broadcasted_iota(jnp.int32, (WIDTH, WIDTH), 1) >= HEAD
        ones_ref[...] = jnp.where(head_row == head_col, 1.0 / HEAD, 0.0).astype(BF16)
        home = place_ref[0]
        tiles = steps * (STEP // TILE)

        @pl.loop(0, tiles)
        def _(t):
            first_ref[t] = -1

        def place(u, begin):
            count = lengths_ref[home, u]
            for t in range(HISTORY):

                @pl.when(t < count)
                def _():
                    first_ref[begin + t] = begin

            return begin + count

        lax.fori_loop(0, lengths_ref.shape[1], place, jnp.int32(0))

    def in_grad_piece(n):
        depth = MODEL // PIECES
        r = slice(n * depth, (n + 1) * depth)
        acc[r, 0 : 4 * WIDTH] += dot(xp_ref[:, r], pgs[...], TN)

    def finish():
        pg_out[:, 0:WIDTH] = pgq[:, 0:WIDTH]
        pg_out[:, WIDTH : 2 * WIDTH] = (dkv[old, 0:WIDTH] * sl[old, 0:WIDTH]).astype(BF16)
        pg_out[:, 2 * WIDTH : 3 * WIDTH] = pgq[:, WIDTH:]
        pg_out[:, 3 * WIDTH :] = (dkv[old, WIDTH:] * sl[old, WIDTH:]).astype(BF16)
        grads = pg_out[...]
        pgs[...] = grads
        sums[:, 0 : 4 * WIDTH] += jnp.sum(grads.astype(F32).reshape(STEP // 8, 8, 4 * WIDTH), axis=0)

    def rows_of(i):
        return slice(i * PAIR, (i + 1) * PAIR)

    def window(i):
        return pl.ds(STEP - PAIR + i * PAIR, 2 * PAIR)

    def first_cols(h):
        return slice(h * HEAD, (h + 1) * HEAD)

    def second_cols(h):
        return slice(WIDTH + h * HEAD, WIDTH + (h + 1) * HEAD)

    def query():
        t0 = j * (STEP // TILE)
        firsts = [first_ref[t0 + i] for i in range(STEP // TILE)]
        base = j * STEP
        starts = [jnp.where(f >= 0, f * TILE - base, STEP) for f in firsts]
        x = x_ref[...]
        used = tile_column(firsts, STEP) >= 0
        g = jnp.where(used, g_ref[...], jnp.zeros((), BF16))
        hg[...] = dot(g, wo_ref[...], NT)
        for part in range(4):
            cols = slice(part * WIDTH, (part + 1) * WIDTH)
            pre = dot(x, w_ref[:, cols]) + b_ref[part : part + 1, :]
            sig = sigmoid(pre)
            act = pre * sig
            slope = sig + act * (1.0 - sig)
            half = slice(0, WIDTH) if part < 2 else slice(WIDTH, SPAN)
            if part % 2 == 0:
                gq[:, half] = act.astype(BF16)
                slgq[:, half] = slope
            else:
                kv[cur, half] = act.astype(BF16)
                sl[cur, half] = slope
        scale = HEAD**-0.5
        row = lax.broadcasted_iota(jnp.int32, (PAIR, 2 * PAIR), 0)
        col = lax.broadcasted_iota(jnp.int32, (PAIR, 2 * PAIR), 1) - PAIR
        visible = []
        for i in range(pairs):
            begin = tile_column(starts[2 * i : 2 * i + 2], PAIR) - i * PAIR
            visible.append((col >= begin) & (col <= row))
        for n, (i, h) in enumerate(chains):
            s = dot(gq[rows_of(i), second_cols(h)], kv[window(i), second_cols(h)], NT) * scale
            sig = jnp.where(visible[i], sigmoid(s), 0.0)
            a = s * sig
            attn = a.astype(BF16)
            attn_s[i, h] = attn
            dsl_s[i, h] = (sig + a * (1.0 - sig)) * scale
            mix_s[rows_of(i), first_cols(h)] = dot(attn, kv[window(i), first_cols(h)])
            for t in range(n * PIECES // len(chains), (n + 1) * PIECES // len(chains)):
                in_grad_piece(t)
        ones = ones_ref[...]
        mix = mix_s[...]
        high = mix.astype(BF16)
        low = (mix - high.astype(F32)).astype(BF16)
        centered = mix - (dot(high, ones) + dot(low, ones))
        inverse = lax.rsqrt(dot((centered * centered).astype(BF16), ones) + EPSILON)
        normed = centered * inverse
        gate = gq[:, 0:WIDTH].astype(F32)
        gain = gain_ref[...]
        local = hg[...]
        scaled = normed * gain
        hid[...] = (scaled * gate).astype(BF16)
        gq[:, 0:WIDTH] = (local * scaled * slgq[:, 0:WIDTH]).astype(BF16)
        lg = local * gate
        gn = lg * normed
        sums[:, 4 * WIDTH :] += jnp.sum(gn.reshape(STEP // 8, 8, WIDTH), axis=0)
        ng = lg * gain
        mean_one = dot(ng.astype(BF16), ones)
        mean_two = dot((gn * gain).astype(BF16), ones)
        dm_s[...] = ((ng - mean_one - normed * mean_two) * inverse).astype(BF16)
        for i, h in chains:
            hc, kc = first_cols(h), second_cols(h)
            dm = dm_s[rows_of(i), hc]
            q = gq[rows_of(i), kc]
            da = dot(dm, kv[window(i), hc], NT)
            sg = (da * dsl_s[i, h]).astype(BF16)
            dq = dot(sg, kv[window(i), kc])
            dv = dot(attn_s[i, h], dm, TN)
            dk = dot(sg, q, TN)
            before = pl.ds(STEP - PAIR + i * PAIR, PAIR)
            here = pl.ds(STEP + i * PAIR, PAIR)
            dkv[before, hc] += dv[:PAIR]
            dkv[here, hc] = dv[PAIR:]
            dkv[before, kc] += dk[:PAIR]
            dkv[here, kc] = dk[PAIR:]
            gq[rows_of(i), kc] = (dq * slgq[rows_of(i), kc]).astype(BF16)
        acc[:, 4 * WIDTH : 5 * WIDTH] += dot(g, hid[...], TN)

    @pl.when(j < steps)
    def _():
        query()
        finish()
        kv[old] = kv[cur]
        dkv[old] = dkv[cur]
        sl[old] = sl[cur]
        pgq[...] = gq[...]

    @pl.when(j == steps)
    def _():
        for n in range(PIECES):
            in_grad_piece(n)
        finish()

    @pl.when(j == steps + 1)
    def _():
        for n in range(PIECES):
            in_grad_piece(n)
        total = jnp.sum(sums[...], axis=0, keepdims=True)
        for p in range(5 * WIDTH // 128):
            acc[pl.ds(32 * p, 8), 5 * WIDTH :] = jnp.broadcast_to(total[:, p * 128 : (p + 1) * 128], (8, 128))
        core = place_ref[1]
        half = MODEL // 2
        mine_out[...] = acc[pl.ds(pl.multiple_of(core * half, half), half), :]
        sent_out[...] = acc[pl.ds(pl.multiple_of((1 - core) * half, half), half), :].astype(BF16)


def layer(lengths, place, x, g, w, wo, bias, gain):
    rows = x.shape[0]
    steps = rows // STEP
    half = MODEL // 2

    def in_block(j, *_):
        return (jnp.minimum(j, steps - 1), 0)

    def out_block(j, *_):
        return (jnp.clip(j - 1, 0, steps - 1), 0)

    def late_block(j, *_):
        return (jnp.maximum(j - 2, 0), 0)

    def whole(j, *_):
        return (0, 0)

    macs = rows * (MODEL * MODEL * 2 + 2 * WIDTH * MODEL + 6 * WIDTH * WIDTH)
    return pl.pallas_call(
        functools.partial(layer_kernel, steps),
        out_shape=[
            jax.ShapeDtypeStruct((rows, MODEL), BF16),
            jax.ShapeDtypeStruct((half, COLUMNS), BF16),
            jax.ShapeDtypeStruct((half, COLUMNS), F32),
            jax.ShapeDtypeStruct((MODEL, 4 * WIDTH), BF16),
        ],
        grid_spec=pltpu.PrefetchScalarGridSpec(
            num_scalar_prefetch=2,
            grid=(steps + 2,),
            in_specs=[
                pl.BlockSpec((STEP, MODEL), in_block),
                pl.BlockSpec((STEP, MODEL), in_block),
                pl.BlockSpec((STEP, MODEL), late_block),
                pl.BlockSpec(w.shape, lambda j, *_: (0, 0, 0)),
                pl.BlockSpec(wo.shape, whole),
                pl.BlockSpec(bias.shape, whole),
                pl.BlockSpec(gain.shape, whole),
            ],
            out_specs=[
                pl.BlockSpec((STEP, MODEL), out_block),
                pl.BlockSpec((half, COLUMNS), whole),
                pl.BlockSpec((half, COLUMNS), whole),
                pl.BlockSpec((MODEL, 4 * WIDTH), whole),
            ],
            scratch_shapes=[
                pltpu.SMEM((steps * (STEP // TILE),), jnp.int32),
                pltpu.VMEM((WIDTH, WIDTH), BF16),
                pltpu.VMEM((2 * STEP, SPAN), BF16),
                pltpu.VMEM((2 * STEP, SPAN), F32),
                pltpu.VMEM((2 * STEP, SPAN), F32),
                pltpu.VMEM((STEP, SPAN), BF16),
                pltpu.VMEM((STEP, SPAN), BF16),
                pltpu.VMEM((STEP, SPAN), F32),
                pltpu.VMEM((STEP, WIDTH), F32),
                pltpu.VMEM((STEP, WIDTH), BF16),
                pltpu.VMEM((STEP, MODEL), BF16),
                pltpu.VMEM((MODEL, COLUMNS), F32),
                pltpu.VMEM((8, 5 * WIDTH), F32),
                pltpu.VMEM((STEP // PAIR, 2, PAIR, 2 * PAIR), BF16),
                pltpu.VMEM((STEP // PAIR, 2, PAIR, 2 * PAIR), F32),
                pltpu.VMEM((STEP, WIDTH), F32),
                pltpu.VMEM((STEP, WIDTH), BF16),
            ],
        ),
        compiler_params=pltpu.CompilerParams(
            dimension_semantics=("arbitrary",), vmem_limit_bytes=56 * 1024 * 1024
        ),
        cost_estimate=pl.CostEstimate(flops=2 * macs, bytes_accessed=rows * 8000, transcendentals=rows * 2048),
        name="layer",
    )(lengths, place, x, g, x, w, wo, bias, gain)


def partial_kernel(pg_ref, w_ref, out_ref):
    grads = pg_ref[...]
    for d in range(4):
        cols = slice(d * WIDTH, (d + 1) * WIDTH)
        out_ref[:, cols] = dot(grads, w_ref[cols, :], NT).astype(BF16)


def partial_rows(grads, w):
    block = 512
    rows = grads.shape[0]
    wide = pl.BlockSpec((block, MODEL), lambda i: (i, 0))
    return pl.pallas_call(
        partial_kernel,
        out_shape=jax.ShapeDtypeStruct((rows, MODEL), BF16),
        grid=(rows // block,),
        in_specs=[wide, pl.BlockSpec(w.shape, lambda i: (0, 0))],
        out_specs=wide,
        compiler_params=pltpu.CompilerParams(
            dimension_semantics=("arbitrary",), vmem_limit_bytes=56 * 1024 * 1024
        ),
        cost_estimate=pl.CostEstimate(
            flops=2 * rows * MODEL * MODEL, bytes_accessed=rows * 4096 + w.size * 2, transcendentals=0
        ),
        name="partial_rows",
    )(grads, w)


def event_kernel(block, lengths_ref, place_ref, got_ref, g_ref, out_ref, tiles_ref):
    home = place_ref[0]

    @pl.when(pl.program_id(0) == 0)
    def _():
        tiles_ref[0] = lax.fori_loop(0, lengths_ref.shape[1], lambda u, t: t + lengths_ref[home, u], jnp.int32(0))

    row = lax.broadcasted_iota(jnp.int32, (block, WIDTH), 0) + pl.program_id(0) * block
    g = jnp.where(row < tiles_ref[0] * TILE, g_ref[...].astype(F32), 0.0)
    out_ref[...] = (got_ref[...].astype(F32) + g).astype(BF16)


def event_rows(lengths, place, got, g):
    block = 768
    rows = g.shape[0]
    wide = pl.BlockSpec((block, WIDTH), lambda i, f, p: (i, 0))
    return pl.pallas_call(
        functools.partial(event_kernel, block),
        out_shape=jax.ShapeDtypeStruct((rows, WIDTH), BF16),
        grid_spec=pltpu.PrefetchScalarGridSpec(
            num_scalar_prefetch=2,
            grid=(rows // block,),
            in_specs=[wide, pl.BlockSpec((block, WIDTH), lambda i, f, p: (i, p[2]))],
            out_specs=wide,
            scratch_shapes=[pltpu.SMEM((1,), jnp.int32)],
        ),
        compiler_params=pltpu.CompilerParams(
            dimension_semantics=("arbitrary",), vmem_limit_bytes=56 * 1024 * 1024
        ),
        cost_estimate=pl.CostEstimate(flops=rows * 1024, bytes_accessed=rows * 1536, transcendentals=0),
        name="event_rows",
    )(lengths, place, got, g)


def spread_kernel(got_ref, out_ref):
    total = jnp.sum(got_ref[...].astype(F32), axis=0).astype(BF16)
    out_ref[...] = jnp.broadcast_to(total[None], out_ref.shape)


def spread(pieces):
    return pl.pallas_call(
        spread_kernel,
        out_shape=jax.ShapeDtypeStruct(pieces.shape, BF16),
        compiler_params=pltpu.CompilerParams(vmem_limit_bytes=32 * 1024 * 1024),
        cost_estimate=pl.CostEstimate(flops=pieces.size, bytes_accessed=pieces.size * 4, transcendentals=0),
        name="spread",
    )(pieces)


def weights_kernel(other, place_ref, got_ref, *refs):
    pw_out, ow_out, bias_out, gain_out = refs[-4:]
    k = pl.program_id(0)
    core = place_ref[1]
    first_half = (1 - core if other else core) == 0
    values = got_ref[...].astype(F32) * (1.0 / 32.0)
    for p in range(4):
        pw_out[:, p, :] = values[:, p * WIDTH : (p + 1) * WIDTH]
    ow_out[...] = values[:, 4 * WIDTH : 5 * WIDTH].T
    if other:

        @pl.when(k == 0)
        def _():
            bias_out[...] = refs[2][...]
            gain_out[...] = refs[3][...]

    for p in range(5 * WIDTH // 128):
        block, at = divmod(32 * p, values.shape[0])

        @pl.when(first_half & (k == block))
        def _():
            lanes = slice(p % 2 * 128, p % 2 * 128 + 128)
            small = values[at : at + 1, 5 * WIDTH :]
            if p < 8:
                bias_out[p // 2 : p // 2 + 1, lanes] = small
            else:
                gain_out[:, lanes] = small


def weights_out(place, got, earlier):
    other = earlier is not None
    block = 128
    per = got.shape[0] // block

    def half(p):
        return (1 - p[1] if other else p[1]) * per

    small_specs = [
        pl.BlockSpec((4, WIDTH), lambda k, p: (0, 0)),
        pl.BlockSpec((1, WIDTH), lambda k, p: (0, 0)),
    ]
    in_specs = [pl.BlockSpec((block, COLUMNS), lambda k, p: (k, 0))]
    operands = [got]
    aliases = {}
    if other:
        in_specs += [pl.BlockSpec(memory_space=pl.ANY)] * 2 + small_specs
        operands += list(earlier)
        aliases = {2: 0, 3: 1}
    return pl.pallas_call(
        functools.partial(weights_kernel, other),
        out_shape=[
            jax.ShapeDtypeStruct((MODEL, 4, WIDTH), F32),
            jax.ShapeDtypeStruct((WIDTH, MODEL), F32),
            jax.ShapeDtypeStruct((4, WIDTH), F32),
            jax.ShapeDtypeStruct((1, WIDTH), F32),
        ],
        grid_spec=pltpu.PrefetchScalarGridSpec(
            num_scalar_prefetch=1,
            grid=(per,),
            in_specs=in_specs,
            out_specs=[
                pl.BlockSpec((block, 4, WIDTH), lambda k, p: (half(p) + k, 0, 0)),
                pl.BlockSpec((WIDTH, block), lambda k, p: (0, half(p) + k)),
            ]
            + small_specs,
        ),
        input_output_aliases=aliases,
        compiler_params=pltpu.CompilerParams(
            dimension_semantics=("arbitrary",), vmem_limit_bytes=40 * 1024 * 1024
        ),
        cost_estimate=pl.CostEstimate(flops=2000000, bytes_accessed=4200000, transcendentals=0),
        name="weights_out",
    )(place, *operands)


def body(events, upstream, proj_weight, proj_bias, norm_gain, out_weight, lengths, owners):
    rows = events.shape[0]
    place = jnp.stack([lax.axis_index(DP), lax.axis_index("c"), lax.axis_index("mp")]).astype(jnp.int32)
    gain = norm_gain.reshape(1, WIDTH)
    grads, sent, kept, weight_in = layer(lengths, place, events, upstream, proj_weight, out_weight, proj_bias, gain)

    swap = [(0, 1), (1, 0)]
    half = MODEL // 2
    other = lax.ppermute(sent, "c", swap)
    shares = partial_rows(grads, weight_in)
    kept = (kept + other.astype(F32)).astype(BF16)
    got = lax.psum_scatter(shares, "mp", scatter_dimension=1, tiled=True)
    pieces = lax.all_to_all(kept.reshape(16, half // 16, COLUMNS), ("z", "y"), 0, 0, tiled=True)
    pieces = lax.all_to_all(spread(pieces), ("z", "y"), 0, 0, tiled=True).reshape(half, COLUMNS)
    other = lax.ppermute(pieces, "c", swap)
    weights = weights_out(place, pieces, None)
    proj_grad, out_grad, bias_grad, gain_grad = weights_out(place, other, weights)
    event_grads = event_rows(lengths, place, got, upstream)
    return event_grads, proj_grad, bias_grad, gain_grad.reshape(WIDTH), out_grad


def solution(mesh):
    grid = Mesh(mesh.devices.reshape(4, 4, 2, 4), ("z", "y", "c", "mp"))
    placed = (
        P(DP, None),
        P(DP, None),
        P(None, None, "mp"),
        P(None, "mp"),
        P("mp"),
        P("mp", None),
        P(),
        P(),
    )
    return jax.shard_map(
        body,
        mesh=grid,
        in_specs=placed,
        out_specs=(P(DP, "mp"), P(None, None, "mp"), P(None, "mp"), P("mp"), P("mp", None)),
        check_vma=False,
    )
```

```python
import functools

import jax
import jax.numpy as jnp
from jax import lax
from jax.experimental import pallas as pl
from jax.experimental.pallas import tpu as pltpu
from jax.sharding import Mesh, PartitionSpec as P

HEADS = 8
TILE = 64
EPSILON = 1e-05
STEP = 512
PAIR = 128
HEAD = 128
WIDTH = 256
SPAN = 512
MODEL = 1024
COLUMNS = 5 * WIDTH + 128
PIECES = 8
HISTORY = 3
F32 = jnp.float32
BF16 = jnp.bfloat16
NT = (((1,), (1,)), ((), ()))
TN = (((0,), (0,)), ((), ()))
DP = ("z", "y", "c")


def dot(a, b, dims=(((1,), (0,)), ((), ()))):
    return lax.dot_general(a, b, dims, preferred_element_type=F32)


def sigmoid(v):
    return 0.5 * jnp.tanh(0.5 * v) + 0.5


def tile_column(values, rows):
    ids = lax.broadcasted_iota(jnp.int32, (rows, 1), 0)
    column = jnp.full((rows, 1), values[0], jnp.int32)
    for i in range(1, len(values)):
        column = jnp.where(ids >= i * TILE, values[i], column)
    return column


def layer_kernel(
    steps, lengths_ref, place_ref, x_ref, g_ref, xp_ref, wp_ref, wo_ref, b_ref, gain_ref,
    pg_out, sent_out, mine_out, w_ref,
    first_ref, ones_ref, kv, dkv, sl, pgq, gq, slgq, hg, hid, pgs, acc, sums, attn_s, dsl_s, mix_s, dm_s,
):
    j = pl.program_id(0)
    cur = pl.ds(STEP, STEP)
    old = pl.ds(0, STEP)
    pairs = STEP // PAIR
    chains = [(i, h) for i in range(pairs) for h in range(2)]

    @pl.when(j == 0)
    def _():
        kv[old] = jnp.zeros((STEP, SPAN), BF16)
        dkv[old] = jnp.zeros((STEP, SPAN), F32)
        sl[old] = jnp.zeros((STEP, SPAN), F32)
        pgq[...] = jnp.zeros((STEP, SPAN), BF16)
        pgs[...] = jnp.zeros(pgs.shape, BF16)
        acc[...] = jnp.zeros(acc.shape, F32)
        sums[...] = jnp.zeros(sums.shape, F32)
        for p in range(4):
            w_ref[:, p * WIDTH : (p + 1) * WIDTH] = wp_ref[:, p, :]
        head_row = lax.broadcasted_iota(jnp.int32, (WIDTH, WIDTH), 0) >= HEAD
        head_col = lax.broadcasted_iota(jnp.int32, (WIDTH, WIDTH), 1) >= HEAD
        ones_ref[...] = jnp.where(head_row == head_col, 1.0 / HEAD, 0.0).astype(BF16)
        home = place_ref[0]
        tiles = steps * (STEP // TILE)

        @pl.loop(0, tiles)
        def _(t):
            first_ref[t] = -1

        def place(u, begin):
            count = lengths_ref[home, u]
            for t in range(HISTORY):

                @pl.when(t < count)
                def _():
                    first_ref[begin + t] = begin

            return begin + count

        lax.fori_loop(0, lengths_ref.shape[1], place, jnp.int32(0))

    def in_grad_piece(n):
        depth = MODEL // PIECES
        r = slice(n * depth, (n + 1) * depth)
        acc[r, 0 : 4 * WIDTH] += dot(xp_ref[:, r], pgs[...], TN)

    def finish():
        pg_out[:, 0:WIDTH] = pgq[:, 0:WIDTH]
        pg_out[:, WIDTH : 2 * WIDTH] = (dkv[old, 0:WIDTH] * sl[old, 0:WIDTH]).astype(BF16)
        pg_out[:, 2 * WIDTH : 3 * WIDTH] = pgq[:, WIDTH:]
        pg_out[:, 3 * WIDTH :] = (dkv[old, WIDTH:] * sl[old, WIDTH:]).astype(BF16)
        grads = pg_out[...]
        pgs[...] = grads
        sums[:, 0 : 4 * WIDTH] += jnp.sum(grads.astype(F32).reshape(STEP // 8, 8, 4 * WIDTH), axis=0)

    def rows_of(i):
        return slice(i * PAIR, (i + 1) * PAIR)

    def window(i):
        return pl.ds(STEP - PAIR + i * PAIR, 2 * PAIR)

    def first_cols(h):
        return slice(h * HEAD, (h + 1) * HEAD)

    def second_cols(h):
        return slice(WIDTH + h * HEAD, WIDTH + (h + 1) * HEAD)

    def query():
        t0 = j * (STEP // TILE)
        firsts = [first_ref[t0 + i] for i in range(STEP // TILE)]
        base = j * STEP
        starts = [jnp.where(f >= 0, f * TILE - base, STEP) for f in firsts]
        x = x_ref[...]
        used = tile_column(firsts, STEP) >= 0
        g = jnp.where(used, g_ref[...], jnp.zeros((), BF16))
        hg[...] = dot(g, wo_ref[...], NT)
        for part in range(4):
            cols = slice(part * WIDTH, (part + 1) * WIDTH)
            pre = dot(x, w_ref[:, cols]) + b_ref[part : part + 1, :]
            sig = sigmoid(pre)
            act = pre * sig
            slope = sig + act * (1.0 - sig)
            half = slice(0, WIDTH) if part < 2 else slice(WIDTH, SPAN)
            if part % 2 == 0:
                gq[:, half] = act.astype(BF16)
                slgq[:, half] = slope
            else:
                kv[cur, half] = act.astype(BF16)
                sl[cur, half] = slope
        scale = HEAD**-0.5
        row = lax.broadcasted_iota(jnp.int32, (PAIR, 2 * PAIR), 0)
        col = lax.broadcasted_iota(jnp.int32, (PAIR, 2 * PAIR), 1) - PAIR
        visible = []
        for i in range(pairs):
            begin = tile_column(starts[2 * i : 2 * i + 2], PAIR) - i * PAIR
            visible.append((col >= begin) & (col <= row))
        for n, (i, h) in enumerate(chains):
            s = dot(gq[rows_of(i), second_cols(h)], kv[window(i), second_cols(h)], NT) * scale
            sig = jnp.where(visible[i], sigmoid(s), 0.0)
            a = s * sig
            attn = a.astype(BF16)
            attn_s[i, h] = attn
            dsl_s[i, h] = (sig + a * (1.0 - sig)) * scale
            mix_s[rows_of(i), first_cols(h)] = dot(attn, kv[window(i), first_cols(h)])
            for t in range(n * PIECES // len(chains), (n + 1) * PIECES // len(chains)):
                in_grad_piece(t)
        ones = ones_ref[...]
        mix = mix_s[...]
        high = mix.astype(BF16)
        low = (mix - high.astype(F32)).astype(BF16)
        centered = mix - (dot(high, ones) + dot(low, ones))
        inverse = lax.rsqrt(dot((centered * centered).astype(BF16), ones) + EPSILON)
        normed = centered * inverse
        gate = gq[:, 0:WIDTH].astype(F32)
        gain = gain_ref[...]
        local = hg[...]
        scaled = normed * gain
        hid[...] = (scaled * gate).astype(BF16)
        gq[:, 0:WIDTH] = (local * scaled * slgq[:, 0:WIDTH]).astype(BF16)
        lg = local * gate
        gn = lg * normed
        sums[:, 4 * WIDTH :] += jnp.sum(gn.reshape(STEP // 8, 8, WIDTH), axis=0)
        ng = lg * gain
        mean_one = dot(ng.astype(BF16), ones)
        mean_two = dot((gn * gain).astype(BF16), ones)
        dm_s[...] = ((ng - mean_one - normed * mean_two) * inverse).astype(BF16)
        for i, h in chains:
            hc, kc = first_cols(h), second_cols(h)
            dm = dm_s[rows_of(i), hc]
            q = gq[rows_of(i), kc]
            da = dot(dm, kv[window(i), hc], NT)
            sg = (da * dsl_s[i, h]).astype(BF16)
            dq = dot(sg, kv[window(i), kc])
            dv = dot(attn_s[i, h], dm, TN)
            dk = dot(sg, q, TN)
            before = pl.ds(STEP - PAIR + i * PAIR, PAIR)
            here = pl.ds(STEP + i * PAIR, PAIR)
            dkv[before, hc] += dv[:PAIR]
            dkv[here, hc] = dv[PAIR:]
            dkv[before, kc] += dk[:PAIR]
            dkv[here, kc] = dk[PAIR:]
            gq[rows_of(i), kc] = (dq * slgq[rows_of(i), kc]).astype(BF16)
        acc[:, 4 * WIDTH : 5 * WIDTH] += dot(g, hid[...], TN)

    @pl.when(j < steps)
    def _():
        query()
        finish()
        kv[old] = kv[cur]
        dkv[old] = dkv[cur]
        sl[old] = sl[cur]
        pgq[...] = gq[...]

    @pl.when(j == steps)
    def _():
        for n in range(PIECES):
            in_grad_piece(n)
        finish()

    @pl.when(j == steps + 1)
    def _():
        for n in range(PIECES):
            in_grad_piece(n)
        total = jnp.sum(sums[...], axis=0, keepdims=True)
        for p in range(5 * WIDTH // 128):
            acc[pl.ds(32 * p, 8), 5 * WIDTH :] = jnp.broadcast_to(total[:, p * 128 : (p + 1) * 128], (8, 128))
        core = place_ref[1]
        half = MODEL // 2
        mine_out[...] = acc[pl.ds(pl.multiple_of(core * half, half), half), :]
        sent_out[...] = acc[pl.ds(pl.multiple_of((1 - core) * half, half), half), :].astype(BF16)


def layer(lengths, place, x, g, w, wo, bias, gain):
    rows = x.shape[0]
    steps = rows // STEP
    half = MODEL // 2

    def in_block(j, *_):
        return (jnp.minimum(j, steps - 1), 0)

    def out_block(j, *_):
        return (jnp.clip(j - 1, 0, steps - 1), 0)

    def late_block(j, *_):
        return (jnp.maximum(j - 2, 0), 0)

    def whole(j, *_):
        return (0, 0)

    macs = rows * (MODEL * MODEL * 2 + 2 * WIDTH * MODEL + 6 * WIDTH * WIDTH)
    return pl.pallas_call(
        functools.partial(layer_kernel, steps),
        out_shape=[
            jax.ShapeDtypeStruct((rows, MODEL), BF16),
            jax.ShapeDtypeStruct((half, COLUMNS), BF16),
            jax.ShapeDtypeStruct((half, COLUMNS), F32),
            jax.ShapeDtypeStruct((MODEL, 4 * WIDTH), BF16),
        ],
        grid_spec=pltpu.PrefetchScalarGridSpec(
            num_scalar_prefetch=2,
            grid=(steps + 2,),
            in_specs=[
                pl.BlockSpec((STEP, MODEL), in_block),
                pl.BlockSpec((STEP, MODEL), in_block),
                pl.BlockSpec((STEP, MODEL), late_block),
                pl.BlockSpec(w.shape, lambda j, *_: (0, 0, 0)),
                pl.BlockSpec(wo.shape, whole),
                pl.BlockSpec(bias.shape, whole),
                pl.BlockSpec(gain.shape, whole),
            ],
            out_specs=[
                pl.BlockSpec((STEP, MODEL), out_block),
                pl.BlockSpec((half, COLUMNS), whole),
                pl.BlockSpec((half, COLUMNS), whole),
                pl.BlockSpec((MODEL, 4 * WIDTH), whole),
            ],
            scratch_shapes=[
                pltpu.SMEM((steps * (STEP // TILE),), jnp.int32),
                pltpu.VMEM((WIDTH, WIDTH), BF16),
                pltpu.VMEM((2 * STEP, SPAN), BF16),
                pltpu.VMEM((2 * STEP, SPAN), F32),
                pltpu.VMEM((2 * STEP, SPAN), F32),
                pltpu.VMEM((STEP, SPAN), BF16),
                pltpu.VMEM((STEP, SPAN), BF16),
                pltpu.VMEM((STEP, SPAN), F32),
                pltpu.VMEM((STEP, WIDTH), F32),
                pltpu.VMEM((STEP, WIDTH), BF16),
                pltpu.VMEM((STEP, MODEL), BF16),
                pltpu.VMEM((MODEL, COLUMNS), F32),
                pltpu.VMEM((8, 5 * WIDTH), F32),
                pltpu.VMEM((STEP // PAIR, 2, PAIR, 2 * PAIR), BF16),
                pltpu.VMEM((STEP // PAIR, 2, PAIR, 2 * PAIR), F32),
                pltpu.VMEM((STEP, WIDTH), F32),
                pltpu.VMEM((STEP, WIDTH), BF16),
            ],
        ),
        compiler_params=pltpu.CompilerParams(
            dimension_semantics=("arbitrary",), vmem_limit_bytes=56 * 1024 * 1024
        ),
        cost_estimate=pl.CostEstimate(flops=2 * macs, bytes_accessed=rows * 8000, transcendentals=rows * 2048),
        name="layer",
    )(lengths, place, x, g, x, w, wo, bias, gain)


def partial_kernel(block, lengths_ref, place_ref, pg_ref, w_ref, g_ref, out_ref, tiles_ref):
    home, me = place_ref[0], place_ref[2]

    @pl.when(pl.program_id(0) == 0)
    def _():
        tiles_ref[0] = lax.fori_loop(0, lengths_ref.shape[1], lambda u, t: t + lengths_ref[home, u], jnp.int32(0))

    row = lax.broadcasted_iota(jnp.int32, (block, WIDTH), 0) + pl.program_id(0) * block
    grads = pg_ref[...]
    for d in range(4):
        cols = slice(d * WIDTH, (d + 1) * WIDTH)
        g = jnp.where(row < jnp.where(me == d, tiles_ref[0] * TILE, 0), g_ref[...].astype(F32), 0.0)
        out_ref[:, cols] = (dot(grads, w_ref[cols, :], NT) + g).astype(BF16)


def partial_rows(lengths, place, grads, w, g):
    block = 1024
    rows = grads.shape[0]
    here = pl.BlockSpec((block, MODEL), lambda i, f, p: (i, 0))
    return pl.pallas_call(
        functools.partial(partial_kernel, block),
        out_shape=jax.ShapeDtypeStruct((rows, MODEL), BF16),
        grid_spec=pltpu.PrefetchScalarGridSpec(
            num_scalar_prefetch=2,
            grid=(rows // block,),
            in_specs=[
                here,
                pl.BlockSpec(w.shape, lambda i, f, p: (0, 0)),
                pl.BlockSpec((block, WIDTH), lambda i, f, p: (i, p[2])),
            ],
            out_specs=here,
            scratch_shapes=[pltpu.SMEM((1,), jnp.int32)],
        ),
        compiler_params=pltpu.CompilerParams(
            dimension_semantics=("arbitrary",), vmem_limit_bytes=56 * 1024 * 1024
        ),
        cost_estimate=pl.CostEstimate(
            flops=2 * rows * MODEL * MODEL, bytes_accessed=rows * 4608 + w.size * 2, transcendentals=0
        ),
        name="partial_rows",
    )(lengths, place, grads, w, g)


def spread_kernel(got_ref, out_ref):
    total = jnp.sum(got_ref[...].astype(F32), axis=0).astype(BF16)
    out_ref[...] = jnp.broadcast_to(total[None], out_ref.shape)


def spread(pieces):
    return pl.pallas_call(
        spread_kernel,
        out_shape=jax.ShapeDtypeStruct(pieces.shape, BF16),
        compiler_params=pltpu.CompilerParams(vmem_limit_bytes=32 * 1024 * 1024),
        cost_estimate=pl.CostEstimate(flops=pieces.size, bytes_accessed=pieces.size * 4, transcendentals=0),
        name="spread",
    )(pieces)


def weights_kernel(other, place_ref, got_ref, *refs):
    pw_out, ow_out, bias_out, gain_out = refs[-4:]
    k = pl.program_id(0)
    core = place_ref[1]
    first_half = (1 - core if other else core) == 0
    values = got_ref[...].astype(F32) * (1.0 / 32.0)
    for p in range(4):
        pw_out[:, p, :] = values[:, p * WIDTH : (p + 1) * WIDTH]
    ow_out[...] = values[:, 4 * WIDTH : 5 * WIDTH].T
    if other:

        @pl.when(k == 0)
        def _():
            bias_out[...] = refs[2][...]
            gain_out[...] = refs[3][...]

    for p in range(5 * WIDTH // 128):
        block, at = divmod(32 * p, values.shape[0])

        @pl.when(first_half & (k == block))
        def _():
            lanes = slice(p % 2 * 128, p % 2 * 128 + 128)
            small = values[at : at + 1, 5 * WIDTH :]
            if p < 8:
                bias_out[p // 2 : p // 2 + 1, lanes] = small
            else:
                gain_out[:, lanes] = small


def weights_out(place, got, earlier):
    other = earlier is not None
    block = 128
    per = got.shape[0] // block

    def half(p):
        return (1 - p[1] if other else p[1]) * per

    small_specs = [
        pl.BlockSpec((4, WIDTH), lambda k, p: (0, 0)),
        pl.BlockSpec((1, WIDTH), lambda k, p: (0, 0)),
    ]
    in_specs = [pl.BlockSpec((block, COLUMNS), lambda k, p: (k, 0))]
    operands = [got]
    aliases = {}
    if other:
        in_specs += [pl.BlockSpec(memory_space=pl.ANY)] * 2 + small_specs
        operands += list(earlier)
        aliases = {2: 0, 3: 1}
    return pl.pallas_call(
        functools.partial(weights_kernel, other),
        out_shape=[
            jax.ShapeDtypeStruct((MODEL, 4, WIDTH), F32),
            jax.ShapeDtypeStruct((WIDTH, MODEL), F32),
            jax.ShapeDtypeStruct((4, WIDTH), F32),
            jax.ShapeDtypeStruct((1, WIDTH), F32),
        ],
        grid_spec=pltpu.PrefetchScalarGridSpec(
            num_scalar_prefetch=1,
            grid=(per,),
            in_specs=in_specs,
            out_specs=[
                pl.BlockSpec((block, 4, WIDTH), lambda k, p: (half(p) + k, 0, 0)),
                pl.BlockSpec((WIDTH, block), lambda k, p: (0, half(p) + k)),
            ]
            + small_specs,
        ),
        input_output_aliases=aliases,
        compiler_params=pltpu.CompilerParams(
            dimension_semantics=("arbitrary",), vmem_limit_bytes=40 * 1024 * 1024
        ),
        cost_estimate=pl.CostEstimate(flops=2000000, bytes_accessed=4200000, transcendentals=0),
        name="weights_out",
    )(place, *operands)


def body(events, upstream, proj_weight, proj_bias, norm_gain, out_weight, lengths, owners):
    rows = events.shape[0]
    place = jnp.stack([lax.axis_index(DP), lax.axis_index("c"), lax.axis_index("mp")]).astype(jnp.int32)
    gain = norm_gain.reshape(1, WIDTH)
    grads, sent, kept, weight_in = layer(lengths, place, events, upstream, proj_weight, out_weight, proj_bias, gain)

    swap = [(0, 1), (1, 0)]
    half = MODEL // 2
    other = lax.ppermute(sent, "c", swap)
    shares = partial_rows(lengths, place, grads, weight_in, upstream)
    event_grads = lax.psum_scatter(shares, "mp", scatter_dimension=1, tiled=True)
    kept = (kept + other.astype(F32)).astype(BF16)
    pieces = lax.all_to_all(kept.reshape(16, half // 16, COLUMNS), ("z", "y"), 0, 0, tiled=True)
    pieces = lax.all_to_all(spread(pieces), ("z", "y"), 0, 0, tiled=True).reshape(half, COLUMNS)
    other = lax.ppermute(pieces, "c", swap)
    weights = weights_out(place, pieces, None)
    proj_grad, out_grad, bias_grad, gain_grad = weights_out(place, other, weights)
    return event_grads, proj_grad, bias_grad, gain_grad.reshape(WIDTH), out_grad


def solution(mesh):
    grid = Mesh(mesh.devices.reshape(4, 4, 2, 4), ("z", "y", "c", "mp"))
    placed = (
        P(DP, None),
        P(DP, None),
        P(None, None, "mp"),
        P(None, "mp"),
        P("mp"),
        P("mp", None),
        P(),
        P(),
    )
    return jax.shard_map(
        body,
        mesh=grid,
        in_specs=placed,
        out_specs=(P(DP, "mp"), P(None, None, "mp"), P(None, "mp"), P("mp"), P("mp", None)),
        check_vma=False,
    )
```

```python
import functools

import jax
import jax.numpy as jnp
from jax import lax
from jax.experimental import pallas as pl
from jax.experimental.pallas import tpu as pltpu
from jax.sharding import Mesh, PartitionSpec as P

HEADS = 8
TILE = 64
EPSILON = 1e-05
STEP = 512
PAIR = 128
HEAD = 128
WIDTH = 256
SPAN = 512
MODEL = 1024
COLUMNS = 5 * WIDTH + 128
PIECES = 8
HISTORY = 3
F32 = jnp.float32
BF16 = jnp.bfloat16
NT = (((1,), (1,)), ((), ()))
TN = (((0,), (0,)), ((), ()))
DP = ("z", "y", "c")


def dot(a, b, dims=(((1,), (0,)), ((), ()))):
    return lax.dot_general(a, b, dims, preferred_element_type=F32)


def sigmoid(v):
    return 0.5 * jnp.tanh(0.5 * v) + 0.5


def tile_column(values, rows):
    ids = lax.broadcasted_iota(jnp.int32, (rows, 1), 0)
    column = jnp.full((rows, 1), values[0], jnp.int32)
    for i in range(1, len(values)):
        column = jnp.where(ids >= i * TILE, values[i], column)
    return column


def layer_kernel(
    steps, lengths_ref, place_ref, x_ref, g_ref, xp_ref, wp_ref, wo_ref, b_ref, gain_ref,
    pg_out, sent_out, mine_out, w_ref,
    first_ref, ones_ref, kv, dkv, sl, pgq, gq, slgq, hg, hid, pgs, acc, sums, attn_s, dsl_s, mix_s, dm_s,
):
    j = pl.program_id(0)
    cur = pl.ds(STEP, STEP)
    old = pl.ds(0, STEP)
    pairs = STEP // PAIR
    chains = [(i, h) for i in range(pairs) for h in range(2)]

    @pl.when(j == 0)
    def _():
        kv[old] = jnp.zeros((STEP, SPAN), BF16)
        dkv[old] = jnp.zeros((STEP, SPAN), F32)
        sl[old] = jnp.zeros((STEP, SPAN), F32)
        pgq[...] = jnp.zeros((STEP, SPAN), BF16)
        pgs[...] = jnp.zeros(pgs.shape, BF16)
        acc[...] = jnp.zeros(acc.shape, F32)
        sums[...] = jnp.zeros(sums.shape, F32)
        for p in range(4):
            w_ref[:, p * WIDTH : (p + 1) * WIDTH] = wp_ref[:, p, :]
        head_row = lax.broadcasted_iota(jnp.int32, (WIDTH, WIDTH), 0) >= HEAD
        head_col = lax.broadcasted_iota(jnp.int32, (WIDTH, WIDTH), 1) >= HEAD
        ones_ref[...] = jnp.where(head_row == head_col, 1.0 / HEAD, 0.0).astype(BF16)
        home = place_ref[0]
        tiles = steps * (STEP // TILE)

        @pl.loop(0, tiles)
        def _(t):
            first_ref[t] = -1

        def place(u, begin):
            count = lengths_ref[home, u]
            for t in range(HISTORY):

                @pl.when(t < count)
                def _():
                    first_ref[begin + t] = begin

            return begin + count

        lax.fori_loop(0, lengths_ref.shape[1], place, jnp.int32(0))

    def in_grad_piece(n):
        depth = MODEL // PIECES
        r = slice(n * depth, (n + 1) * depth)
        acc[r, 0 : 4 * WIDTH] += dot(xp_ref[:, r], pgs[...], TN)

    def finish():
        pg_out[:, 0:WIDTH] = pgq[:, 0:WIDTH]
        pg_out[:, WIDTH : 2 * WIDTH] = (dkv[old, 0:WIDTH] * sl[old, 0:WIDTH]).astype(BF16)
        pg_out[:, 2 * WIDTH : 3 * WIDTH] = pgq[:, WIDTH:]
        pg_out[:, 3 * WIDTH :] = (dkv[old, WIDTH:] * sl[old, WIDTH:]).astype(BF16)
        grads = pg_out[...]
        pgs[...] = grads
        sums[:, 0 : 4 * WIDTH] += jnp.sum(grads.astype(F32).reshape(STEP // 8, 8, 4 * WIDTH), axis=0)

    def rows_of(i):
        return slice(i * PAIR, (i + 1) * PAIR)

    def window(i):
        return pl.ds(STEP - PAIR + i * PAIR, 2 * PAIR)

    def first_cols(h):
        return slice(h * HEAD, (h + 1) * HEAD)

    def second_cols(h):
        return slice(WIDTH + h * HEAD, WIDTH + (h + 1) * HEAD)

    def query():
        t0 = j * (STEP // TILE)
        firsts = [first_ref[t0 + i] for i in range(STEP // TILE)]
        base = j * STEP
        starts = [jnp.where(f >= 0, f * TILE - base, STEP) for f in firsts]
        x = x_ref[...]
        used = tile_column(firsts, STEP) >= 0
        g = jnp.where(used, g_ref[...], jnp.zeros((), BF16))
        hg[...] = dot(g, wo_ref[...], NT)
        for part in range(4):
            cols = slice(part * WIDTH, (part + 1) * WIDTH)
            pre = dot(x, w_ref[:, cols]) + b_ref[part : part + 1, :]
            sig = sigmoid(pre)
            act = pre * sig
            slope = sig + act * (1.0 - sig)
            half = slice(0, WIDTH) if part < 2 else slice(WIDTH, SPAN)
            if part % 2 == 0:
                gq[:, half] = act.astype(BF16)
                slgq[:, half] = slope
            else:
                kv[cur, half] = act.astype(BF16)
                sl[cur, half] = slope
        scale = HEAD**-0.5
        row = lax.broadcasted_iota(jnp.int32, (PAIR, 2 * PAIR), 0)
        col = lax.broadcasted_iota(jnp.int32, (PAIR, 2 * PAIR), 1) - PAIR
        visible = []
        for i in range(pairs):
            begin = tile_column(starts[2 * i : 2 * i + 2], PAIR) - i * PAIR
            visible.append((col >= begin) & (col <= row))
        for n, (i, h) in enumerate(chains):
            s = dot(gq[rows_of(i), second_cols(h)], kv[window(i), second_cols(h)], NT) * scale
            sig = jnp.where(visible[i], sigmoid(s), 0.0)
            a = s * sig
            attn = a.astype(BF16)
            attn_s[i, h] = attn
            dsl_s[i, h] = (sig + a * (1.0 - sig)) * scale
            mix_s[rows_of(i), first_cols(h)] = dot(attn, kv[window(i), first_cols(h)])
            for t in range(n * PIECES // len(chains), (n + 1) * PIECES // len(chains)):
                in_grad_piece(t)
        ones = ones_ref[...]
        mix = mix_s[...]
        high = mix.astype(BF16)
        low = (mix - high.astype(F32)).astype(BF16)
        centered = mix - (dot(high, ones) + dot(low, ones))
        inverse = lax.rsqrt(dot((centered * centered).astype(BF16), ones) + EPSILON)
        normed = centered * inverse
        gate = gq[:, 0:WIDTH].astype(F32)
        gain = gain_ref[...]
        local = hg[...]
        scaled = normed * gain
        hid[...] = (scaled * gate).astype(BF16)
        gq[:, 0:WIDTH] = (local * scaled * slgq[:, 0:WIDTH]).astype(BF16)
        lg = local * gate
        gn = lg * normed
        sums[:, 4 * WIDTH :] += jnp.sum(gn.reshape(STEP // 8, 8, WIDTH), axis=0)
        ng = lg * gain
        mean_one = dot(ng.astype(BF16), ones)
        mean_two = dot((gn * gain).astype(BF16), ones)
        dm_s[...] = ((ng - mean_one - normed * mean_two) * inverse).astype(BF16)
        for i, h in chains:
            hc, kc = first_cols(h), second_cols(h)
            dm = dm_s[rows_of(i), hc]
            q = gq[rows_of(i), kc]
            da = dot(dm, kv[window(i), hc], NT)
            sg = (da * dsl_s[i, h]).astype(BF16)
            dq = dot(sg, kv[window(i), kc])
            dv = dot(attn_s[i, h], dm, TN)
            dk = dot(sg, q, TN)
            before = pl.ds(STEP - PAIR + i * PAIR, PAIR)
            here = pl.ds(STEP + i * PAIR, PAIR)
            dkv[before, hc] += dv[:PAIR]
            dkv[here, hc] = dv[PAIR:]
            dkv[before, kc] += dk[:PAIR]
            dkv[here, kc] = dk[PAIR:]
            gq[rows_of(i), kc] = (dq * slgq[rows_of(i), kc]).astype(BF16)
        acc[:, 4 * WIDTH : 5 * WIDTH] += dot(g, hid[...], TN)

    @pl.when(j < steps)
    def _():
        query()
        finish()
        kv[old] = kv[cur]
        dkv[old] = dkv[cur]
        sl[old] = sl[cur]
        pgq[...] = gq[...]

    @pl.when(j == steps)
    def _():
        for n in range(PIECES):
            in_grad_piece(n)
        finish()

    @pl.when(j == steps + 1)
    def _():
        for n in range(PIECES):
            in_grad_piece(n)
        total = jnp.sum(sums[...], axis=0, keepdims=True)
        for p in range(5 * WIDTH // 128):
            acc[pl.ds(32 * p, 8), 5 * WIDTH :] = jnp.broadcast_to(total[:, p * 128 : (p + 1) * 128], (8, 128))
        core = place_ref[1]
        half = MODEL // 2
        mine_out[...] = acc[pl.ds(pl.multiple_of(core * half, half), half), :]
        sent_out[...] = acc[pl.ds(pl.multiple_of((1 - core) * half, half), half), :].astype(BF16)


def layer(lengths, place, x, g, w, wo, bias, gain):
    rows = x.shape[0]
    steps = rows // STEP
    half = MODEL // 2

    def in_block(j, *_):
        return (jnp.minimum(j, steps - 1), 0)

    def out_block(j, *_):
        return (jnp.clip(j - 1, 0, steps - 1), 0)

    def late_block(j, *_):
        return (jnp.maximum(j - 2, 0), 0)

    def whole(j, *_):
        return (0, 0)

    macs = rows * (MODEL * MODEL * 2 + 2 * WIDTH * MODEL + 6 * WIDTH * WIDTH)
    return pl.pallas_call(
        functools.partial(layer_kernel, steps),
        out_shape=[
            jax.ShapeDtypeStruct((rows, MODEL), BF16),
            jax.ShapeDtypeStruct((half, COLUMNS), BF16),
            jax.ShapeDtypeStruct((half, COLUMNS), F32),
            jax.ShapeDtypeStruct((MODEL, 4 * WIDTH), BF16),
        ],
        grid_spec=pltpu.PrefetchScalarGridSpec(
            num_scalar_prefetch=2,
            grid=(steps + 2,),
            in_specs=[
                pl.BlockSpec((STEP, MODEL), in_block),
                pl.BlockSpec((STEP, MODEL), in_block),
                pl.BlockSpec((STEP, MODEL), late_block),
                pl.BlockSpec(w.shape, lambda j, *_: (0, 0, 0)),
                pl.BlockSpec(wo.shape, whole),
                pl.BlockSpec(bias.shape, whole),
                pl.BlockSpec(gain.shape, whole),
            ],
            out_specs=[
                pl.BlockSpec((STEP, MODEL), out_block),
                pl.BlockSpec((half, COLUMNS), whole),
                pl.BlockSpec((half, COLUMNS), whole),
                pl.BlockSpec((MODEL, 4 * WIDTH), whole),
            ],
            scratch_shapes=[
                pltpu.SMEM((steps * (STEP // TILE),), jnp.int32),
                pltpu.VMEM((WIDTH, WIDTH), BF16),
                pltpu.VMEM((2 * STEP, SPAN), BF16),
                pltpu.VMEM((2 * STEP, SPAN), F32),
                pltpu.VMEM((2 * STEP, SPAN), F32),
                pltpu.VMEM((STEP, SPAN), BF16),
                pltpu.VMEM((STEP, SPAN), BF16),
                pltpu.VMEM((STEP, SPAN), F32),
                pltpu.VMEM((STEP, WIDTH), F32),
                pltpu.VMEM((STEP, WIDTH), BF16),
                pltpu.VMEM((STEP, MODEL), BF16),
                pltpu.VMEM((MODEL, COLUMNS), F32),
                pltpu.VMEM((8, 5 * WIDTH), F32),
                pltpu.VMEM((STEP // PAIR, 2, PAIR, 2 * PAIR), BF16),
                pltpu.VMEM((STEP // PAIR, 2, PAIR, 2 * PAIR), F32),
                pltpu.VMEM((STEP, WIDTH), F32),
                pltpu.VMEM((STEP, WIDTH), BF16),
            ],
        ),
        compiler_params=pltpu.CompilerParams(
            dimension_semantics=("arbitrary",), vmem_limit_bytes=56 * 1024 * 1024
        ),
        cost_estimate=pl.CostEstimate(flops=2 * macs, bytes_accessed=rows * 8000, transcendentals=rows * 2048),
        name="layer",
    )(lengths, place, x, g, x, w, wo, bias, gain)


def partial_kernel(block, lengths_ref, place_ref, pg_ref, w_ref, g_ref, out_ref, tiles_ref):
    home, me = place_ref[0], place_ref[2]

    @pl.when(pl.program_id(0) == 0)
    def _():
        tiles_ref[0] = lax.fori_loop(0, lengths_ref.shape[1], lambda u, t: t + lengths_ref[home, u], jnp.int32(0))

    row = lax.broadcasted_iota(jnp.int32, (block, WIDTH), 0) + pl.program_id(0) * block
    grads = pg_ref[...]
    for d in range(4):
        cols = slice(d * WIDTH, (d + 1) * WIDTH)
        g = jnp.where(row < jnp.where(me == d, tiles_ref[0] * TILE, 0), g_ref[...].astype(F32), 0.0)
        out_ref[d] = (dot(grads, w_ref[cols, :], NT) + g).astype(BF16)


def partial_rows(lengths, place, grads, w, g):
    block = 1024
    rows = grads.shape[0]
    here = pl.BlockSpec((block, MODEL), lambda i, f, p: (i, 0))
    return pl.pallas_call(
        functools.partial(partial_kernel, block),
        out_shape=jax.ShapeDtypeStruct((4, rows, WIDTH), BF16),
        grid_spec=pltpu.PrefetchScalarGridSpec(
            num_scalar_prefetch=2,
            grid=(rows // block,),
            in_specs=[
                here,
                pl.BlockSpec(w.shape, lambda i, f, p: (0, 0)),
                pl.BlockSpec((block, WIDTH), lambda i, f, p: (i, p[2])),
            ],
            out_specs=pl.BlockSpec((4, block, WIDTH), lambda i, f, p: (0, i, 0)),
            scratch_shapes=[pltpu.SMEM((1,), jnp.int32)],
        ),
        compiler_params=pltpu.CompilerParams(
            dimension_semantics=("arbitrary",), vmem_limit_bytes=56 * 1024 * 1024
        ),
        cost_estimate=pl.CostEstimate(
            flops=2 * rows * MODEL * MODEL, bytes_accessed=rows * 4608 + w.size * 2, transcendentals=0
        ),
        name="partial_rows",
    )(lengths, place, grads, w, g)


def spread_kernel(got_ref, out_ref):
    total = jnp.sum(got_ref[...].astype(F32), axis=0).astype(BF16)
    out_ref[...] = jnp.broadcast_to(total[None], out_ref.shape)


def spread(pieces):
    return pl.pallas_call(
        spread_kernel,
        out_shape=jax.ShapeDtypeStruct(pieces.shape, BF16),
        compiler_params=pltpu.CompilerParams(vmem_limit_bytes=32 * 1024 * 1024),
        cost_estimate=pl.CostEstimate(flops=pieces.size, bytes_accessed=pieces.size * 4, transcendentals=0),
        name="spread",
    )(pieces)


def weights_kernel(other, place_ref, got_ref, *refs):
    pw_out, ow_out, bias_out, gain_out = refs[-4:]
    k = pl.program_id(0)
    core = place_ref[1]
    first_half = (1 - core if other else core) == 0
    values = got_ref[...].astype(F32) * (1.0 / 32.0)
    for p in range(4):
        pw_out[:, p, :] = values[:, p * WIDTH : (p + 1) * WIDTH]
    ow_out[...] = values[:, 4 * WIDTH : 5 * WIDTH].T
    if other:

        @pl.when(k == 0)
        def _():
            bias_out[...] = refs[2][...]
            gain_out[...] = refs[3][...]

    for p in range(5 * WIDTH // 128):
        block, at = divmod(32 * p, values.shape[0])

        @pl.when(first_half & (k == block))
        def _():
            lanes = slice(p % 2 * 128, p % 2 * 128 + 128)
            small = values[at : at + 1, 5 * WIDTH :]
            if p < 8:
                bias_out[p // 2 : p // 2 + 1, lanes] = small
            else:
                gain_out[:, lanes] = small


def weights_out(place, got, earlier):
    other = earlier is not None
    block = 128
    per = got.shape[0] // block

    def half(p):
        return (1 - p[1] if other else p[1]) * per

    small_specs = [
        pl.BlockSpec((4, WIDTH), lambda k, p: (0, 0)),
        pl.BlockSpec((1, WIDTH), lambda k, p: (0, 0)),
    ]
    in_specs = [pl.BlockSpec((block, COLUMNS), lambda k, p: (k, 0))]
    operands = [got]
    aliases = {}
    if other:
        in_specs += [pl.BlockSpec(memory_space=pl.ANY)] * 2 + small_specs
        operands += list(earlier)
        aliases = {2: 0, 3: 1}
    return pl.pallas_call(
        functools.partial(weights_kernel, other),
        out_shape=[
            jax.ShapeDtypeStruct((MODEL, 4, WIDTH), F32),
            jax.ShapeDtypeStruct((WIDTH, MODEL), F32),
            jax.ShapeDtypeStruct((4, WIDTH), F32),
            jax.ShapeDtypeStruct((1, WIDTH), F32),
        ],
        grid_spec=pltpu.PrefetchScalarGridSpec(
            num_scalar_prefetch=1,
            grid=(per,),
            in_specs=in_specs,
            out_specs=[
                pl.BlockSpec((block, 4, WIDTH), lambda k, p: (half(p) + k, 0, 0)),
                pl.BlockSpec((WIDTH, block), lambda k, p: (0, half(p) + k)),
            ]
            + small_specs,
        ),
        input_output_aliases=aliases,
        compiler_params=pltpu.CompilerParams(
            dimension_semantics=("arbitrary",), vmem_limit_bytes=40 * 1024 * 1024
        ),
        cost_estimate=pl.CostEstimate(flops=2000000, bytes_accessed=4200000, transcendentals=0),
        name="weights_out",
    )(place, *operands)


def body(events, upstream, proj_weight, proj_bias, norm_gain, out_weight, lengths, owners):
    rows = events.shape[0]
    place = jnp.stack([lax.axis_index(DP), lax.axis_index("c"), lax.axis_index("mp")]).astype(jnp.int32)
    gain = norm_gain.reshape(1, WIDTH)
    grads, sent, kept, weight_in = layer(lengths, place, events, upstream, proj_weight, out_weight, proj_bias, gain)

    swap = [(0, 1), (1, 0)]
    half = MODEL // 2
    other = lax.ppermute(sent, "c", swap)
    shares = partial_rows(lengths, place, grads, weight_in, upstream)
    event_grads = lax.psum_scatter(shares, "mp", scatter_dimension=0, tiled=False)
    kept = (kept + other.astype(F32)).astype(BF16)
    pieces = lax.all_to_all(kept.reshape(16, half // 16, COLUMNS), ("z", "y"), 0, 0, tiled=True)
    pieces = lax.all_to_all(spread(pieces), ("z", "y"), 0, 0, tiled=True).reshape(half, COLUMNS)
    other = lax.ppermute(pieces, "c", swap)
    weights = weights_out(place, pieces, None)
    proj_grad, out_grad, bias_grad, gain_grad = weights_out(place, other, weights)
    return event_grads, proj_grad, bias_grad, gain_grad.reshape(WIDTH), out_grad


def solution(mesh):
    grid = Mesh(mesh.devices.reshape(4, 4, 2, 4), ("z", "y", "c", "mp"))
    placed = (
        P(DP, None),
        P(DP, None),
        P(None, None, "mp"),
        P(None, "mp"),
        P("mp"),
        P("mp", None),
        P(),
        P(),
    )
    return jax.shard_map(
        body,
        mesh=grid,
        in_specs=placed,
        out_specs=(P(DP, "mp"), P(None, None, "mp"), P(None, "mp"), P("mp"), P("mp", None)),
        check_vma=False,
    )
```
